512 devices in a mesh: dom: 64 (over x_lo, z, core), cls: 8 (over x_hi, y).
Axes of the slice: x: 4 (x_hi: 2, x_lo: 2; x = x_hi * 2 + x_lo), y: 4, z: 16, core: 2. Of those that a mesh axis runs over, the one named last changes fastest.
Arguments:
- particles: bfloat16 [1024, 64, 288], P(('dom', 'cls')), may hold values from -200 to 200
- group_ids: int32 [1024], P(('dom', 'cls')), may hold values from 0 to 31
- ctf_table: float32 [32, 64], replicated, may hold values from 0.1 to 1
- references: bfloat16 [400, 64, 288], P('cls'), may hold values from -4 to 4
Outputs:
- new_references: bfloat16 [400, 64, 288], P('cls')
The draws below stay inside these ranges and needn't reach their ends.
All inputs are finite; a program needn't handle non-finite values.
Results may differ from the reference program's by a relative error of at most 0.0075.
The reference program's roundings to bfloat16 on the way count: a program that leaves them out, or rounds other values in their place, can miss the bound.
Values may be sent and summed in bfloat16 or wider, within the bound.
No kernel may reach another device: no remote copies, remote signals or barrier semaphores. Data moves between devices by JAX's collectives and lax.ppermute only.
A program may use at most 128 MiB of HBM per device.

```python
import math
import jax
import jax.numpy as jnp
from jax import lax

CLASSES = 400
CYCLES = 64
ANG = 288
ROT = 72
GROUPS = 32
PARTICLES = 1024


def class_images(key):
    return jax.random.truncated_normal(jax.random.fold_in(key, 11), -4.0, 4.0, (CLASSES, CYCLES, ANG), jnp.float32)


def draw_references(key, part):
    images = class_images(key)
    return images.astype(jnp.bfloat16)


def turned(picked, shifts):
    angle = jnp.arange(ANG, dtype=jnp.int32)
    index = (angle[None, :] - ANG // ROT * shifts[:, None]) % ANG
    index = jnp.broadcast_to(index[:, None, :], picked.shape)
    return jnp.take_along_axis(picked, index, axis=2)


def draw_particles(key, part):
    images = class_images(key)
    key = jax.random.fold_in(key, 3)
    keys = jax.random.split(key, 8)
    shape = (PARTICLES, CYCLES, ANG)
    base = 150.0 / math.sqrt(CYCLES * ANG)
    chosen = (jax.random.randint(keys[2], (PARTICLES,), 0, 8) == 0).astype(jnp.float32)
    which = jax.random.randint(keys[3], (PARTICLES,), 0, CLASSES)
    first = jax.random.randint(keys[4], (PARTICLES,), 0, ROT)
    second = (first + jax.random.randint(keys[5], (PARTICLES,), 1, ROT)) % ROT
    strength = base * (1.0 + 0.75 * jax.random.randint(keys[6], (PARTICLES,), 0, 3).astype(jnp.float32))
    spacing = jax.random.uniform(keys[7], (PARTICLES,), jnp.float32, 1.0, 3.0) / (1.56 * math.sqrt(CYCLES * ANG))
    picked = jnp.take(images, which, axis=0)
    planted = strength[:, None, None] * turned(picked, first) + (strength - spacing)[:, None, None] * turned(picked, second)
    noise = jax.random.truncated_normal(keys[1], -5.0, 5.0, shape, jnp.float32)
    values = noise + chosen[:, None, None] * planted
    return values.astype(jnp.bfloat16)


def set_ends(entries, own_key, low, high):
    index_at = [jax.random.randint(jax.random.fold_in(own_key, axis), (), 0, length) for axis, length in enumerate(entries.shape)]
    widest = entries.shape.index(max(entries.shape))
    neighbour = index_at[:widest] + [(index_at[widest] + 1) % entries.shape[widest]] + index_at[widest + 1:]
    return entries.at[tuple(index_at)].set(low).at[tuple(neighbour)].set(high)


def setup_inputs(seed: int = 0) -> dict:
    key_list = jax.random.split(jax.random.key(seed), 5)
    return {
        "particles": draw_particles(jax.random.fold_in(key_list[4], 71), 0),
        "group_ids": set_ends(jax.random.randint(key_list[1], (PARTICLES,), 0, GROUPS), jax.random.fold_in(key_list[1], 1), 0, GROUPS - 1).astype(jnp.int32),
        "ctf_table": jnp.clip(jnp.exp(jax.random.uniform(key_list[2], (GROUPS, CYCLES), jnp.float32, math.log(0.1), math.log(1.0))), 0.1, 1.0),
        "references": draw_references(jax.random.fold_in(key_list[4], 71), 0),
    }


PRIOR_WEIGHT = 1.0

def rounded(values):
    return lax.optimization_barrier(values.astype(jnp.bfloat16)).astype(jnp.float32)

def angular_spectrum(values):
    spec = jnp.fft.rfft(values, axis=-1)
    return (jnp.real(spec).astype(jnp.float32), (-jnp.imag(spec)).astype(jnp.float32))

def search_tables():
    freqs = ANG // 2 + 1
    index = jnp.arange(freqs, dtype=jnp.int32)[:, None] * (ANG // ROT) * jnp.arange(ROT, dtype=jnp.int32)[None, :] % ANG
    phase = 2.0 * math.pi * index.astype(jnp.float32) / ANG
    freq = jnp.arange(freqs, dtype=jnp.int32)
    scale = jnp.where((freq == 0) | (freq == ANG // 2), 1.0, 2.0).astype(jnp.float32) / ANG
    return (jnp.cos(phase), jnp.sin(phase), scale)

def inverse_tables():
    freqs = ANG // 2 + 1
    index = jnp.arange(freqs, dtype=jnp.int32)[:, None] * jnp.arange(ANG, dtype=jnp.int32)[None, :] % ANG
    phase = 2.0 * math.pi * index.astype(jnp.float32) / ANG
    return (jnp.cos(phase), jnp.sin(phase))

def reference(particles, group_ids, ctf_table, references):
    highest = lax.Precision.HIGHEST
    cos_rot, sin_rot, scale = search_tables()
    cos_weighted = cos_rot * scale[:, None]
    sin_weighted = sin_rot * scale[:, None]
    ref_float = references.astype(jnp.float32)
    ref_c, ref_s = angular_spectrum(ref_float)
    ref_c = rounded(ref_c)
    ref_s = rounded(ref_s)
    power = lax.optimization_barrier(jnp.sum(ref_float * ref_float, axis=-1))
    score_scale = 4.0 / math.sqrt(CYCLES * ANG)
    count = particles.shape[0]
    block = math.gcd(count, 256)
    blocks_x = particles.reshape(count // block, block, CYCLES, ANG)
    blocks_g = group_ids.reshape(count // block, block)

    def block_terms(carry, inputs):
        rows, ids = inputs
        onehot = (ids[:, None] == jnp.arange(GROUPS, dtype=jnp.int32)[None, :]).astype(jnp.float32)
        ctf = jnp.dot(onehot, ctf_table, precision=highest)
        spec_c, spec_s = angular_spectrum(rows.astype(jnp.float32))
        y_c = rounded(ctf[:, :, None] * spec_c)
        y_s = rounded(ctf[:, :, None] * spec_s)
        part_a = jnp.einsum('prm,krm->pkm', y_c, ref_c) + jnp.einsum('prm,krm->pkm', y_s, ref_s)
        part_b = jnp.einsum('prm,krm->pkm', y_c, ref_s) - jnp.einsum('prm,krm->pkm', y_s, ref_c)
        cross = jnp.einsum('pkm,mr->pkr', part_a, cos_weighted, precision=highest) - jnp.einsum('pkm,mr->pkr', part_b, sin_weighted, precision=highest)
        energy = jnp.dot(ctf * ctf, power.T, precision=highest)
        score = score_scale * (cross - 0.5 * energy[:, :, None])
        top = lax.optimization_barrier(jnp.max(score, axis=(1, 2), keepdims=True))
        expo = jnp.exp(score - top)
        post = expo / lax.optimization_barrier(jnp.sum(expo, axis=(1, 2), keepdims=True))
        q_c = rounded(jnp.einsum('pkr,mr->pkm', post, cos_rot, precision=highest))
        q_s = rounded(jnp.einsum('pkr,mr->pkm', post, sin_rot, precision=highest))
        sum_c = jnp.einsum('pkm,prm->krm', q_c, y_c) + jnp.einsum('pkm,prm->krm', q_s, y_s)
        sum_s = jnp.einsum('pkm,prm->krm', q_c, y_s) - jnp.einsum('pkm,prm->krm', q_s, y_c)
        weight = jnp.dot(lax.optimization_barrier(jnp.sum(post, axis=2)).T, ctf * ctf, precision=highest)
        return ((carry[0] + sum_c, carry[1] + sum_s, carry[2] + weight), None)
    freqs = ANG // 2 + 1
    start = (jnp.zeros((CLASSES, CYCLES, freqs), jnp.float32), jnp.zeros((CLASSES, CYCLES, freqs), jnp.float32), jnp.zeros((CLASSES, CYCLES), jnp.float32))
    totals, unused = lax.scan(block_terms, start, (blocks_x, blocks_g))
    sum_c, sum_s, weight = totals
    denom = weight[:, :, None] + PRIOR_WEIGHT
    hat_c = rounded(sum_c / denom)
    hat_s = rounded(sum_s / denom)
    inv_cos, inv_sin = inverse_tables()
    inv_cos = inv_cos * scale[:, None]
    inv_sin = inv_sin * scale[:, None]
    result = jnp.einsum('krm,ma->kra', hat_c, inv_cos, precision=highest) + jnp.einsum('krm,ma->kra', hat_s, inv_sin, precision=highest)
    return result.astype(jnp.bfloat16)
```

```python
import math

import jax
import jax.numpy as jnp
from jax import lax
from jax.sharding import Mesh
from jax.sharding import PartitionSpec as P

CYCLES = 64
ANG = 288
ROT = 72
GROUPS = 32
HALF = ANG // 2
LANES = 2 * CYCLES
PRIOR_WEIGHT = 1.0

X, Z, CORE = 2, 16, 2
CHUNK = 113
SLOT = 128

DOM = ("x_lo", "z", "core")
CLS = ("x_hi", "y")
SHARE = ("core", "x_hi", "y")


def phase(rows, cols, factor):
    index = jnp.arange(rows, dtype=jnp.int32)[:, None] * factor * jnp.arange(cols, dtype=jnp.int32)[None, :]
    return 2.0 * math.pi * (index % ANG).astype(jnp.float32) / ANG


def forward_table():
    angle = phase(ANG, HALF + 1, 1)
    cos, sin = jnp.cos(angle), jnp.sin(angle)
    return jnp.concatenate([cos[:, :HALF], cos[:, HALF:], sin[:, 1:HALF]], axis=1)


def inverse_table():
    angle = phase(HALF + 1, ANG, 1)
    cos, sin = jnp.cos(angle), jnp.sin(angle)
    real = jnp.concatenate([cos[:1], 2.0 * cos[1:HALF]], axis=0) / ANG
    imag = jnp.concatenate([cos[HALF:], 2.0 * sin[1:HALF]], axis=0) / ANG
    return real, imag


def narrow(values):
    return lax.optimization_barrier(values.astype(jnp.bfloat16))


def parts(values):
    high = narrow(values)
    low = (values - high.astype(jnp.float32)).astype(jnp.bfloat16)
    return jnp.concatenate([high, low], axis=-1)


def spectra(images):
    rows = images.astype(jnp.float32).reshape(-1, ANG)
    spec = jnp.dot(rows, forward_table(), precision=lax.Precision.HIGHEST)
    return spec.reshape(images.shape[0], CYCLES, 2, HALF)


def swap(axis, value):
    return lax.ppermute(value, axis, [(0, 1), (1, 0)])


def both(axis, mine):
    other = swap(axis, mine)
    first = lax.axis_index(axis) == 0
    return jnp.stack([jnp.where(first, mine, other), jnp.where(first, other, mine)])


def body(particles, group_ids, ctf_table, references):
    highest = lax.Precision.HIGHEST
    core, x_lo, z = (lax.axis_index(name) for name in ("core", "x_lo", "z"))
    kd = references.shape[0] // CORE
    mine = particles.shape[0]

    def factors(ids):
        onehot = (ids[:, None] == jnp.arange(GROUPS, dtype=jnp.int32)[None, :]).astype(jnp.float32)
        return jnp.dot(onehot, ctf_table, precision=highest)

    own = spectra(particles) * factors(group_ids)[:, :, None, None]
    own = own.astype(jnp.bfloat16).transpose(0, 3, 2, 1).reshape(mine * HALF, LANES)
    tags = jnp.broadcast_to(group_ids.astype(jnp.bfloat16)[:, None], (mine, LANES))
    tags = jnp.pad(tags, ((0, 16 - mine), (0, 0)))
    message = jnp.concatenate([own, tags], axis=0)
    shares = CORE * 8
    gathered = lax.all_to_all(
        jnp.broadcast_to(message[None], (shares,) + message.shape), SHARE, 0, 0, tiled=True
    )
    ydata = gathered[:, : mine * HALF].reshape(shares * mine, HALF, LANES).transpose(1, 0, 2)
    ids = gathered[:, mine * HALF : mine * HALF + mine, 0].reshape(-1).astype(jnp.int32)
    ctf_square = factors(ids) ** 2

    refs = lax.dynamic_slice_in_dim(references, core * kd, kd, 0)
    ref_float = refs.astype(jnp.float32)
    power = jnp.sum(ref_float * ref_float, axis=-1)
    ref_spec = spectra(refs).astype(jnp.bfloat16).transpose(3, 0, 2, 1)
    straight = ref_spec.reshape(HALF, kd, LANES)
    turned = jnp.concatenate([ref_spec[:, :, 1], -ref_spec[:, :, 0]], axis=2)
    paired = jnp.einsum(
        "jpl,jkl->jpk",
        ydata,
        jnp.concatenate([straight, turned], axis=1),
        preferred_element_type=jnp.float32,
    )
    angle = phase(HALF, ROT, ANG // ROT)
    cos_rot, sin_rot = jnp.cos(angle), jnp.sin(angle)
    scale = jnp.where(jnp.arange(HALF) == 0, 1.0, 2.0).astype(jnp.float32)[:, None] / ANG
    cross = jnp.einsum("jpk,jr->pkr", paired[:, :, :kd], cos_rot * scale, precision=highest)
    cross = cross - jnp.einsum("jpk,jr->pkr", paired[:, :, kd:], sin_rot * scale, precision=highest)
    energy = jnp.dot(ctf_square, power.T, precision=highest)
    score = 4.0 / math.sqrt(CYCLES * ANG) * (cross - 0.5 * energy[:, :, None])
    top = jnp.max(score, axis=(1, 2))
    expo = jnp.exp(score - top[:, None, None])
    by_class = jnp.sum(expo, axis=2)
    total = jnp.sum(by_class, axis=1)
    stats = jnp.concatenate([top[None], total[None]], axis=0)
    stats = lax.all_to_all(
        jnp.broadcast_to(stats[None], (shares,) + stats.shape), SHARE, 0, 0, tiled=True
    )
    top_all = jnp.max(stats[:, 0], axis=0)
    total_all = jnp.sum(stats[:, 1] * jnp.exp(stats[:, 0] - top_all[None]), axis=0)
    share = jnp.exp(top - top_all) / total_all
    post = expo * share[:, None, None]
    q_cos = jnp.einsum("pkr,jr->jpk", post, cos_rot, precision=highest).astype(jnp.bfloat16)
    q_sin = jnp.einsum("pkr,jr->jpk", post, sin_rot, precision=highest).astype(jnp.bfloat16)
    yturned = jnp.concatenate([ydata[:, :, CYCLES:], -ydata[:, :, :CYCLES]], axis=2)
    sums = jnp.einsum(
        "jpk,jpl->kjl",
        jnp.concatenate([q_cos, q_sin], axis=1),
        jnp.concatenate([ydata, yturned], axis=1),
        preferred_element_type=jnp.float32,
    )
    weight = jnp.einsum("pk,pr->kr", by_class * share[:, None], ctf_square, precision=highest)

    chunks = X * Z
    sums = jnp.pad(sums.reshape(kd * HALF, LANES), ((0, chunks * CHUNK - kd * HALF), (0, 0)))
    sums = sums.reshape(X, Z, CHUNK, LANES)
    first = jnp.minimum(jnp.arange(chunks, dtype=jnp.int32) * CHUNK // HALF, kd - 1)
    second = jnp.minimum(first + 1, kd - 1)
    weights = jnp.stack([weight[first], weight[second]], axis=1).reshape(X, Z, 2, CYCLES)

    def packed(values, scales):
        rows = jnp.concatenate([values.astype(jnp.bfloat16), parts(scales)], axis=-2)
        return jnp.pad(rows, ((0, 0),) * (rows.ndim - 2) + ((0, SLOT - CHUNK - 2), (0, 0)))

    def unpacked(rows):
        rows = rows.astype(jnp.float32)
        scales = rows[..., CHUNK : CHUNK + 2, :]
        return rows[..., :CHUNK, :], scales[..., :CYCLES] + scales[..., CYCLES:]

    def half(values, index):
        return lax.dynamic_index_in_dim(values, index, 0, keepdims=False)

    got, got_scale = unpacked(swap("x_lo", packed(half(sums, 1 - x_lo), half(weights, 1 - x_lo))))
    sent = packed(half(sums, x_lo) + got, half(weights, x_lo) + got_scale)
    got, got_scale = unpacked(lax.all_to_all(sent, "z", 0, 0, tiled=True))
    got, got_scale = jnp.sum(got, axis=0), jnp.sum(got_scale, axis=0) + PRIOR_WEIGHT
    chunk = x_lo * Z + z
    row_class = (chunk * CHUNK + jnp.arange(CHUNK, dtype=jnp.int32)) // HALF
    lead = (row_class == jnp.minimum(chunk * CHUNK // HALF, kd - 1))[:, None]
    scale_rows = jnp.where(lead, got_scale[:1], got_scale[1:])
    hat = (got / jnp.concatenate([scale_rows, scale_rows], axis=1)).astype(jnp.bfloat16)
    hat = jnp.pad(hat, ((0, SLOT - CHUNK), (0, 0)))

    hats = lax.all_to_all(jnp.broadcast_to(hat[None], (Z,) + hat.shape), "z", 0, 0, tiled=True)
    hats = both("core", both("x_lo", hats))
    hats = hats[..., :CHUNK, :].reshape(CORE, chunks * CHUNK, LANES)[:, : kd * HALF]
    hats = hats.reshape(CORE * kd, HALF, LANES).astype(jnp.float32)
    real, imag = inverse_table()
    result = jnp.einsum("kjc,ja->kca", hats[..., :CYCLES], real, precision=highest)
    result = result + jnp.einsum("kjc,ja->kca", hats[..., CYCLES:], imag, precision=highest)
    return result.astype(jnp.bfloat16)


def solution(mesh):
    fine = Mesh(mesh.devices.reshape(X, Z, CORE, 2, 4), DOM + CLS)
    in_specs = (P(DOM + CLS, None, None), P(DOM + CLS), P(), P(CLS, None, None))
    return jax.shard_map(body, mesh=fine, in_specs=in_specs, out_specs=P(CLS, None, None), check_vma=False)
```

```python
import functools
import math

import jax
import jax.numpy as jnp
import ml_dtypes
import numpy as np
from jax import lax
from jax.experimental import pallas as pl
from jax.experimental.pallas import tpu as pltpu
from jax.sharding import Mesh
from jax.sharding import PartitionSpec as P

CYCLES = 64
ANG = 288
ROT = 72
HALF = ANG // 2
LANES = 2 * CYCLES
PRIOR_WEIGHT = 1.0
SCORE_SCALE = 4.0 / math.sqrt(CYCLES * ANG)

X, Z, CORE, SIDE = 2, 16, 2, 8
MINE = 2
PER_CORE = 25
KD = 13
KPAD = 16
KROWS = KPAD // 2
SOURCES = X * SIDE
COUNT = MINE * CORE * SOURCES
MSG = MINE * HALF + 16
CHUNK = KD * HALF // Z
SLOT = 128

DOM = ("x_lo", "z", "core")
CLS = ("x_hi", "y")

NT = (((1,), (1,)), ((), ()))
NN = (((1,), (0,)), ((), ()))
f32 = jnp.float32
bf16 = jnp.bfloat16


def angles(rows, cols, factor):
    index = np.arange(rows)[:, None] * factor * np.arange(cols)[None, :] % ANG
    return 2.0 * math.pi * index / ANG


def split(table):
    table = table.astype(np.float32)
    high = table.astype(ml_dtypes.bfloat16)
    low = (table - high.astype(np.float32)).astype(ml_dtypes.bfloat16)
    return np.stack([high, low])


def forward_table():
    angle = angles(HALF + 1, ANG, 1)
    real = np.cos(angle[:HALF])
    imag = np.concatenate([np.cos(angle[HALF:]), np.sin(angle[1:HALF])])
    return split(np.concatenate([real, imag]))


def weights_of_rows():
    return np.where(np.arange(HALF) == 0, 1.0, 2.0)[:, None] / ANG


def search_table():
    angle = angles(HALF, ROT, ANG // ROT)
    scale = weights_of_rows()
    return split(np.concatenate([np.cos(angle) * scale, -np.sin(angle) * scale]).T)


def post_table():
    angle = angles(HALF, ROT, ANG // ROT)
    return split(np.concatenate([np.cos(angle), np.sin(angle)]))


def inverse_table():
    angle = angles(HALF + 1, ANG, 1)
    scale = weights_of_rows()
    real = np.cos(angle[:HALF]) * scale
    imag = np.concatenate([np.cos(angle[HALF:]), np.sin(angle[1:HALF])]) * scale
    return np.concatenate([split(real), split(imag)])


def dot(a, b, dims=NN):
    return lax.dot_general(a, b, dims, preferred_element_type=f32)


def halves(values):
    high = values.astype(bf16)
    return high, (values - high.astype(f32)).astype(bf16)


def dot3(table, values):
    high, low = halves(values)
    return dot(table[0], high) + (dot(table[0], low) + dot(table[1], high))


def turn(values):
    return pltpu.roll(values, CYCLES, 1)


def left(shape):
    return lax.broadcasted_iota(jnp.int32, shape, len(shape) - 1) < CYCLES


def fold(spec):
    real, imag = spec[:HALF], spec[HALF:]
    side = left(real.shape)
    return jnp.where(side, real, turn(imag)), jnp.where(side, turn(real), imag)


def share_kernel(ids, x, ctf, table, out):
    images = x[...].reshape(MINE * CYCLES, ANG)
    factor = jnp.concatenate([ctf[pl.ds(ids[0], 1), :], ctf[pl.ds(ids[1], 1), :]], axis=1)
    spec = (dot(table[0], images, NT) + dot(table[1], images, NT)) * factor
    first, second = fold(spec)
    out[0:HALF] = first.astype(bf16)
    out[HALF : 2 * HALF] = second.astype(bf16)
    high, rest = halves(factor)
    rest = factor - high.astype(f32)
    mid = rest.astype(bf16)
    low = rest - mid.astype(f32)
    row = lax.broadcasted_iota(jnp.int32, (16, LANES), 0)
    tags = jnp.where(row == 0, high.astype(f32), jnp.where(row == 1, mid.astype(f32), jnp.where(row == 2, low, 0.0)))
    out[2 * HALF : MSG] = tags.astype(bf16)


def class_kernel(start, refs, table, out, power, images, rows, sem):
    copy = pltpu.make_async_copy(refs.at[pl.ds(start[0], KD)], images.at[pl.ds(0, KD)], sem)
    copy.start()
    images[KD:] = jnp.zeros((KPAD - KD, CYCLES, ANG), bf16)
    ones = jnp.ones((8, ANG), bf16)
    copy.wait()
    for step in range(KPAD // 4):
        block = images[4 * step : 4 * step + 4].reshape(4 * CYCLES, ANG)
        spec = dot(table[0], block, NT) + dot(table[1], block, NT)
        wide = block.astype(f32)
        high, low = halves(wide * wide)
        energy = dot(ones, high, NT) + dot(ones, low, NT)
        for pair in range(2):
            k = 4 * step + 2 * pair
            lanes = slice(pair * LANES, (pair + 1) * LANES)
            first, second = fold(spec[:, lanes])
            rows[k * HALF : (k + 1) * HALF] = first.astype(bf16).astype(f32)
            rows[(k + 1) * HALF : (k + 2) * HALF] = second.astype(bf16).astype(f32)
            part = energy[:, lanes]
            side = left(part.shape)
            power[k : k + 1] = jnp.where(side, part, 0.0)[0:1]
            power[k + 1 : k + 2] = jnp.where(side, turn(part), 0.0)[0:1]

    def step(j, carry):
        plain = rows[pl.ds(j, KPAD, stride=HALF), :]
        other = turn(plain)
        other = jnp.where(left(other.shape), other, -other)
        out[j] = jnp.concatenate([plain, other], axis=0).astype(bf16)
        return carry

    lax.fori_loop(0, HALF, step, 0, unroll=8)


def score_kernel(place, own, other, rmat, power, table, expo, stats, by_class, ydata, csq, wide, pairs):
    core, x_lo = place[0], place[1]

    def widen(s, carry):
        mine = pl.multiple_of((core * SOURCES + s) * MSG, 8)
        theirs = pl.multiple_of(((1 - core) * SOURCES + s) * MSG, 8)
        wide[pl.ds(mine, MSG), :] = own[s].astype(f32)
        wide[pl.ds(theirs, MSG), :] = other[s].astype(f32)
        return carry

    lax.fori_loop(0, SOURCES, widen, 0)
    many = CORE * SOURCES
    factor = wide[pl.ds(2 * HALF, many, stride=MSG), :] + wide[pl.ds(2 * HALF + 1, many, stride=MSG), :]
    factor = factor + wide[pl.ds(2 * HALF + 2, many, stride=MSG), :]
    square = factor * factor
    side = left(square.shape)
    square = jnp.concatenate([jnp.where(side, square, 0.0), jnp.where(side, turn(square), 0.0)], axis=0)
    csq[...] = square
    energy = lax.dot_general(
        power[...],
        jnp.concatenate([square, square], axis=0),
        NT,
        precision=lax.Precision.HIGHEST,
        preferred_element_type=f32,
    )
    side = left((KROWS, LANES))
    energy = jnp.where(side, energy[:KROWS], energy[KROWS:])

    def step(j, carry):
        rows = jnp.concatenate([wide[pl.ds(j, many, stride=MSG), :], wide[pl.ds(HALF + j, many, stride=MSG), :]], axis=0)
        rows = rows.astype(bf16)
        ydata[j] = rows
        both = dot(rmat[j], jnp.concatenate([rows, rows], axis=0), NT)
        side = left((KROWS, LANES))
        straight = jnp.where(side, both[:KROWS], both[KROWS : 2 * KROWS])
        crossed = jnp.where(side, both[2 * KROWS : 3 * KROWS], both[3 * KROWS :])
        pairs[pl.ds(j, KROWS, stride=ANG), :] = straight
        pairs[pl.ds(HALF + j, KROWS, stride=ANG), :] = crossed
        return carry

    lax.fori_loop(0, HALF, step, 0, unroll=8)
    top = jnp.full((1, LANES), -3.0e38, f32)
    lane_side = left((ROT, LANES))
    for kk in range(KROWS):
        cross = dot3(table, pairs[kk * ANG : (kk + 1) * ANG])
        score = SCORE_SCALE * (cross - 0.5 * energy[kk : kk + 1])
        if kk + KROWS >= KD:
            score = jnp.where(lane_side, score, -3.0e38)
        if kk == 0:
            score = jnp.where(jnp.logical_and(lane_side, x_lo == 1), -3.0e38, score)
        expo[:, kk * LANES : (kk + 1) * LANES] = score
        top = jnp.maximum(top, jnp.max(score, axis=0, keepdims=True))
    top = jnp.maximum(top, turn(top))
    total = jnp.zeros((1, LANES), f32)
    for kk in range(KROWS):
        value = jnp.exp(expo[:, kk * LANES : (kk + 1) * LANES] - top)
        expo[:, kk * LANES : (kk + 1) * LANES] = value
        part = jnp.sum(value, axis=0, keepdims=True)
        by_class[kk : kk + 1] = part
        total = total + part
    total = total + turn(total)
    stats[...] = jnp.where(lax.broadcasted_iota(jnp.int32, (8, LANES), 0) == 0, top, total)


def post_kernel(expo, table, out, rows):
    for kk in range(KROWS):
        rows[kk * ANG : (kk + 1) * ANG] = dot3(table, expo[:, kk * LANES : (kk + 1) * LANES])

    def step(j, carry):
        real = rows[pl.ds(j, KROWS, stride=ANG), :]
        imag = rows[pl.ds(HALF + j, KROWS, stride=ANG), :]
        out[j] = jnp.concatenate([real, turn(real), imag, turn(imag)], axis=0)
        return carry

    lax.fori_loop(0, HALF, step, 0, unroll=8)


def sum_kernel(all_stats, stats, post, ydata, by_class, csq, out, rows, slots):
    tops, totals = all_stats[:, 0, :], all_stats[:, 1, :]
    top = jnp.max(tops, axis=0, keepdims=True)
    total = jnp.sum(totals * jnp.exp(tops - top), axis=0, keepdims=True)
    share = jnp.exp(stats[0:1] - top) / total

    def step(j, carry):
        weights = (post[j] * share)[:, :CYCLES].astype(bf16)
        both = dot(weights, ydata[j])
        other = turn(both[KPAD:])
        other = jnp.where(left(other.shape), other, -other)
        rows[pl.ds(j, KPAD, stride=HALF), :] = both[:KPAD] + other
        return carry

    lax.fori_loop(0, HALF, step, 0, unroll=8)
    mass = by_class[...] * share
    mass = jnp.concatenate([mass, turn(mass)], axis=0)[:, :CYCLES]
    weight = lax.dot_general(mass, csq[...], NN, precision=lax.Precision.HIGHEST, preferred_element_type=f32)
    high, low = halves(weight)
    scales = jnp.where(left(weight.shape), high.astype(f32), turn(low.astype(f32)))
    for z in range(Z):
        first = z * CHUNK // HALF
        second = min(first + 1, KD - 1)
        base = z * SLOT
        slots[base + SLOT - 16 : base + SLOT] = jnp.zeros((16, LANES), f32)
        slots[base : base + CHUNK] = rows[z * CHUNK : (z + 1) * CHUNK]
        slots[base + CHUNK : base + CHUNK + 1] = scales[first : first + 1]
        slots[base + CHUNK + 1 : base + CHUNK + 2] = scales[second : second + 1]
        out[z] = slots[base : base + SLOT].astype(bf16)


def image_kernel(place, hats, table, *rest):
    out, flat, real, imag, stage, sem = rest[-6:]
    core, x_lo = place[0], place[1]
    for z in range(Z):
        flat[z * CHUNK : (z + 1) * CHUNK] = hats[z].astype(f32)[:CHUNK]
    for k in range(KD):
        rows = flat[k * HALF : (k + 1) * HALF].T.astype(bf16)
        real[k * CYCLES : (k + 1) * CYCLES] = rows[:CYCLES]
        imag[k * CYCLES : (k + 1) * CYCLES] = rows[CYCLES:]
    for k in range(KD):
        lines = slice(k * CYCLES, (k + 1) * CYCLES)
        image = dot(real[lines], table[0]) + dot(imag[lines], table[2])
        image = image + (dot(real[lines], table[1]) + dot(imag[lines], table[3]))
        stage[k] = image.astype(bf16)
    base = core * PER_CORE + x_lo * (KD - 1)
    copy = pltpu.make_async_copy(stage.at[pl.ds(x_lo, KD - 1)], out.at[pl.ds(base + x_lo, KD - 1)], sem.at[0])
    copy.start()

    @pl.when(x_lo == 0)
    def _():
        last = pltpu.make_async_copy(stage.at[pl.ds(KD - 1, 1)], out.at[pl.ds(base + KD - 1, 1)], sem.at[1])
        last.start()
        last.wait()

    copy.wait()


VMEM = pl.BlockSpec(memory_space=pltpu.VMEM)
SMEM = pl.BlockSpec(memory_space=pltpu.SMEM)
ANYWHERE = pl.BlockSpec(memory_space=pl.ANY)


def call(kernel, ins, outs, scratch, flops, nbytes, aliases=None, out_specs=None):
    out_shape = [jax.ShapeDtypeStruct(shape, dtype) for shape, dtype in outs]
    single = len(out_shape) == 1
    specs = out_specs or [VMEM] * len(out_shape)
    return pl.pallas_call(
        kernel,
        out_shape=out_shape[0] if single else out_shape,
        in_specs=ins,
        out_specs=specs[0] if single else specs,
        scratch_shapes=scratch,
        input_output_aliases=aliases or {},
        compiler_params=pltpu.CompilerParams(vmem_limit_bytes=48 * 2**20),
        cost_estimate=pl.CostEstimate(flops=flops, bytes_accessed=nbytes, transcendentals=0),
    )


def swap(axis, value):
    return lax.ppermute(value, axis, [(0, 1), (1, 0)])


def spread(value, axes, count):
    return lax.all_to_all(jnp.broadcast_to(value[None], (count,) + value.shape), axes, 0, 0, tiled=True)


def body(particles, group_ids, ctf_table, references):
    core, x_lo, z = (lax.axis_index(name) for name in ("core", "x_lo", "z"))
    forward = jnp.asarray(forward_table())
    place = jnp.stack([core, x_lo])

    message = call(
        share_kernel, [SMEM, VMEM, VMEM, VMEM], [((MSG, LANES), bf16)], [], 10**7, 10**6
    )(group_ids, particles, ctf_table, forward)
    own = spread(message, ("x_lo", "x_hi", "y"), SOURCES)
    other = swap("core", own)

    start = (core * PER_CORE + x_lo * (KD - 1)).reshape(1)
    rmat, power = call(
        class_kernel,
        [SMEM, ANYWHERE, VMEM],
        [((HALF, 2 * KPAD, LANES), bf16), ((KPAD, LANES), f32)],
        [
            pltpu.VMEM((KPAD, CYCLES, ANG), bf16),
            pltpu.VMEM((KPAD * HALF, LANES), f32),
            pltpu.SemaphoreType.DMA,
        ],
        10**9,
        4 * 10**6,
    )(start, references, forward)

    expo, stats, by_class, ydata, csq = call(
        score_kernel,
        [SMEM] + [VMEM] * 5,
        [
            ((ROT, KROWS * LANES), f32),
            ((8, LANES), f32),
            ((KROWS, LANES), f32),
            ((HALF, COUNT, LANES), bf16),
            ((COUNT, LANES), f32),
        ],
        [
            pltpu.VMEM((CORE * SOURCES * MSG, LANES), f32),
            pltpu.VMEM((KROWS * ANG, LANES), f32),
        ],
        10**9,
        8 * 10**6,
    )(place, own, other, rmat, power, jnp.asarray(search_table()))
    all_stats = spread(stats, ("core", "x_lo", "x_hi", "y"), CORE * SOURCES)
    post = call(
        post_kernel,
        [VMEM, VMEM],
        [((HALF, 2 * KPAD, LANES), f32)],
        [pltpu.VMEM((KROWS * ANG, LANES), f32)],
        10**9,
        3 * 10**6,
    )(expo, jnp.asarray(post_table()))
    sums = call(
        sum_kernel,
        [VMEM] * 6,
        [((Z, SLOT, LANES), bf16)],
        [pltpu.VMEM((KPAD * HALF, LANES), f32), pltpu.VMEM((Z * SLOT, LANES), f32)],
        10**9,
        8 * 10**6,
    )(all_stats, stats, post, ydata, by_class, csq)

    got = jnp.sum(lax.all_to_all(sums, "z", 0, 0, tiled=True).astype(f32), axis=0)
    scales = got[CHUNK : CHUNK + 2]
    scales = scales[:, :CYCLES] + scales[:, CYCLES:] + PRIOR_WEIGHT
    scales = jnp.concatenate([scales, scales], axis=1)
    row = lax.broadcasted_iota(jnp.int32, (SLOT, LANES), 0)
    edge = (z * CHUNK // HALF + 1) * HALF - z * CHUNK
    hat = (got / jnp.where(row < edge, scales[:1], scales[1:])).astype(bf16)

    near = lax.all_gather(hat, "z")
    far = swap("x_lo", near)
    inverse = jnp.asarray(inverse_table())
    result = None
    for hats, which in (
        (near, (core, x_lo)),
        (swap("core", near), (1 - core, x_lo)),
        (far, (core, 1 - x_lo)),
        (swap("core", far), (1 - core, 1 - x_lo)),
    ):
        extra = [] if result is None else [result]
        result = call(
            image_kernel,
            [SMEM, VMEM, VMEM] + [ANYWHERE] * len(extra),
            [((CORE * PER_CORE, CYCLES, ANG), bf16)],
            [
                pltpu.VMEM((KD * HALF, LANES), f32),
                pltpu.VMEM((KD * CYCLES, HALF), bf16),
                pltpu.VMEM((KD * CYCLES, HALF), bf16),
                pltpu.VMEM((KD, CYCLES, ANG), bf16),
                pltpu.SemaphoreType.DMA((2,)),
            ],
            10**9,
            2 * 10**6,
            {3: 0} if extra else None,
            [ANYWHERE],
        )(jnp.stack(which), hats, inverse, *extra)
    return result


def solution(mesh):
    fine = Mesh(mesh.devices.reshape(X, Z, CORE, 2, 4), DOM + CLS)
    in_specs = (P(DOM + CLS, None, None), P(DOM + CLS), P(), P(CLS, None, None))
    return jax.shard_map(body, mesh=fine, in_specs=in_specs, out_specs=P(CLS, None, None), check_vma=False)
```

```python
import math

import jax
import jax.numpy as jnp
import ml_dtypes
import numpy as np
from jax import lax
from jax.experimental import pallas as pl
from jax.experimental.pallas import tpu as pltpu
from jax.sharding import Mesh
from jax.sharding import PartitionSpec as P

CYCLES = 64
ANG = 288
ROT = 72
HALF = ANG // 2
LANES = 2 * CYCLES
PRIOR_WEIGHT = 1.0
SCORE_SCALE = 4.0 / math.sqrt(CYCLES * ANG)

X, Z, CORE, SIDE = 2, 16, 2, 8
ZH, ZL = 4, 4
MINE = 2
PER_CORE = 25
KD = 13
KPAD = 16
KROWS = KPAD // 2
PARTS = 2
SOURCES = X * SIDE
COUNT = MINE * CORE * SOURCES
MSG = MINE * HALF + 16
CHUNK = KD * HALF // Z
SLOT = 120

DOM = ("x_lo", "z_hi", "z_lo", "core")
CLS = ("x_hi", "y")

NT = (((1,), (1,)), ((), ()))
NN = (((1,), (0,)), ((), ()))
f32 = jnp.float32
bf16 = jnp.bfloat16


def angles(rows, cols, factor):
    index = np.arange(rows)[:, None] * factor * np.arange(cols)[None, :] % ANG
    return 2.0 * math.pi * index / ANG


def split(table):
    table = table.astype(np.float32)
    high = table.astype(ml_dtypes.bfloat16)
    low = (table - high.astype(np.float32)).astype(ml_dtypes.bfloat16)
    return np.stack([high, low])


def forward_table():
    angle = angles(HALF + 1, ANG, 1)
    real = np.cos(angle[:HALF])
    imag = np.concatenate([np.cos(angle[HALF:]), np.sin(angle[1:HALF])])
    return split(np.concatenate([real, imag]))


def weights_of_rows():
    return np.where(np.arange(HALF) == 0, 1.0, 2.0)[:, None] / ANG


def search_table():
    angle = angles(HALF, ROT, ANG // ROT)
    scale = weights_of_rows()
    return split(np.concatenate([np.cos(angle) * scale, -np.sin(angle) * scale]).T)


def post_table():
    angle = angles(HALF, ROT, ANG // ROT)
    return split(np.concatenate([np.cos(angle), np.sin(angle)]))


def inverse_table():
    angle = angles(HALF + 1, ANG, 1)
    scale = weights_of_rows()
    real = np.cos(angle[:HALF]) * scale
    imag = np.concatenate([np.cos(angle[HALF:]), np.sin(angle[1:HALF])]) * scale
    return np.concatenate([split(real), split(imag)])


def dot(a, b, dims=NN):
    return lax.dot_general(a, b, dims, preferred_element_type=f32)


def halves(values):
    high = values.astype(bf16)
    return high, (values - high.astype(f32)).astype(bf16)


def dot3(table, values):
    high, low = halves(values)
    rows = table.shape[0] // 2
    both = dot(table[...], high)
    return both[:rows] + (both[rows:] + dot(table[:rows], low))


def turn(values):
    return pltpu.roll(values, CYCLES, 1)


def left(shape):
    return lax.broadcasted_iota(jnp.int32, shape, len(shape) - 1) < CYCLES


def fold(spec):
    real, imag = spec[:HALF], spec[HALF:]
    side = left(real.shape)
    return jnp.where(side, real, turn(imag)), jnp.where(side, turn(real), imag)


def share_kernel(ids, x, ctf, table, outs, out, sem):
    images = x[...].reshape(MINE * CYCLES, ANG)
    factor = jnp.concatenate([ctf[pl.ds(ids[0], 1), :], ctf[pl.ds(ids[1], 1), :]], axis=1)
    spec = (dot(table[0], images, NT) + dot(table[1], images, NT)) * factor
    first, second = fold(spec)
    out[0:HALF] = first.astype(bf16)
    out[HALF : 2 * HALF] = second.astype(bf16)
    high, rest = halves(factor)
    rest = factor - high.astype(f32)
    mid = rest.astype(bf16)
    low = rest - mid.astype(f32)
    row = lax.broadcasted_iota(jnp.int32, (16, LANES), 0)
    tags = jnp.where(row == 0, high.astype(f32), jnp.where(row == 1, mid.astype(f32), jnp.where(row == 2, low, 0.0)))
    out[2 * HALF : MSG] = tags.astype(bf16)
    copies = [pltpu.make_async_copy(out, outs.at[s], sem.at[s]) for s in range(SOURCES)]
    for copy in copies:
        copy.start()
    for copy in copies:
        copy.wait()


def class_kernel(start, refs, table, out, power, images, rows, sem):
    copy = pltpu.make_async_copy(refs.at[pl.ds(start[0], KD)], images.at[pl.ds(0, KD)], sem)
    copy.start()
    images[KD:] = jnp.zeros((KPAD - KD, CYCLES, ANG), bf16)
    ones = jnp.ones((8, ANG), bf16)
    copy.wait()
    for step in range(KPAD // 4):
        block = images[4 * step : 4 * step + 4].reshape(4 * CYCLES, ANG)
        spec = dot(table[0], block, NT) + dot(table[1], block, NT)
        wide = block.astype(f32)
        high, low = halves(wide * wide)
        energy = dot(ones, high, NT) + dot(ones, low, NT)
        for pair in range(2):
            k = 4 * step + 2 * pair
            lanes = slice(pair * LANES, (pair + 1) * LANES)
            first, second = fold(spec[:, lanes])
            rows[k * HALF : (k + 1) * HALF] = first.astype(bf16).astype(f32)
            rows[(k + 1) * HALF : (k + 2) * HALF] = second.astype(bf16).astype(f32)
            part = energy[:, lanes]
            side = left(part.shape)
            power[k : k + 1] = jnp.where(side, part, 0.0)[0:1]
            power[k + 1 : k + 2] = jnp.where(side, turn(part), 0.0)[0:1]

    def step(j, carry):
        plain = rows[pl.ds(j, KPAD, stride=HALF), :]
        other = turn(plain)
        other = jnp.where(left(other.shape), other, -other)
        out[j] = jnp.concatenate([plain, other], axis=0).astype(bf16)
        return carry

    lax.fori_loop(0, HALF, step, 0, unroll=36)


def score_kernel(place, own, other, rmat, power, table, expo, stats, by_class, csq, far, wide, pairs, ydata, sem):
    core, x_lo = place[0], place[1]

    def widen(s, carry):
        mine = pl.multiple_of((core * SOURCES + s) * MSG, 8)
        theirs = pl.multiple_of(((1 - core) * SOURCES + s) * MSG, 8)
        wide[pl.ds(mine, MSG), :] = own[s].astype(f32)
        wide[pl.ds(theirs, MSG), :] = other[s].astype(f32)
        return carry

    lax.fori_loop(0, SOURCES, widen, 0)
    many = CORE * SOURCES
    factor = wide[pl.ds(2 * HALF, many, stride=MSG), :] + wide[pl.ds(2 * HALF + 1, many, stride=MSG), :]
    factor = factor + wide[pl.ds(2 * HALF + 2, many, stride=MSG), :]
    square = factor * factor
    side = left(square.shape)
    square = jnp.concatenate([jnp.where(side, square, 0.0), jnp.where(side, turn(square), 0.0)], axis=0)
    csq[...] = square
    energy = lax.dot_general(
        power[...],
        jnp.concatenate([square, square], axis=0),
        NT,
        precision=lax.Precision.HIGHEST,
        preferred_element_type=f32,
    )
    side = left((KROWS, LANES))
    energy = jnp.where(side, energy[:KROWS], energy[KROWS:])

    def step(j, carry):
        rows = jnp.concatenate([wide[pl.ds(j, many, stride=MSG), :], wide[pl.ds(HALF + j, many, stride=MSG), :]], axis=0)
        rows = rows.astype(bf16)
        ydata[j] = rows
        both = dot(rmat[j], rows, NT)
        straight = jnp.concatenate([both[:KROWS], both[KROWS : 2 * KROWS]], axis=1)
        crossed = jnp.concatenate([both[2 * KROWS : 3 * KROWS], both[3 * KROWS :]], axis=1)
        pairs[pl.ds(j, KROWS, stride=ANG), :] = straight
        pairs[pl.ds(HALF + j, KROWS, stride=ANG), :] = crossed
        return carry

    lax.fori_loop(0, HALF, step, 0, unroll=48)
    keep = pltpu.make_async_copy(ydata, far, sem)
    keep.start()
    top = jnp.full((1, LANES), -3.0e38, f32)
    lane_side = left((ROT, LANES))
    for kk in range(KROWS):
        cross = dot3(table, pairs[kk * ANG : (kk + 1) * ANG])
        score = SCORE_SCALE * (cross - 0.5 * energy[kk : kk + 1])
        if kk + KROWS >= KD:
            score = jnp.where(lane_side, score, -3.0e38)
        if kk == 0:
            score = jnp.where(jnp.logical_and(lane_side, x_lo == 1), -3.0e38, score)
        expo[:, kk * LANES : (kk + 1) * LANES] = score
        top = jnp.maximum(top, jnp.max(score, axis=0, keepdims=True))
    top = jnp.maximum(top, turn(top))
    total = jnp.zeros((1, LANES), f32)
    for kk in range(KROWS):
        value = jnp.exp(expo[:, kk * LANES : (kk + 1) * LANES] - top)
        expo[:, kk * LANES : (kk + 1) * LANES] = value
        part = jnp.sum(value, axis=0, keepdims=True)
        by_class[kk : kk + 1] = part
        total = total + part
    total = total + turn(total)
    pair = jnp.where(lax.broadcasted_iota(jnp.int32, (8, LANES), 0) == 0, top, total)
    for s in range(CORE * SOURCES):
        stats[s] = pair
    keep.wait()


def post_kernel(expo, table, far, rows, out, sem):
    for kk in range(KROWS):
        rows[kk * ANG : (kk + 1) * ANG] = dot3(table, expo[:, kk * LANES : (kk + 1) * LANES])

    def step(j, carry):
        real = rows[pl.ds(j, KROWS, stride=ANG), :]
        imag = rows[pl.ds(HALF + j, KROWS, stride=ANG), :]
        out[j] = jnp.concatenate([real, imag], axis=0)
        return carry

    lax.fori_loop(0, HALF, step, 0, unroll=36)
    keep = pltpu.make_async_copy(out, far, sem)
    keep.start()
    keep.wait()


def sum_kernel(all_stats, stats, by_class, csq, far_post, far_ydata, out, rows, slots, post, ydata, sem):
    copies = []
    for part in range(PARTS):
        lines = pl.ds(part * HALF // PARTS, HALF // PARTS)
        copies.append(pltpu.make_async_copy(far_post.at[lines], post.at[lines], sem.at[0, part]))
        copies.append(pltpu.make_async_copy(far_ydata.at[lines], ydata.at[lines], sem.at[1, part]))
    for copy in copies:
        copy.start()
    tops, totals = all_stats[:, 0, :], all_stats[:, 1, :]
    top = jnp.max(tops, axis=0, keepdims=True)
    total = jnp.sum(totals * jnp.exp(tops - top), axis=0, keepdims=True)
    share = jnp.exp(stats[0, 0:1] - top) / total

    def step(j, carry):
        wide = post[j] * share
        real, imag = wide[:KROWS], wide[KROWS:]
        weights = jnp.concatenate([real, turn(real), imag, turn(imag)], axis=0)[:, :CYCLES]
        both = dot(weights.astype(bf16), ydata[j])
        other = turn(both[KPAD:])
        other = jnp.where(left(other.shape), other, -other)
        rows[pl.ds(j, KPAD, stride=HALF), :] = both[:KPAD] + other
        return carry

    for part in range(PARTS):
        copies[2 * part].wait()
        copies[2 * part + 1].wait()
        lax.fori_loop(part * HALF // PARTS, (part + 1) * HALF // PARTS, step, 0, unroll=HALF // PARTS)
    mass = by_class[...] * share
    mass = jnp.concatenate([mass, turn(mass)], axis=0)[:, :CYCLES]
    weight = lax.dot_general(mass, csq[...], NN, precision=lax.Precision.HIGHEST, preferred_element_type=f32)
    high, low = halves(weight)
    scales = jnp.where(left(weight.shape), high.astype(f32), turn(low.astype(f32)))
    for z in range(Z):
        first = z * CHUNK // HALF
        second = min(first + 1, KD - 1)
        base = z * SLOT
        slots[base + SLOT - 8 : base + SLOT] = jnp.zeros((8, LANES), f32)
        slots[base : base + CHUNK] = rows[z * CHUNK : (z + 1) * CHUNK]
        slots[base + CHUNK : base + CHUNK + 1] = scales[first : first + 1]
        slots[base + CHUNK + 1 : base + CHUNK + 2] = scales[second : second + 1]
        out[z % ZL, z // ZL] = slots[base : base + SLOT].astype(bf16)


def fold_kernel(pieces, out):
    total = pieces[0].astype(f32)
    for s in range(1, ZL):
        total = total + pieces[s].astype(f32)
    last = SLOT - 8
    row = lax.broadcasted_iota(jnp.int32, (8, LANES), 0)
    for h in range(ZH):
        rows = total[h, last:]
        scales = rows + turn(rows)
        high = scales.astype(bf16).astype(f32)
        scales = jnp.where(left(scales.shape), high, scales - high)
        rows = jnp.where(row < CHUNK - last, rows, scales)
        out[h] = jnp.concatenate([total[h, :last], rows], axis=0).astype(bf16)


def image_kernel(place, hats, table, *rest):
    out, flat, real, imag, stage, sem = rest[-6:]
    core, x_lo = place[0], place[1]
    for z in range(Z):
        flat[z * CHUNK : (z + 1) * CHUNK] = hats[z].astype(f32)[:CHUNK]
    for k in range(KD):
        rows = flat[k * HALF : (k + 1) * HALF].T.astype(bf16)
        real[k * CYCLES : (k + 1) * CYCLES] = rows[:CYCLES]
        imag[k * CYCLES : (k + 1) * CYCLES] = rows[CYCLES:]
    image = dot(real[...], table[0]) + dot(imag[...], table[2])
    image = image + (dot(real[...], table[1]) + dot(imag[...], table[3]))
    stage[...] = image.astype(bf16).reshape(KD, CYCLES, ANG)
    base = core * PER_CORE + x_lo * (KD - 1)
    copy = pltpu.make_async_copy(stage.at[pl.ds(x_lo, KD - 1)], out.at[pl.ds(base + x_lo, KD - 1)], sem.at[0])
    copy.start()

    @pl.when(x_lo == 0)
    def _():
        last = pltpu.make_async_copy(stage.at[pl.ds(KD - 1, 1)], out.at[pl.ds(base + KD - 1, 1)], sem.at[1])
        last.start()
        last.wait()

    copy.wait()


VMEM = pl.BlockSpec(memory_space=pltpu.VMEM)
SMEM = pl.BlockSpec(memory_space=pltpu.SMEM)
HBM = pl.BlockSpec(memory_space=pltpu.HBM)


def call(kernel, ins, outs, scratch, flops, nbytes, aliases=None, out_specs=None, limit=48):
    out_shape = [jax.ShapeDtypeStruct(shape, dtype) for shape, dtype in outs]
    single = len(out_shape) == 1
    specs = out_specs or [VMEM] * len(out_shape)
    return pl.pallas_call(
        kernel,
        out_shape=out_shape[0] if single else out_shape,
        in_specs=ins,
        out_specs=specs[0] if single else specs,
        scratch_shapes=scratch,
        input_output_aliases=aliases or {},
        compiler_params=pltpu.CompilerParams(vmem_limit_bytes=limit * 2**20),
        cost_estimate=pl.CostEstimate(flops=flops, bytes_accessed=nbytes, transcendentals=0),
    )


def swap(axis, value):
    return lax.ppermute(value, axis, [(0, 1), (1, 0)])


def share(group_ids, particles, ctf_table, forward):
    return call(
        share_kernel,
        [SMEM, VMEM, VMEM, VMEM],
        [((SOURCES, MSG, LANES), bf16)],
        [pltpu.VMEM((MSG, LANES), bf16), pltpu.SemaphoreType.DMA((SOURCES,))],
        10**7,
        10**6,
        out_specs=[HBM],
        limit=64,
    )(group_ids, particles, ctf_table, forward)


def classes(start, references, forward):
    return call(
        class_kernel,
        [SMEM, HBM, VMEM],
        [((HALF, 2 * KPAD, LANES), bf16), ((KPAD, LANES), f32)],
        [
            pltpu.VMEM((KPAD, CYCLES, ANG), bf16),
            pltpu.VMEM((KPAD * HALF, LANES), f32),
            pltpu.SemaphoreType.DMA,
        ],
        10**9,
        4 * 10**6,
        limit=64,
    )(start, references, forward)


def scores(place, own, other, rmat, power, table):
    return call(
        score_kernel,
        [SMEM] + [VMEM] * 5,
        [
            ((ROT, KROWS * LANES), f32),
            ((CORE * SOURCES, 8, LANES), f32),
            ((KROWS, LANES), f32),
            ((COUNT, LANES), f32),
            ((HALF, COUNT, LANES), bf16),
        ],
        [
            pltpu.VMEM((CORE * SOURCES * MSG, LANES), f32),
            pltpu.VMEM((KROWS * ANG, LANES), f32),
            pltpu.VMEM((HALF, COUNT, LANES), bf16),
            pltpu.SemaphoreType.DMA,
        ],
        10**9,
        8 * 10**6,
        limit=64,
        out_specs=[VMEM] * 4 + [HBM],
    )(place, own, other, rmat, power, table)


def posts(expo, table):
    return call(
        post_kernel,
        [VMEM, VMEM],
        [((HALF, KPAD, LANES), f32)],
        [
            pltpu.VMEM((KROWS * ANG, LANES), f32),
            pltpu.VMEM((HALF, KPAD, LANES), f32),
            pltpu.SemaphoreType.DMA,
        ],
        10**9,
        3 * 10**6,
        limit=64,
        out_specs=[HBM],
    )(expo, table)


def sums_of(all_stats, stats, by_class, csq, post, ydata):
    return call(
        sum_kernel,
        [VMEM] * 4 + [HBM] * 2,
        [((ZL, ZH, SLOT, LANES), bf16)],
        [
            pltpu.VMEM((KPAD * HALF, LANES), f32),
            pltpu.VMEM((Z * SLOT, LANES), f32),
            pltpu.VMEM((HALF, KPAD, LANES), f32),
            pltpu.VMEM((HALF, COUNT, LANES), bf16),
            pltpu.SemaphoreType.DMA((2, PARTS)),
        ],
        10**9,
        8 * 10**6,
        limit=64,
    )(all_stats, stats, by_class, csq, post, ydata)


def images(which, hats, inverse, result):
    extra = [] if result is None else [result]
    return call(
        image_kernel,
        [SMEM, VMEM, VMEM] + [HBM] * len(extra),
        [((CORE * PER_CORE, CYCLES, ANG), bf16)],
        [
            pltpu.VMEM((KD * HALF, LANES), f32),
            pltpu.VMEM((KD * CYCLES, HALF), bf16),
            pltpu.VMEM((KD * CYCLES, HALF), bf16),
            pltpu.VMEM((KD, CYCLES, ANG), bf16),
            pltpu.SemaphoreType.DMA((2,)),
        ],
        1000,
        1000,
        {3: 0} if extra else None,
        [HBM],
    )(which, hats, inverse, *extra)


def body(particles, group_ids, ctf_table, references):
    core, x_lo, z = (lax.axis_index(name) for name in ("core", "x_lo", ("z_hi", "z_lo")))
    forward = jnp.asarray(forward_table())
    place = jnp.stack([core, x_lo])

    messages = share(group_ids, particles, ctf_table, forward)
    own = lax.all_to_all(messages, ("x_lo", "x_hi", "y"), 0, 0, tiled=True)
    start = (core * PER_CORE + x_lo * (KD - 1)).reshape(1)
    rmat, power = classes(start, references, forward)
    row = lax.broadcasted_iota(jnp.int32, (SLOT, LANES), 0)
    edge = (z * CHUNK // HALF + 1) * HALF - z * CHUNK
    before = (row < edge).astype(f32)
    own, rmat, power, before = lax.optimization_barrier((own, rmat, power, before))
    other = swap("core", own)

    expo, stats, by_class, csq, ydata = scores(
        place, own, other, rmat, power, jnp.asarray(search_table().reshape(2 * ROT, ANG))
    )
    all_stats = lax.all_to_all(stats, ("core", "x_lo", "x_hi", "y"), 0, 0, tiled=True)
    post = posts(expo, jnp.asarray(post_table().reshape(2 * ANG, ROT)))
    sums = sums_of(all_stats, stats, by_class, csq, post, ydata)

    near = lax.all_to_all(sums, "z_lo", 0, 0, tiled=True)
    near = call(fold_kernel, [VMEM], [((ZH, SLOT, LANES), bf16)], [], 10**6, 10**6, limit=20)(near)
    got = jnp.sum(lax.all_to_all(near, "z_hi", 0, 0, tiled=True).astype(f32), axis=0)
    scales = got[CHUNK : CHUNK + 2]
    scales = scales[:, :CYCLES] + scales[:, CYCLES:] + PRIOR_WEIGHT
    scales = jnp.concatenate([scales, scales], axis=1)
    hat = (got / jnp.where(before > 0.5, scales[:1], scales[1:])).astype(bf16)

    inverse = jnp.asarray(inverse_table())
    near = lax.all_gather(hat, ("z_hi", "z_lo"))
    far = swap("x_lo", near)
    near_other = swap("core", near)
    result = images(jnp.stack([core, x_lo]), near, inverse, None)
    far, result = lax.optimization_barrier((far, result))
    far_other = swap("core", far)
    result = images(jnp.stack([core, 1 - x_lo]), far, inverse, result)
    result = images(jnp.stack([1 - core, x_lo]), near_other, inverse, result)
    return images(jnp.stack([1 - core, 1 - x_lo]), far_other, inverse, result)


def solution(mesh):
    fine = Mesh(mesh.devices.reshape(X, ZH, ZL, CORE, 2, 4), DOM + CLS)
    in_specs = (P(DOM + CLS, None, None), P(DOM + CLS), P(), P(CLS, None, None))
    return jax.shard_map(body, mesh=fine, in_specs=in_specs, out_specs=P(CLS, None, None), check_vma=False)
```

```python
import math

import jax
import jax.numpy as jnp
import ml_dtypes
import numpy as np
from jax import lax
from jax.experimental import pallas as pl
from jax.experimental.pallas import tpu as pltpu
from jax.sharding import Mesh
from jax.sharding import PartitionSpec as P

CYCLES = 64
ANG = 288
ROT = 72
HALF = ANG // 2
LANES = 2 * CYCLES
PRIOR_WEIGHT = 1.0
SCORE_SCALE = 4.0 / math.sqrt(CYCLES * ANG)

X, Z, CORE, SIDE = 2, 16, 2, 8
ZH, ZL = 4, 4
MINE = 2
PER_CORE = 25
KD = 13
KPAD = 16
KROWS = KPAD // 2
PARTS = 2
SOURCES = X * SIDE
COUNT = MINE * CORE * SOURCES
MSG = MINE * HALF + 16
CHUNK = KD * HALF // ZL
SPAN = -(-CHUNK // HALF) + 1
SLOT = 480

DOM = ("x_lo", "z_hi", "z_lo", "core")
CLS = ("x_hi", "y")

NT = (((1,), (1,)), ((), ()))
NN = (((1,), (0,)), ((), ()))
f32 = jnp.float32
bf16 = jnp.bfloat16


def angles(rows, cols, factor):
    index = np.arange(rows)[:, None] * factor * np.arange(cols)[None, :] % ANG
    return 2.0 * math.pi * index / ANG


def split(table):
    table = table.astype(np.float32)
    high = table.astype(ml_dtypes.bfloat16)
    low = (table - high.astype(np.float32)).astype(ml_dtypes.bfloat16)
    return np.stack([high, low])


def forward_table():
    angle = angles(HALF + 1, ANG, 1)
    real = np.cos(angle[:HALF])
    imag = np.concatenate([np.cos(angle[HALF:]), np.sin(angle[1:HALF])])
    return split(np.concatenate([real, imag]))


def weights_of_rows():
    return np.where(np.arange(HALF) == 0, 1.0, 2.0)[:, None] / ANG


def search_table():
    angle = angles(HALF, ROT, ANG // ROT)
    scale = weights_of_rows()
    return split(np.concatenate([np.cos(angle) * scale, -np.sin(angle) * scale]).T)


def post_table():
    angle = angles(HALF, ROT, ANG // ROT)
    return split(np.concatenate([np.cos(angle), np.sin(angle)]))


def inverse_table():
    angle = angles(HALF + 1, ANG, 1)
    scale = weights_of_rows()
    real = np.cos(angle[:HALF]) * scale
    imag = np.concatenate([np.cos(angle[HALF:]), np.sin(angle[1:HALF])]) * scale
    return np.concatenate([split(real), split(imag)])


def dot(a, b, dims=NN):
    return lax.dot_general(a, b, dims, preferred_element_type=f32)


def halves(values):
    high = values.astype(bf16)
    return high, (values - high.astype(f32)).astype(bf16)


def dot3(table, values):
    high, low = halves(values)
    rows = table.shape[0] // 2
    both = dot(table[...], high)
    return both[:rows] + (both[rows:] + dot(table[:rows], low))


def turn(values):
    return pltpu.roll(values, CYCLES, 1)


def left(shape):
    return lax.broadcasted_iota(jnp.int32, shape, len(shape) - 1) < CYCLES


def fold(spec):
    real, imag = spec[:HALF], spec[HALF:]
    side = left(real.shape)
    return jnp.where(side, real, turn(imag)), jnp.where(side, turn(real), imag)


def share_kernel(ids, x, ctf, table, outs, out, sem):
    images = x[...].reshape(MINE * CYCLES, ANG)
    factor = jnp.concatenate([ctf[pl.ds(ids[0], 1), :], ctf[pl.ds(ids[1], 1), :]], axis=1)
    spec = (dot(table[0], images, NT) + dot(table[1], images, NT)) * factor
    first, second = fold(spec)
    out[0:HALF] = first.astype(bf16)
    out[HALF : 2 * HALF] = second.astype(bf16)
    high, rest = halves(factor)
    rest = factor - high.astype(f32)
    mid = rest.astype(bf16)
    low = rest - mid.astype(f32)
    row = lax.broadcasted_iota(jnp.int32, (16, LANES), 0)
    tags = jnp.where(row == 0, high.astype(f32), jnp.where(row == 1, mid.astype(f32), jnp.where(row == 2, low, 0.0)))
    out[2 * HALF : MSG] = tags.astype(bf16)
    copies = [pltpu.make_async_copy(out, outs.at[s], sem.at[s]) for s in range(SOURCES)]
    for copy in copies:
        copy.start()
    for copy in copies:
        copy.wait()


def class_kernel(start, refs, table, out, power, images, rows, sem):
    copy = pltpu.make_async_copy(refs.at[pl.ds(start[0], KD)], images.at[pl.ds(0, KD)], sem)
    copy.start()
    images[KD:] = jnp.zeros((KPAD - KD, CYCLES, ANG), bf16)
    ones = jnp.ones((8, ANG), bf16)
    copy.wait()
    for step in range(KPAD // 4):
        block = images[4 * step : 4 * step + 4].reshape(4 * CYCLES, ANG)
        spec = dot(table[0], block, NT) + dot(table[1], block, NT)
        wide = block.astype(f32)
        high, low = halves(wide * wide)
        energy = dot(ones, high, NT) + dot(ones, low, NT)
        for pair in range(2):
            k = 4 * step + 2 * pair
            lanes = slice(pair * LANES, (pair + 1) * LANES)
            first, second = fold(spec[:, lanes])
            rows[k * HALF : (k + 1) * HALF] = first.astype(bf16).astype(f32)
            rows[(k + 1) * HALF : (k + 2) * HALF] = second.astype(bf16).astype(f32)
            part = energy[:, lanes]
            side = left(part.shape)
            power[k : k + 1] = jnp.where(side, part, 0.0)[0:1]
            power[k + 1 : k + 2] = jnp.where(side, turn(part), 0.0)[0:1]

    def step(j, carry):
        plain = rows[pl.ds(j, KPAD, stride=HALF), :]
        other = turn(plain)
        other = jnp.where(left(other.shape), other, -other)
        out[j] = jnp.concatenate([plain, other], axis=0).astype(bf16)
        return carry

    lax.fori_loop(0, HALF, step, 0, unroll=36)


def score_kernel(place, own, other, rmat, power, table, expo, stats, by_class, csq, far, wide, pairs, ydata, sem):
    core, x_lo = place[0], place[1]

    def widen(s, carry):
        mine = pl.multiple_of((core * SOURCES + s) * MSG, 8)
        theirs = pl.multiple_of(((1 - core) * SOURCES + s) * MSG, 8)
        wide[pl.ds(mine, MSG), :] = own[s].astype(f32)
        wide[pl.ds(theirs, MSG), :] = other[s].astype(f32)
        return carry

    lax.fori_loop(0, SOURCES, widen, 0)
    many = CORE * SOURCES
    factor = wide[pl.ds(2 * HALF, many, stride=MSG), :] + wide[pl.ds(2 * HALF + 1, many, stride=MSG), :]
    factor = factor + wide[pl.ds(2 * HALF + 2, many, stride=MSG), :]
    square = factor * factor
    side = left(square.shape)
    square = jnp.concatenate([jnp.where(side, square, 0.0), jnp.where(side, turn(square), 0.0)], axis=0)
    csq[...] = square
    energy = lax.dot_general(
        power[...],
        jnp.concatenate([square, square], axis=0),
        NT,
        precision=lax.Precision.HIGHEST,
        preferred_element_type=f32,
    )
    side = left((KROWS, LANES))
    energy = jnp.where(side, energy[:KROWS], energy[KROWS:])

    def step(j, carry):
        rows = jnp.concatenate([wide[pl.ds(j, many, stride=MSG), :], wide[pl.ds(HALF + j, many, stride=MSG), :]], axis=0)
        rows = rows.astype(bf16)
        ydata[j] = rows
        both = dot(rmat[j], rows, NT)
        straight = jnp.concatenate([both[:KROWS], both[KROWS : 2 * KROWS]], axis=1)
        crossed = jnp.concatenate([both[2 * KROWS : 3 * KROWS], both[3 * KROWS :]], axis=1)
        pairs[pl.ds(j, KROWS, stride=ANG), :] = straight
        pairs[pl.ds(HALF + j, KROWS, stride=ANG), :] = crossed
        return carry

    lax.fori_loop(0, HALF, step, 0, unroll=48)
    keep = pltpu.make_async_copy(ydata, far, sem)
    keep.start()
    top = jnp.full((1, LANES), -3.0e38, f32)
    lane_side = left((ROT, LANES))
    for kk in range(KROWS):
        cross = dot3(table, pairs[kk * ANG : (kk + 1) * ANG])
        score = SCORE_SCALE * (cross - 0.5 * energy[kk : kk + 1])
        if kk + KROWS >= KD:
            score = jnp.where(lane_side, score, -3.0e38)
        if kk == 0:
            score = jnp.where(jnp.logical_and(lane_side, x_lo == 1), -3.0e38, score)
        expo[:, kk * LANES : (kk + 1) * LANES] = score
        top = jnp.maximum(top, jnp.max(score, axis=0, keepdims=True))
    top = jnp.maximum(top, turn(top))
    total = jnp.zeros((1, LANES), f32)
    for kk in range(KROWS):
        value = jnp.exp(expo[:, kk * LANES : (kk + 1) * LANES] - top)
        expo[:, kk * LANES : (kk + 1) * LANES] = value
        part = jnp.sum(value, axis=0, keepdims=True)
        by_class[kk : kk + 1] = part
        total = total + part
    total = total + turn(total)
    pair = jnp.where(lax.broadcasted_iota(jnp.int32, (8, LANES), 0) == 0, top, total)
    for s in range(CORE * SOURCES):
        stats[s] = pair
    keep.wait()


def post_kernel(expo, table, far, rows, out, sem):
    for kk in range(KROWS):
        rows[kk * ANG : (kk + 1) * ANG] = dot3(table, expo[:, kk * LANES : (kk + 1) * LANES])

    def step(j, carry):
        real = rows[pl.ds(j, KROWS, stride=ANG), :]
        imag = rows[pl.ds(HALF + j, KROWS, stride=ANG), :]
        out[j] = jnp.concatenate([real, imag], axis=0)
        return carry

    lax.fori_loop(0, HALF, step, 0, unroll=36)
    keep = pltpu.make_async_copy(out, far, sem)
    keep.start()
    keep.wait()


def sum_kernel(all_stats, stats, by_class, csq, far_post, far_ydata, out, rows, slots, post, ydata, sem):
    copies = []
    for part in range(PARTS):
        lines = pl.ds(part * HALF // PARTS, HALF // PARTS)
        copies.append(pltpu.make_async_copy(far_post.at[lines], post.at[lines], sem.at[0, part]))
        copies.append(pltpu.make_async_copy(far_ydata.at[lines], ydata.at[lines], sem.at[1, part]))
    for copy in copies:
        copy.start()
    tops, totals = all_stats[:, 0, :], all_stats[:, 1, :]
    top = jnp.max(tops, axis=0, keepdims=True)
    total = jnp.sum(totals * jnp.exp(tops - top), axis=0, keepdims=True)
    share = jnp.exp(stats[0, 0:1] - top) / total

    def step(j, carry):
        wide = post[j] * share
        real, imag = wide[:KROWS], wide[KROWS:]
        weights = jnp.concatenate([real, turn(real), imag, turn(imag)], axis=0)[:, :CYCLES]
        both = dot(weights.astype(bf16), ydata[j])
        other = turn(both[KPAD:])
        other = jnp.where(left(other.shape), other, -other)
        rows[pl.ds(j, KPAD, stride=HALF), :] = both[:KPAD] + other
        return carry

    for part in range(PARTS):
        copies[2 * part].wait()
        copies[2 * part + 1].wait()
        lax.fori_loop(part * HALF // PARTS, (part + 1) * HALF // PARTS, step, 0, unroll=HALF // PARTS)
    mass = by_class[...] * share
    mass = jnp.concatenate([mass, turn(mass)], axis=0)[:, :CYCLES]
    weight = lax.dot_general(mass, csq[...], NN, precision=lax.Precision.HIGHEST, preferred_element_type=f32)
    high, low = halves(weight)
    scales = jnp.where(left(weight.shape), high.astype(f32), turn(low.astype(f32)))
    for part in range(ZL):
        first = part * CHUNK // HALF
        base = part * SLOT
        slots[base + CHUNK : base + SLOT] = jnp.zeros((SLOT - CHUNK, LANES), f32)
        slots[base : base + CHUNK] = rows[part * CHUNK : (part + 1) * CHUNK]
        slots[base + CHUNK : base + CHUNK + SPAN] = scales[first : first + SPAN]
        out[part] = slots[base : base + SLOT].astype(bf16)


LAST = CHUNK // 8 * 8


def fold_kernel(pieces, out):
    total = pieces[0].astype(f32)
    for s in range(1, ZL):
        total = total + pieces[s].astype(f32)
    rows = total[LAST:]
    scales = rows + turn(rows)
    high = scales.astype(bf16).astype(f32)
    scales = jnp.where(left(scales.shape), high, scales - high)
    row = lax.broadcasted_iota(jnp.int32, rows.shape, 0)
    rows = jnp.where(row < CHUNK - LAST, rows, scales)
    out[...] = jnp.concatenate([total[:LAST], rows], axis=0).astype(bf16)


def hat_kernel(part, pieces, out):
    total = pieces[0].astype(f32)
    for s in range(1, ZH):
        total = total + pieces[s].astype(f32)
    scales = total[CHUNK : CHUNK + SPAN]
    scales = 1.0 / (scales + turn(scales) + PRIOR_WEIGHT)
    row = lax.broadcasted_iota(jnp.int32, total.shape, 0) + part[0] * (CHUNK % HALF)
    factor = jnp.broadcast_to(scales[SPAN - 1 :], total.shape)
    for i in range(SPAN - 2, -1, -1):
        factor = jnp.where(row < (i + 1) * HALF, scales[i : i + 1], factor)
    out[...] = (total * factor).astype(bf16)


def image_kernel(place, hats, table, *rest):
    out, flat, real, imag, stage, sem = rest[-6:]
    core, x_lo = place[0], place[1]
    for part in range(ZL):
        flat[part * CHUNK : (part + 1) * CHUNK] = hats[part].astype(f32)[:CHUNK]
    for k in range(KD):
        rows = flat[k * HALF : (k + 1) * HALF].T.astype(bf16)
        real[k * CYCLES : (k + 1) * CYCLES] = rows[:CYCLES]
        imag[k * CYCLES : (k + 1) * CYCLES] = rows[CYCLES:]
    image = dot(real[...], table[0]) + dot(imag[...], table[2])
    image = image + (dot(real[...], table[1]) + dot(imag[...], table[3]))
    stage[...] = image.astype(bf16).reshape(KD, CYCLES, ANG)
    base = core * PER_CORE + x_lo * (KD - 1)
    copy = pltpu.make_async_copy(stage.at[pl.ds(x_lo, KD - 1)], out.at[pl.ds(base + x_lo, KD - 1)], sem.at[0])
    copy.start()

    @pl.when(x_lo == 0)
    def _():
        last = pltpu.make_async_copy(stage.at[pl.ds(KD - 1, 1)], out.at[pl.ds(base + KD - 1, 1)], sem.at[1])
        last.start()
        last.wait()

    copy.wait()


VMEM = pl.BlockSpec(memory_space=pltpu.VMEM)
SMEM = pl.BlockSpec(memory_space=pltpu.SMEM)
HBM = pl.BlockSpec(memory_space=pltpu.HBM)


def call(kernel, ins, outs, scratch, flops, nbytes, aliases=None, out_specs=None, limit=48):
    out_shape = [jax.ShapeDtypeStruct(shape, dtype) for shape, dtype in outs]
    single = len(out_shape) == 1
    specs = out_specs or [VMEM] * len(out_shape)
    return pl.pallas_call(
        kernel,
        out_shape=out_shape[0] if single else out_shape,
        in_specs=ins,
        out_specs=specs[0] if single else specs,
        scratch_shapes=scratch,
        input_output_aliases=aliases or {},
        compiler_params=pltpu.CompilerParams(vmem_limit_bytes=limit * 2**20),
        cost_estimate=pl.CostEstimate(flops=flops, bytes_accessed=nbytes, transcendentals=0),
    )


def swap(axis, value):
    return lax.ppermute(value, axis, [(0, 1), (1, 0)])


def share(group_ids, particles, ctf_table, forward):
    return call(
        share_kernel,
        [SMEM, VMEM, VMEM, VMEM],
        [((SOURCES, MSG, LANES), bf16)],
        [pltpu.VMEM((MSG, LANES), bf16), pltpu.SemaphoreType.DMA((SOURCES,))],
        10**7,
        10**6,
        out_specs=[HBM],
        limit=64,
    )(group_ids, particles, ctf_table, forward)


def classes(start, references, forward):
    return call(
        class_kernel,
        [SMEM, HBM, VMEM],
        [((HALF, 2 * KPAD, LANES), bf16), ((KPAD, LANES), f32)],
        [
            pltpu.VMEM((KPAD, CYCLES, ANG), bf16),
            pltpu.VMEM((KPAD * HALF, LANES), f32),
            pltpu.SemaphoreType.DMA,
        ],
        10**9,
        4 * 10**6,
        limit=64,
    )(start, references, forward)


def scores(place, own, other, rmat, power, table):
    return call(
        score_kernel,
        [SMEM] + [VMEM] * 5,
        [
            ((ROT, KROWS * LANES), f32),
            ((CORE * SOURCES, 8, LANES), f32),
            ((KROWS, LANES), f32),
            ((COUNT, LANES), f32),
            ((HALF, COUNT, LANES), bf16),
        ],
        [
            pltpu.VMEM((CORE * SOURCES * MSG, LANES), f32),
            pltpu.VMEM((KROWS * ANG, LANES), f32),
            pltpu.VMEM((HALF, COUNT, LANES), bf16),
            pltpu.SemaphoreType.DMA,
        ],
        10**9,
        8 * 10**6,
        limit=64,
        out_specs=[VMEM] * 4 + [HBM],
    )(place, own, other, rmat, power, table)


def posts(expo, table):
    return call(
        post_kernel,
        [VMEM, VMEM],
        [((HALF, KPAD, LANES), f32)],
        [
            pltpu.VMEM((KROWS * ANG, LANES), f32),
            pltpu.VMEM((HALF, KPAD, LANES), f32),
            pltpu.SemaphoreType.DMA,
        ],
        10**9,
        3 * 10**6,
        limit=64,
        out_specs=[HBM],
    )(expo, table)


def sums_of(all_stats, stats, by_class, csq, post, ydata):
    return call(
        sum_kernel,
        [VMEM] * 4 + [HBM] * 2,
        [((ZL, SLOT, LANES), bf16)],
        [
            pltpu.VMEM((KPAD * HALF, LANES), f32),
            pltpu.VMEM((ZL * SLOT, LANES), f32),
            pltpu.VMEM((HALF, KPAD, LANES), f32),
            pltpu.VMEM((HALF, COUNT, LANES), bf16),
            pltpu.SemaphoreType.DMA((2, PARTS)),
        ],
        10**9,
        8 * 10**6,
        limit=64,
    )(all_stats, stats, by_class, csq, post, ydata)


def images(which, hats, inverse, result):
    extra = [] if result is None else [result]
    return call(
        image_kernel,
        [SMEM, VMEM, VMEM] + [HBM] * len(extra),
        [((CORE * PER_CORE, CYCLES, ANG), bf16)],
        [
            pltpu.VMEM((KD * HALF, LANES), f32),
            pltpu.VMEM((KD * CYCLES, HALF), bf16),
            pltpu.VMEM((KD * CYCLES, HALF), bf16),
            pltpu.VMEM((KD, CYCLES, ANG), bf16),
            pltpu.SemaphoreType.DMA((2,)),
        ],
        1000,
        1000,
        {3: 0} if extra else None,
        [HBM],
    )(which, hats, inverse, *extra)


def body(particles, group_ids, ctf_table, references):
    core, x_lo = lax.axis_index("core"), lax.axis_index("x_lo")
    forward = jnp.asarray(forward_table())
    place = jnp.stack([core, x_lo])

    messages = share(group_ids, particles, ctf_table, forward)
    own = lax.all_to_all(messages, ("x_lo", "x_hi", "y"), 0, 0, tiled=True)
    start = (core * PER_CORE + x_lo * (KD - 1)).reshape(1)
    rmat, power = classes(start, references, forward)
    part = lax.axis_index("z_lo").reshape(1)
    own, rmat, power, part = lax.optimization_barrier((own, rmat, power, part))
    other = swap("core", own)

    expo, stats, by_class, csq, ydata = scores(
        place, own, other, rmat, power, jnp.asarray(search_table().reshape(2 * ROT, ANG))
    )
    all_stats = lax.all_to_all(stats, ("core", "x_lo", "x_hi", "y"), 0, 0, tiled=True)
    post = posts(expo, jnp.asarray(post_table().reshape(2 * ANG, ROT)))
    sums = sums_of(all_stats, stats, by_class, csq, post, ydata)

    near = lax.all_to_all(sums, "z_lo", 0, 0, tiled=True)
    near = call(fold_kernel, [VMEM], [((SLOT, LANES), bf16)], [], 10**6, 10**6, limit=20)(near)
    near = lax.all_gather(near, "z_hi")
    hat = call(hat_kernel, [SMEM, VMEM], [((SLOT, LANES), bf16)], [], 10**6, 10**6, limit=20)(part, near)

    inverse = jnp.asarray(inverse_table())
    near = lax.all_gather(hat, "z_lo")
    far = swap("x_lo", near)
    near_other = swap("core", near)
    result = images(jnp.stack([core, x_lo]), near, inverse, None)
    far, result = lax.optimization_barrier((far, result))
    far_other = swap("core", far)
    result = images(jnp.stack([core, 1 - x_lo]), far, inverse, result)
    result = images(jnp.stack([1 - core, x_lo]), near_other, inverse, result)
    return images(jnp.stack([1 - core, 1 - x_lo]), far_other, inverse, result)


def solution(mesh):
    fine = Mesh(mesh.devices.reshape(X, ZH, ZL, CORE, 2, 4), DOM + CLS)
    in_specs = (P(DOM + CLS, None, None), P(DOM + CLS), P(), P(CLS, None, None))
    return jax.shard_map(body, mesh=fine, in_specs=in_specs, out_specs=P(CLS, None, None), check_vma=False)
```

```python
import math

import jax
import jax.numpy as jnp
import ml_dtypes
import numpy as np
from jax import lax
from jax.experimental import pallas as pl
from jax.experimental.pallas import tpu as pltpu
from jax.sharding import Mesh
from jax.sharding import PartitionSpec as P

CYCLES = 64
ANG = 288
ROT = 72
HALF = ANG // 2
LANES = 2 * CYCLES
PRIOR_WEIGHT = 1.0
SCORE_SCALE = 4.0 / math.sqrt(CYCLES * ANG)

X, Z, CORE, SIDE = 2, 16, 2, 8
ZH, ZL = 4, 4
MINE = 2
PER_CORE = 25
KD = 13
KPAD = 16
KROWS = KPAD // 2
PARTS = 2
GROUPS = ((0, 5), (5, 9), (9, 13))
SOURCES = X * SIDE
COUNT = MINE * CORE * SOURCES
MSG = MINE * HALF + 16
CHUNK = KD * HALF // ZL
SPAN = -(-CHUNK // HALF) + 1
SLOT = 480

DOM = ("x_lo", "z_hi", "z_lo", "core")
CLS = ("x_hi", "y")

NT = (((1,), (1,)), ((), ()))
NN = (((1,), (0,)), ((), ()))
f32 = jnp.float32
bf16 = jnp.bfloat16


def angles(rows, cols, factor):
    index = np.arange(rows)[:, None] * factor * np.arange(cols)[None, :] % ANG
    return 2.0 * math.pi * index / ANG


def split(table):
    table = table.astype(np.float32)
    high = table.astype(ml_dtypes.bfloat16)
    low = (table - high.astype(np.float32)).astype(ml_dtypes.bfloat16)
    return np.stack([high, low])


def forward_table():
    angle = angles(HALF + 1, ANG, 1)
    real = np.cos(angle[:HALF])
    imag = np.concatenate([np.cos(angle[HALF:]), np.sin(angle[1:HALF])])
    return split(np.concatenate([real, imag]))


def weights_of_rows():
    return np.where(np.arange(HALF) == 0, 1.0, 2.0)[:, None] / ANG


def search_table():
    angle = angles(HALF, ROT, ANG // ROT)
    scale = weights_of_rows()
    return split(np.concatenate([np.cos(angle) * scale, -np.sin(angle) * scale]).T)


def post_table():
    angle = angles(HALF, ROT, ANG // ROT)
    return split(np.concatenate([np.cos(angle), np.sin(angle)]))


def inverse_table():
    angle = angles(HALF + 1, ANG, 1)
    scale = weights_of_rows()
    real = np.cos(angle[:HALF]) * scale
    imag = np.concatenate([np.cos(angle[HALF:]), np.sin(angle[1:HALF])]) * scale
    return np.concatenate([split(real), split(imag)])


def dot(a, b, dims=NN):
    return lax.dot_general(a, b, dims, preferred_element_type=f32)


def halves(values):
    high = values.astype(bf16)
    return high, (values - high.astype(f32)).astype(bf16)


def dot3(table, values):
    high, low = halves(values)
    rows = table.shape[0] // 2
    both = dot(table[...], high)
    return both[:rows] + (both[rows:] + dot(table[:rows], low))


def turn(values):
    return pltpu.roll(values, CYCLES, 1)


def left(shape):
    return lax.broadcasted_iota(jnp.int32, shape, len(shape) - 1) < CYCLES


def fold(spec):
    real, imag = spec[:HALF], spec[HALF:]
    side = left(real.shape)
    return jnp.where(side, real, turn(imag)), jnp.where(side, turn(real), imag)


def share_kernel(ids, x, ctf, table, outs, out, sem):
    images = x[...].reshape(MINE * CYCLES, ANG)
    factor = jnp.concatenate([ctf[pl.ds(ids[0], 1), :], ctf[pl.ds(ids[1], 1), :]], axis=1)
    spec = (dot(table[0], images, NT) + dot(table[1], images, NT)) * factor
    first, second = fold(spec)
    out[0:HALF] = first.astype(bf16)
    out[HALF : 2 * HALF] = second.astype(bf16)
    high, rest = halves(factor)
    rest = factor - high.astype(f32)
    mid = rest.astype(bf16)
    low = rest - mid.astype(f32)
    row = lax.broadcasted_iota(jnp.int32, (16, LANES), 0)
    tags = jnp.where(row == 0, high.astype(f32), jnp.where(row == 1, mid.astype(f32), jnp.where(row == 2, low, 0.0)))
    out[2 * HALF : MSG] = tags.astype(bf16)
    copies = [pltpu.make_async_copy(out, outs.at[s], sem.at[s]) for s in range(SOURCES)]
    for copy in copies:
        copy.start()
    for copy in copies:
        copy.wait()


def class_kernel(start, refs, table, out, power, images, rows, sem):
    copy = pltpu.make_async_copy(refs.at[pl.ds(start[0], KD)], images.at[pl.ds(0, KD)], sem)
    copy.start()
    images[KD:] = jnp.zeros((KPAD - KD, CYCLES, ANG), bf16)
    ones = jnp.ones((8, ANG), bf16)
    copy.wait()
    for step in range(KPAD // 4):
        block = images[4 * step : 4 * step + 4].reshape(4 * CYCLES, ANG)
        spec = dot(table[0], block, NT) + dot(table[1], block, NT)
        wide = block.astype(f32)
        high, low = halves(wide * wide)
        energy = dot(ones, high, NT) + dot(ones, low, NT)
        for pair in range(2):
            k = 4 * step + 2 * pair
            lanes = slice(pair * LANES, (pair + 1) * LANES)
            first, second = fold(spec[:, lanes])
            rows[k * HALF : (k + 1) * HALF] = first.astype(bf16).astype(f32)
            rows[(k + 1) * HALF : (k + 2) * HALF] = second.astype(bf16).astype(f32)
            part = energy[:, lanes]
            side = left(part.shape)
            power[k : k + 1] = jnp.where(side, part, 0.0)[0:1]
            power[k + 1 : k + 2] = jnp.where(side, turn(part), 0.0)[0:1]

    def step(j, carry):
        plain = rows[pl.ds(j, KPAD, stride=HALF), :]
        other = turn(plain)
        other = jnp.where(left(other.shape), other, -other)
        out[j] = jnp.concatenate([plain, other], axis=0).astype(bf16)
        return carry

    lax.fori_loop(0, HALF, step, 0, unroll=36)


def score_kernel(place, own, other, rmat, power, table, expo, stats, by_class, csq, far, wide, pairs, ydata, sem):
    core, x_lo = place[0], place[1]

    def widen(s, carry):
        mine = pl.multiple_of((core * SOURCES + s) * MSG, 8)
        theirs = pl.multiple_of(((1 - core) * SOURCES + s) * MSG, 8)
        wide[pl.ds(mine, MSG), :] = own[s].astype(f32)
        wide[pl.ds(theirs, MSG), :] = other[s].astype(f32)
        return carry

    lax.fori_loop(0, SOURCES, widen, 0)
    many = CORE * SOURCES
    factor = wide[pl.ds(2 * HALF, many, stride=MSG), :] + wide[pl.ds(2 * HALF + 1, many, stride=MSG), :]
    factor = factor + wide[pl.ds(2 * HALF + 2, many, stride=MSG), :]
    square = factor * factor
    side = left(square.shape)
    square = jnp.concatenate([jnp.where(side, square, 0.0), jnp.where(side, turn(square), 0.0)], axis=0)
    csq[...] = square
    energy = lax.dot_general(
        power[...],
        jnp.concatenate([square, square], axis=0),
        NT,
        precision=lax.Precision.HIGHEST,
        preferred_element_type=f32,
    )
    side = left((KROWS, LANES))
    energy = jnp.where(side, energy[:KROWS], energy[KROWS:])

    def step(j, carry):
        rows = jnp.concatenate([wide[pl.ds(j, many, stride=MSG), :], wide[pl.ds(HALF + j, many, stride=MSG), :]], axis=0)
        rows = rows.astype(bf16)
        ydata[j] = rows
        both = dot(rmat[j], rows, NT)
        straight = jnp.concatenate([both[:KROWS], both[KROWS : 2 * KROWS]], axis=1)
        crossed = jnp.concatenate([both[2 * KROWS : 3 * KROWS], both[3 * KROWS :]], axis=1)
        pairs[pl.ds(j, KROWS, stride=ANG), :] = straight
        pairs[pl.ds(HALF + j, KROWS, stride=ANG), :] = crossed
        return carry

    lax.fori_loop(0, HALF, step, 0, unroll=48)
    keep = pltpu.make_async_copy(ydata, far, sem)
    keep.start()
    top = jnp.full((1, LANES), -3.0e38, f32)
    lane_side = left((ROT, LANES))
    for kk in range(KROWS):
        cross = dot3(table, pairs[kk * ANG : (kk + 1) * ANG])
        score = SCORE_SCALE * (cross - 0.5 * energy[kk : kk + 1])
        if kk + KROWS >= KD:
            score = jnp.where(lane_side, score, -3.0e38)
        if kk == 0:
            score = jnp.where(jnp.logical_and(lane_side, x_lo == 1), -3.0e38, score)
        expo[:, kk * LANES : (kk + 1) * LANES] = score
        top = jnp.maximum(top, jnp.max(score, axis=0, keepdims=True))
    top = jnp.maximum(top, turn(top))
    total = jnp.zeros((1, LANES), f32)
    for kk in range(KROWS):
        value = jnp.exp(expo[:, kk * LANES : (kk + 1) * LANES] - top)
        expo[:, kk * LANES : (kk + 1) * LANES] = value
        part = jnp.sum(value, axis=0, keepdims=True)
        by_class[kk : kk + 1] = part
        total = total + part
    total = total + turn(total)
    pair = jnp.where(lax.broadcasted_iota(jnp.int32, (8, LANES), 0) == 0, top, total)
    for s in range(CORE * SOURCES):
        stats[s] = pair
    keep.wait()


def post_kernel(expo, table, far, rows, out, sem):
    for kk in range(KROWS):
        rows[kk * ANG : (kk + 1) * ANG] = dot3(table, expo[:, kk * LANES : (kk + 1) * LANES])

    def step(j, carry):
        real = rows[pl.ds(j, KROWS, stride=ANG), :]
        imag = rows[pl.ds(HALF + j, KROWS, stride=ANG), :]
        out[j] = jnp.concatenate([real, imag], axis=0)
        return carry

    lax.fori_loop(0, HALF, step, 0, unroll=36)
    keep = pltpu.make_async_copy(out, far, sem)
    keep.start()
    keep.wait()


def sum_kernel(*refs):
    far_small, (far_post, far_ydata, out, rows, slots, post, ydata) = refs[:4], refs[4:11]
    small, (sem, small_sem) = refs[11:15], refs[15:]
    all_stats, stats, by_class, csq = small
    first_copies = [pltpu.make_async_copy(a, b, small_sem.at[i]) for i, (a, b) in enumerate(zip(far_small, small))]
    for copy in first_copies:
        copy.start()
    copies = []
    for part in range(PARTS):
        lines = pl.ds(part * HALF // PARTS, HALF // PARTS)
        copies.append(pltpu.make_async_copy(far_post.at[lines], post.at[lines], sem.at[0, part]))
        copies.append(pltpu.make_async_copy(far_ydata.at[lines], ydata.at[lines], sem.at[1, part]))
    for copy in copies:
        copy.start()
    for copy in first_copies:
        copy.wait()
    tops, totals = all_stats[:, 0, :], all_stats[:, 1, :]
    top = jnp.max(tops, axis=0, keepdims=True)
    total = jnp.sum(totals * jnp.exp(tops - top), axis=0, keepdims=True)
    share = jnp.exp(stats[0, 0:1] - top) / total

    def step(j, carry):
        wide = post[j] * share
        real, imag = wide[:KROWS], wide[KROWS:]
        weights = jnp.concatenate([real, turn(real), imag, turn(imag)], axis=0)[:, :CYCLES]
        both = dot(weights.astype(bf16), ydata[j])
        other = turn(both[KPAD:])
        other = jnp.where(left(other.shape), other, -other)
        rows[pl.ds(j, KPAD, stride=HALF), :] = both[:KPAD] + other
        return carry

    for part in range(PARTS):
        copies[2 * part].wait()
        copies[2 * part + 1].wait()
        lax.fori_loop(part * HALF // PARTS, (part + 1) * HALF // PARTS, step, 0, unroll=HALF // PARTS)
    mass = by_class[...] * share
    mass = jnp.concatenate([mass, turn(mass)], axis=0)[:, :CYCLES]
    weight = lax.dot_general(mass, csq[...], NN, precision=lax.Precision.HIGHEST, preferred_element_type=f32)
    high, low = halves(weight)
    scales = jnp.where(left(weight.shape), high.astype(f32), turn(low.astype(f32)))
    for part in range(ZL):
        first = part * CHUNK // HALF
        base = part * SLOT
        slots[base + CHUNK : base + SLOT] = jnp.zeros((SLOT - CHUNK, LANES), f32)
        slots[base : base + CHUNK] = rows[part * CHUNK : (part + 1) * CHUNK]
        slots[base + CHUNK : base + CHUNK + SPAN] = scales[first : first + SPAN]
        out[part] = slots[base : base + SLOT].astype(bf16)


LAST = CHUNK // 8 * 8


def fold_kernel(pieces, out):
    total = pieces[0].astype(f32)
    for s in range(1, ZL):
        total = total + pieces[s].astype(f32)
    rows = total[LAST:]
    scales = rows + turn(rows)
    high = scales.astype(bf16).astype(f32)
    scales = jnp.where(left(scales.shape), high, scales - high)
    row = lax.broadcasted_iota(jnp.int32, rows.shape, 0)
    rows = jnp.where(row < CHUNK - LAST, rows, scales)
    out[...] = jnp.concatenate([total[:LAST], rows], axis=0).astype(bf16)


def hat_kernel(part, pieces, out):
    total = pieces[0].astype(f32)
    for s in range(1, ZH):
        total = total + pieces[s].astype(f32)
    scales = total[CHUNK : CHUNK + SPAN]
    scales = 1.0 / (scales + turn(scales) + PRIOR_WEIGHT)
    row = lax.broadcasted_iota(jnp.int32, total.shape, 0) + part[0] * (CHUNK % HALF)
    factor = jnp.broadcast_to(scales[SPAN - 1 :], total.shape)
    for i in range(SPAN - 2, -1, -1):
        factor = jnp.where(row < (i + 1) * HALF, scales[i : i + 1], factor)
    out[...] = (total * factor).astype(bf16)


def image_kernel(place, table, hats, *refs):
    out, flat, real, imag, stage, sem = refs[-6:]
    x_lo = place[0]
    copies = []
    for core in range(CORE):
        i = core
        base = core * PER_CORE + x_lo * (KD - 1)
        for part in range(ZL):
            flat[i, part * CHUNK : (part + 1) * CHUNK] = hats[i, part].astype(f32)[:CHUNK]
        for step, (first, last) in enumerate(GROUPS):
            for k in range(first, last):
                rows = flat[i, k * HALF : (k + 1) * HALF].T.astype(bf16)
                real[i, k * CYCLES : (k + 1) * CYCLES] = rows[:CYCLES]
                imag[i, k * CYCLES : (k + 1) * CYCLES] = rows[CYCLES:]
            lines = slice(first * CYCLES, last * CYCLES)
            image = dot(real[i, lines], table[0]) + dot(imag[i, lines], table[2])
            image = image + (dot(real[i, lines], table[1]) + dot(imag[i, lines], table[3]))
            stage[i, first:last] = image.astype(bf16).reshape(last - first, CYCLES, ANG)
            begin = max(first, 1)
            here, there = pl.ds(begin, last - begin), pl.ds(base + begin, last - begin)
            copy = pltpu.make_async_copy(stage.at[i, here], out.at[there], sem.at[i, step])
            copy.start()
            copies.append(copy)

        @pl.when(x_lo == 0)
        def _():
            shared = pltpu.make_async_copy(stage.at[i, pl.ds(0, 1)], out.at[pl.ds(base, 1)], sem.at[i, len(GROUPS)])
            shared.start()
            shared.wait()

    for copy in copies:
        copy.wait()


VMEM = pl.BlockSpec(memory_space=pltpu.VMEM)
SMEM = pl.BlockSpec(memory_space=pltpu.SMEM)
HBM = pl.BlockSpec(memory_space=pltpu.HBM)


def call(kernel, ins, outs, scratch, flops, nbytes, aliases=None, out_specs=None, limit=48):
    out_shape = [jax.ShapeDtypeStruct(shape, dtype) for shape, dtype in outs]
    single = len(out_shape) == 1
    specs = out_specs or [VMEM] * len(out_shape)
    return pl.pallas_call(
        kernel,
        out_shape=out_shape[0] if single else out_shape,
        in_specs=ins,
        out_specs=specs[0] if single else specs,
        scratch_shapes=scratch,
        input_output_aliases=aliases or {},
        compiler_params=pltpu.CompilerParams(vmem_limit_bytes=limit * 2**20),
        cost_estimate=pl.CostEstimate(flops=flops, bytes_accessed=nbytes, transcendentals=0),
    )


def swap(axis, value):
    return lax.ppermute(value, axis, [(0, 1), (1, 0)])


def share(group_ids, particles, ctf_table, forward):
    return call(
        share_kernel,
        [SMEM, VMEM, VMEM, VMEM],
        [((SOURCES, MSG, LANES), bf16)],
        [pltpu.VMEM((MSG, LANES), bf16), pltpu.SemaphoreType.DMA((SOURCES,))],
        10**7,
        10**6,
        out_specs=[HBM],
        limit=64,
    )(group_ids, particles, ctf_table, forward)


def classes(start, references, forward):
    return call(
        class_kernel,
        [SMEM, HBM, VMEM],
        [((HALF, 2 * KPAD, LANES), bf16), ((KPAD, LANES), f32)],
        [
            pltpu.VMEM((KPAD, CYCLES, ANG), bf16),
            pltpu.VMEM((KPAD * HALF, LANES), f32),
            pltpu.SemaphoreType.DMA,
        ],
        10**9,
        4 * 10**6,
        limit=64,
    )(start, references, forward)


def scores(place, own, other, rmat, power, table):
    return call(
        score_kernel,
        [SMEM] + [VMEM] * 5,
        [
            ((ROT, KROWS * LANES), f32),
            ((CORE * SOURCES, 8, LANES), f32),
            ((KROWS, LANES), f32),
            ((COUNT, LANES), f32),
            ((HALF, COUNT, LANES), bf16),
        ],
        [
            pltpu.VMEM((CORE * SOURCES * MSG, LANES), f32),
            pltpu.VMEM((KROWS * ANG, LANES), f32),
            pltpu.VMEM((HALF, COUNT, LANES), bf16),
            pltpu.SemaphoreType.DMA,
        ],
        10**9,
        8 * 10**6,
        limit=64,
        out_specs=[VMEM] * 4 + [HBM],
    )(place, own, other, rmat, power, table)


def posts(expo, table):
    return call(
        post_kernel,
        [VMEM, VMEM],
        [((HALF, KPAD, LANES), f32)],
        [
            pltpu.VMEM((KROWS * ANG, LANES), f32),
            pltpu.VMEM((HALF, KPAD, LANES), f32),
            pltpu.SemaphoreType.DMA,
        ],
        10**9,
        3 * 10**6,
        limit=64,
        out_specs=[HBM],
    )(expo, table)


def sums_of(all_stats, stats, by_class, csq, post, ydata):
    return call(
        sum_kernel,
        [HBM] * 6,
        [((ZL, SLOT, LANES), bf16)],
        [
            pltpu.VMEM((KPAD * HALF, LANES), f32),
            pltpu.VMEM((ZL * SLOT, LANES), f32),
            pltpu.VMEM((HALF, KPAD, LANES), f32),
            pltpu.VMEM((HALF, COUNT, LANES), bf16),
            pltpu.VMEM((CORE * SOURCES, 8, LANES), f32),
            pltpu.VMEM((CORE * SOURCES, 8, LANES), f32),
            pltpu.VMEM((KROWS, LANES), f32),
            pltpu.VMEM((COUNT, LANES), f32),
            pltpu.SemaphoreType.DMA((2, PARTS)),
            pltpu.SemaphoreType.DMA((4,)),
        ],
        10**9,
        8 * 10**6,
        limit=64,
    )(all_stats, stats, by_class, csq, post, ydata)


def images(place, hats, inverse, result):
    extra = [] if result is None else [result]
    return call(
        image_kernel,
        [SMEM, VMEM, VMEM] + [HBM] * len(extra),
        [((CORE * PER_CORE, CYCLES, ANG), bf16)],
        [
            pltpu.VMEM((CORE, KD * HALF, LANES), f32),
            pltpu.VMEM((CORE, KD * CYCLES, HALF), bf16),
            pltpu.VMEM((CORE, KD * CYCLES, HALF), bf16),
            pltpu.VMEM((CORE, KD, CYCLES, ANG), bf16),
            pltpu.SemaphoreType.DMA((CORE, len(GROUPS) + 1)),
        ],
        1000,
        1000,
        {3: 0} if extra else None,
        [HBM],
    )(place.reshape(1), inverse, hats, *extra)


def body(particles, group_ids, ctf_table, references):
    core, x_lo = lax.axis_index("core"), lax.axis_index("x_lo")
    forward = jnp.asarray(forward_table())
    place = jnp.stack([core, x_lo])

    messages = share(group_ids, particles, ctf_table, forward)
    own = lax.all_to_all(messages, ("x_lo", "x_hi", "y"), 0, 0, tiled=True)
    start = (core * PER_CORE + x_lo * (KD - 1)).reshape(1)
    rmat, power = classes(start, references, forward)
    part = lax.axis_index("z_lo").reshape(1)
    own, rmat, power, part = lax.optimization_barrier((own, rmat, power, part))
    other = swap("core", own)

    expo, stats, by_class, csq, ydata = scores(
        place, own, other, rmat, power, jnp.asarray(search_table().reshape(2 * ROT, ANG))
    )
    all_stats = lax.all_to_all(stats, ("core", "x_lo", "x_hi", "y"), 0, 0, tiled=True)
    post = posts(expo, jnp.asarray(post_table().reshape(2 * ANG, ROT)))
    sums = sums_of(all_stats, stats, by_class, csq, post, ydata)

    near = lax.all_to_all(sums, "z_lo", 0, 0, tiled=True)
    near = call(fold_kernel, [VMEM], [((SLOT, LANES), bf16)], [], 10**6, 10**6, limit=20)(near)
    near = lax.all_gather(near, "z_hi")
    hat = call(hat_kernel, [SMEM, VMEM], [((SLOT, LANES), bf16)], [], 10**6, 10**6, limit=20)(part, near)

    inverse = jnp.asarray(inverse_table())
    near = lax.all_gather(hat, "z_lo")
    far = swap("x_lo", near)
    result = images(x_lo, lax.all_gather(near, "core"), inverse, None)
    far, result = lax.optimization_barrier((far, result))
    return images(1 - x_lo, lax.all_gather(far, "core"), inverse, result)


def solution(mesh):
    fine = Mesh(mesh.devices.reshape(X, ZH, ZL, CORE, 2, 4), DOM + CLS)
    in_specs = (P(DOM + CLS, None, None), P(DOM + CLS), P(), P(CLS, None, None))
    return jax.shard_map(body, mesh=fine, in_specs=in_specs, out_specs=P(CLS, None, None), check_vma=False)
```

```python
import math

import jax
import jax.numpy as jnp
import ml_dtypes
import numpy as np
from jax import lax
from jax.experimental import pallas as pl
from jax.experimental.pallas import tpu as pltpu
from jax.sharding import Mesh
from jax.sharding import PartitionSpec as P

CYCLES = 64
ANG = 288
ROT = 72
HALF = ANG // 2
LANES = 2 * CYCLES
PRIOR_WEIGHT = 1.0
SCORE_SCALE = 4.0 / math.sqrt(CYCLES * ANG)

X, Z, CORE, SIDE = 2, 16, 2, 8
ZH, ZL = 4, 4
MINE = 2
PER_CORE = 25
KD = 13
KPAD = 16
KROWS = KPAD // 2
PARTS = 2
GROUPS = ((0, 5), (5, 9), (9, 13))
SOURCES = X * SIDE
COUNT = MINE * CORE * SOURCES
MSG = MINE * HALF + 16
CHUNK = KD * HALF // ZL
SPAN = -(-CHUNK // HALF) + 1
SLOT = 480

DOM = ("x_lo", "z_hi", "z_lo", "core")
CLS = ("x_hi", "y")

NT = (((1,), (1,)), ((), ()))
NN = (((1,), (0,)), ((), ()))
f32 = jnp.float32
bf16 = jnp.bfloat16


def angles(rows, cols, factor):
    index = np.arange(rows)[:, None] * factor * np.arange(cols)[None, :] % ANG
    return 2.0 * math.pi * index / ANG


def split(table, count):
    rest, pieces = table.astype(np.float32), []
    for _ in range(count):
        pieces.append(rest.astype(ml_dtypes.bfloat16))
        rest = rest - pieces[-1].astype(np.float32)
    return np.stack(pieces)


def forward_table():
    angle = angles(HALF + 1, ANG, 1)
    real = np.cos(angle[:HALF])
    imag = np.concatenate([np.cos(angle[HALF:]), np.sin(angle[1:HALF])])
    return split(np.concatenate([real, imag]), 3)


def weights_of_rows():
    return np.where(np.arange(HALF) == 0, 1.0, 2.0)[:, None] / ANG


def search_table():
    angle = angles(HALF, ROT, ANG // ROT)
    scale = weights_of_rows()
    return split(np.concatenate([np.cos(angle) * scale, -np.sin(angle) * scale]).T, 3)


def post_table():
    angle = angles(HALF, ROT, ANG // ROT)
    return split(np.concatenate([np.cos(angle), np.sin(angle)]), 3)


def inverse_table():
    angle = angles(HALF + 1, ANG, 1)
    scale = weights_of_rows()
    real = np.cos(angle[:HALF]) * scale
    imag = np.concatenate([np.cos(angle[HALF:]), np.sin(angle[1:HALF])]) * scale
    return np.concatenate([split(real, 2), split(imag, 2)])


def dot(a, b, dims=NN):
    return lax.dot_general(a, b, dims, preferred_element_type=f32)


def halves(values):
    high = values.astype(bf16)
    return high, (values - high.astype(f32)).astype(bf16)


def thirds(values):
    high = values.astype(bf16)
    rest = values - high.astype(f32)
    mid = rest.astype(bf16)
    return high, mid, (rest - mid.astype(f32)).astype(bf16)


def dot3(table, values):
    high, mid, low = thirds(values)
    rows = table.shape[0] // 3
    first = dot(table[...], high)
    second = dot(table[: 2 * rows], mid)
    small = (first[2 * rows :] + second[rows:]) + dot(table[:rows], low)
    return first[:rows] + (first[rows : 2 * rows] + second[:rows] + small)


def transform(table, images):
    return dot(table[0], images, NT) + (dot(table[1], images, NT) + dot(table[2], images, NT))


def turn(values):
    return pltpu.roll(values, CYCLES, 1)


def left(shape):
    return lax.broadcasted_iota(jnp.int32, shape, len(shape) - 1) < CYCLES


def fold(spec):
    real, imag = spec[:HALF], spec[HALF:]
    side = left(real.shape)
    return jnp.where(side, real, turn(imag)), jnp.where(side, turn(real), imag)


def share_kernel(ids, x, ctf, table, outs, out, sem):
    images = x[...].reshape(MINE * CYCLES, ANG)
    factor = jnp.concatenate([ctf[pl.ds(ids[0], 1), :], ctf[pl.ds(ids[1], 1), :]], axis=1)
    spec = transform(table, images) * factor
    first, second = fold(spec)
    out[0:HALF] = first.astype(bf16)
    out[HALF : 2 * HALF] = second.astype(bf16)
    high, mid, low = thirds(factor)
    row = lax.broadcasted_iota(jnp.int32, (16, LANES), 0)
    tags = jnp.where(row == 0, high.astype(f32), jnp.where(row == 1, mid.astype(f32), jnp.where(row == 2, low.astype(f32), 0.0)))
    out[2 * HALF : MSG] = tags.astype(bf16)
    copies = [pltpu.make_async_copy(out, outs.at[s], sem.at[s]) for s in range(SOURCES)]
    for copy in copies:
        copy.start()
    for copy in copies:
        copy.wait()


def class_kernel(start, refs, table, out, power, images, rows, sem):
    copy = pltpu.make_async_copy(refs.at[pl.ds(start[0], KD)], images.at[pl.ds(0, KD)], sem)
    copy.start()
    images[KD:] = jnp.zeros((KPAD - KD, CYCLES, ANG), bf16)
    ones = jnp.ones((8, ANG), bf16)
    copy.wait()
    for step in range(KPAD // 4):
        block = images[4 * step : 4 * step + 4].reshape(4 * CYCLES, ANG)
        spec = transform(table, block)
        wide = block.astype(f32)
        high, low = halves(wide * wide)
        energy = dot(ones, high, NT) + dot(ones, low, NT)
        for pair in range(2):
            k = 4 * step + 2 * pair
            lanes = slice(pair * LANES, (pair + 1) * LANES)
            first, second = fold(spec[:, lanes])
            rows[k * HALF : (k + 1) * HALF] = first.astype(bf16).astype(f32)
            rows[(k + 1) * HALF : (k + 2) * HALF] = second.astype(bf16).astype(f32)
            part = energy[:, lanes]
            side = left(part.shape)
            power[k : k + 1] = jnp.where(side, part, 0.0)[0:1]
            power[k + 1 : k + 2] = jnp.where(side, turn(part), 0.0)[0:1]

    def step(j, carry):
        plain = rows[pl.ds(j, KPAD, stride=HALF), :]
        out[j] = plain.astype(bf16)
        return carry

    lax.fori_loop(0, HALF, step, 0, unroll=36)


def score_kernel(place, own, other, rmat, power, table, expo, stats, by_class, csq, far, wide, pairs, ydata, sem):
    core, x_lo = place[0], place[1]

    def widen(s, carry):
        mine = pl.multiple_of((core * SOURCES + s) * MSG, 8)
        theirs = pl.multiple_of(((1 - core) * SOURCES + s) * MSG, 8)
        wide[pl.ds(mine, MSG), :] = own[s].astype(f32)
        wide[pl.ds(theirs, MSG), :] = other[s].astype(f32)
        return carry

    lax.fori_loop(0, SOURCES, widen, 0, unroll=2)
    many = CORE * SOURCES
    factor = wide[pl.ds(2 * HALF, many, stride=MSG), :] + wide[pl.ds(2 * HALF + 1, many, stride=MSG), :]
    factor = factor + wide[pl.ds(2 * HALF + 2, many, stride=MSG), :]
    square = factor * factor
    side = left(square.shape)
    square = jnp.concatenate([jnp.where(side, square, 0.0), jnp.where(side, turn(square), 0.0)], axis=0)
    csq[...] = square
    energy = lax.dot_general(
        power[...],
        jnp.concatenate([square, square], axis=0),
        NT,
        precision=lax.Precision.HIGHEST,
        preferred_element_type=f32,
    )
    side = left((KROWS, LANES))
    energy = jnp.where(side, energy[:KROWS], energy[KROWS:])

    def step(j, carry):
        rows = jnp.concatenate([wide[pl.ds(j, many, stride=MSG), :], wide[pl.ds(HALF + j, many, stride=MSG), :]], axis=0)
        rows = rows.astype(bf16)
        ydata[j] = rows
        plain = rmat[j].astype(f32)
        cross = turn(plain)
        cross = jnp.where(left(cross.shape), cross, -cross)
        both = dot(jnp.concatenate([plain, cross], axis=0).astype(bf16), rows, NT)
        straight = jnp.concatenate([both[:KROWS], both[KROWS : 2 * KROWS]], axis=1)
        crossed = jnp.concatenate([both[2 * KROWS : 3 * KROWS], both[3 * KROWS :]], axis=1)
        pairs[pl.ds(j, KROWS, stride=ANG), :] = straight
        pairs[pl.ds(HALF + j, KROWS, stride=ANG), :] = crossed
        return carry

    lax.fori_loop(0, HALF, step, 0, unroll=48)
    keep = pltpu.make_async_copy(ydata, far, sem)
    keep.start()
    top = jnp.full((1, LANES), -3.0e38, f32)
    lane_side = left((ROT, LANES))
    crosses = []
    for kk in range(0, KROWS, 2):
        two = [pairs[k * ANG : (k + 1) * ANG] for k in (kk, kk + 1)]
        wide_cross = dot3(table, jnp.concatenate(two, axis=1))
        crosses += [wide_cross[:, :LANES], wide_cross[:, LANES:]]
    for kk in range(KROWS):
        cross = crosses[kk]
        score = SCORE_SCALE * (cross - 0.5 * energy[kk : kk + 1])
        if kk + KROWS >= KD:
            score = jnp.where(lane_side, score, -3.0e38)
        if kk == 0:
            score = jnp.where(jnp.logical_and(lane_side, x_lo == 1), -3.0e38, score)
        expo[:, kk * LANES : (kk + 1) * LANES] = score
        top = jnp.maximum(top, jnp.max(score, axis=0, keepdims=True))
    top = jnp.maximum(top, turn(top))
    total = jnp.zeros((1, LANES), f32)
    for kk in range(KROWS):
        value = jnp.exp(expo[:, kk * LANES : (kk + 1) * LANES] - top)
        expo[:, kk * LANES : (kk + 1) * LANES] = value
        part = jnp.sum(value, axis=0, keepdims=True)
        by_class[kk : kk + 1] = part
        total = total + part
    total = total + turn(total)
    pair = jnp.where(lax.broadcasted_iota(jnp.int32, (8, LANES), 0) == 0, top, total)
    for s in range(CORE * SOURCES):
        stats[s] = pair
    keep.wait()


def post_kernel(expo, table, far, rows, out, sem):
    for kk in range(0, KROWS, 2):
        both = dot3(table, expo[:, kk * LANES : (kk + 2) * LANES])
        rows[kk * ANG : (kk + 1) * ANG] = both[:, :LANES]
        rows[(kk + 1) * ANG : (kk + 2) * ANG] = both[:, LANES:]

    def step(j, carry):
        real = rows[pl.ds(j, KROWS, stride=ANG), :]
        imag = rows[pl.ds(HALF + j, KROWS, stride=ANG), :]
        out[j] = jnp.concatenate([real, imag], axis=0)
        return carry

    lax.fori_loop(0, HALF, step, 0, unroll=36)
    keep = pltpu.make_async_copy(out, far, sem)
    keep.start()
    keep.wait()


def sum_kernel(*refs):
    far_small, (far_post, far_ydata, out, rows, slots, post, ydata) = refs[:4], refs[4:11]
    small, (sem, small_sem) = refs[11:15], refs[15:]
    all_stats, stats, by_class, csq = small
    first_copies = [pltpu.make_async_copy(a, b, small_sem.at[i]) for i, (a, b) in enumerate(zip(far_small, small))]
    for copy in first_copies:
        copy.start()
    copies = []
    for part in range(PARTS):
        lines = pl.ds(part * HALF // PARTS, HALF // PARTS)
        copies.append(pltpu.make_async_copy(far_post.at[lines], post.at[lines], sem.at[0, part]))
        copies.append(pltpu.make_async_copy(far_ydata.at[lines], ydata.at[lines], sem.at[1, part]))
    for copy in copies:
        copy.start()
    for copy in first_copies:
        copy.wait()
    tops, totals = all_stats[:, 0, :], all_stats[:, 1, :]
    top = jnp.max(tops, axis=0, keepdims=True)
    total = jnp.sum(totals * jnp.exp(tops - top), axis=0, keepdims=True)
    share = jnp.exp(stats[0, 0:1] - top) / total

    def step(j, carry):
        wide = post[j] * share
        real, imag = wide[:KROWS], wide[KROWS:]
        weights = jnp.concatenate([real, turn(real), imag, turn(imag)], axis=0)[:, :CYCLES]
        both = dot(weights.astype(bf16), ydata[j])
        other = turn(both[KPAD:])
        other = jnp.where(left(other.shape), other, -other)
        rows[pl.ds(j, KPAD, stride=HALF), :] = both[:KPAD] + other
        return carry

    for part in range(PARTS):
        copies[2 * part].wait()
        copies[2 * part + 1].wait()
        lax.fori_loop(part * HALF // PARTS, (part + 1) * HALF // PARTS, step, 0, unroll=HALF // PARTS)
    mass = by_class[...] * share
    mass = jnp.concatenate([mass, turn(mass)], axis=0)[:, :CYCLES]
    weight = lax.dot_general(mass, csq[...], NN, precision=lax.Precision.HIGHEST, preferred_element_type=f32)
    high, low = halves(weight)
    scales = jnp.where(left(weight.shape), high.astype(f32), turn(low.astype(f32)))
    for part in range(ZL):
        first = part * CHUNK // HALF
        base = part * SLOT
        slots[base + CHUNK : base + SLOT] = jnp.zeros((SLOT - CHUNK, LANES), f32)
        slots[base : base + CHUNK] = rows[part * CHUNK : (part + 1) * CHUNK]
        slots[base + CHUNK : base + CHUNK + SPAN] = scales[first : first + SPAN]
        out[part] = slots[base : base + SLOT].astype(bf16)


LAST = CHUNK // 8 * 8


def fold_kernel(pieces, out):
    total = pieces[0].astype(f32)
    for s in range(1, ZL):
        total = total + pieces[s].astype(f32)
    rows = total[LAST:]
    scales = rows + turn(rows)
    high = scales.astype(bf16).astype(f32)
    scales = jnp.where(left(scales.shape), high, scales - high)
    row = lax.broadcasted_iota(jnp.int32, rows.shape, 0)
    rows = jnp.where(row < CHUNK - LAST, rows, scales)
    out[...] = jnp.concatenate([total[:LAST], rows], axis=0).astype(bf16)


def hat_kernel(part, pieces, out):
    total = pieces[0].astype(f32)
    for s in range(1, ZH):
        total = total + pieces[s].astype(f32)
    scales = total[CHUNK : CHUNK + SPAN]
    scales = 1.0 / (scales + turn(scales) + PRIOR_WEIGHT)
    row = lax.broadcasted_iota(jnp.int32, total.shape, 0) + part[0] * (CHUNK % HALF)
    factor = jnp.broadcast_to(scales[SPAN - 1 :], total.shape)
    for i in range(SPAN - 2, -1, -1):
        factor = jnp.where(row < (i + 1) * HALF, scales[i : i + 1], factor)
    out[...] = (total * factor).astype(bf16)


def image_kernel(place, table, hats, *refs):
    out, flat, real, imag, stage, sem = refs[-6:]
    x_lo = place[0]
    copies = []
    for core in range(CORE):
        i = core
        base = core * PER_CORE + x_lo * (KD - 1)
        for part in range(ZL):
            flat[i, part * CHUNK : (part + 1) * CHUNK] = hats[i, part].astype(f32)[:CHUNK]
        for step, (first, last) in enumerate(GROUPS):
            for k in range(first, last):
                rows = flat[i, k * HALF : (k + 1) * HALF].T.astype(bf16)
                real[i, k * CYCLES : (k + 1) * CYCLES] = rows[:CYCLES]
                imag[i, k * CYCLES : (k + 1) * CYCLES] = rows[CYCLES:]
            lines = slice(first * CYCLES, last * CYCLES)
            image = dot(real[i, lines], table[0]) + dot(imag[i, lines], table[2])
            image = image + (dot(real[i, lines], table[1]) + dot(imag[i, lines], table[3]))
            stage[i, first:last] = image.astype(bf16).reshape(last - first, CYCLES, ANG)
            begin = max(first, 1)
            here, there = pl.ds(begin, last - begin), pl.ds(base + begin, last - begin)
            copy = pltpu.make_async_copy(stage.at[i, here], out.at[there], sem.at[i, step])
            copy.start()
            copies.append(copy)

        @pl.when(x_lo == 0)
        def _():
            shared = pltpu.make_async_copy(stage.at[i, pl.ds(0, 1)], out.at[pl.ds(base, 1)], sem.at[i, len(GROUPS)])
            shared.start()
            shared.wait()

    for copy in copies:
        copy.wait()


VMEM = pl.BlockSpec(memory_space=pltpu.VMEM)
SMEM = pl.BlockSpec(memory_space=pltpu.SMEM)
HBM = pl.BlockSpec(memory_space=pltpu.HBM)


def call(kernel, ins, outs, scratch, flops, nbytes, aliases=None, out_specs=None, limit=48):
    out_shape = [jax.ShapeDtypeStruct(shape, dtype) for shape, dtype in outs]
    single = len(out_shape) == 1
    specs = out_specs or [VMEM] * len(out_shape)
    return pl.pallas_call(
        kernel,
        out_shape=out_shape[0] if single else out_shape,
        in_specs=ins,
        out_specs=specs[0] if single else specs,
        scratch_shapes=scratch,
        input_output_aliases=aliases or {},
        compiler_params=pltpu.CompilerParams(vmem_limit_bytes=limit * 2**20),
        cost_estimate=pl.CostEstimate(flops=flops, bytes_accessed=nbytes, transcendentals=0),
    )


def swap(axis, value):
    return lax.ppermute(value, axis, [(0, 1), (1, 0)])


def share(group_ids, particles, ctf_table, forward):
    return call(
        share_kernel,
        [SMEM, VMEM, VMEM, VMEM],
        [((SOURCES, MSG, LANES), bf16)],
        [pltpu.VMEM((MSG, LANES), bf16), pltpu.SemaphoreType.DMA((SOURCES,))],
        10**7,
        10**6,
        out_specs=[HBM],
        limit=64,
    )(group_ids, particles, ctf_table, forward)


def classes(start, references, forward):
    return call(
        class_kernel,
        [SMEM, HBM, VMEM],
        [((HALF, KPAD, LANES), bf16), ((KPAD, LANES), f32)],
        [
            pltpu.VMEM((KPAD, CYCLES, ANG), bf16),
            pltpu.VMEM(((KPAD + 1) * HALF, LANES), f32),
            pltpu.SemaphoreType.DMA,
        ],
        10**9,
        4 * 10**6,
        limit=64,
    )(start, references, forward)


def scores(place, own, other, rmat, power, table):
    return call(
        score_kernel,
        [SMEM] + [VMEM] * 5,
        [
            ((ROT, KROWS * LANES), f32),
            ((CORE * SOURCES, 8, LANES), f32),
            ((KROWS, LANES), f32),
            ((COUNT, LANES), f32),
            ((HALF, COUNT, LANES), bf16),
        ],
        [
            pltpu.VMEM(((CORE * SOURCES + 1) * MSG, LANES), f32),
            pltpu.VMEM(((KROWS + 1) * ANG, LANES), f32),
            pltpu.VMEM((HALF, COUNT, LANES), bf16),
            pltpu.SemaphoreType.DMA,
        ],
        10**9,
        8 * 10**6,
        limit=64,
        out_specs=[VMEM] * 4 + [HBM],
    )(place, own, other, rmat, power, table)


def posts(expo, table):
    return call(
        post_kernel,
        [VMEM, VMEM],
        [((HALF, KPAD, LANES), f32)],
        [
            pltpu.VMEM(((KROWS + 1) * ANG, LANES), f32),
            pltpu.VMEM((HALF, KPAD, LANES), f32),
            pltpu.SemaphoreType.DMA,
        ],
        10**9,
        3 * 10**6,
        limit=64,
        out_specs=[HBM],
    )(expo, table)


def sums_of(all_stats, stats, by_class, csq, post, ydata):
    return call(
        sum_kernel,
        [HBM] * 6,
        [((ZL, SLOT, LANES), bf16)],
        [
            pltpu.VMEM(((KPAD + 1) * HALF, LANES), f32),
            pltpu.VMEM((ZL * SLOT, LANES), f32),
            pltpu.VMEM((HALF, KPAD, LANES), f32),
            pltpu.VMEM((HALF, COUNT, LANES), bf16),
            pltpu.VMEM((CORE * SOURCES, 8, LANES), f32),
            pltpu.VMEM((CORE * SOURCES, 8, LANES), f32),
            pltpu.VMEM((KROWS, LANES), f32),
            pltpu.VMEM((COUNT, LANES), f32),
            pltpu.SemaphoreType.DMA((2, PARTS)),
            pltpu.SemaphoreType.DMA((4,)),
        ],
        10**9,
        8 * 10**6,
        limit=64,
    )(all_stats, stats, by_class, csq, post, ydata)


def images(place, hats, inverse, result):
    extra = [] if result is None else [result]
    return call(
        image_kernel,
        [SMEM, VMEM, VMEM] + [HBM] * len(extra),
        [((CORE * PER_CORE, CYCLES, ANG), bf16)],
        [
            pltpu.VMEM((CORE, KD * HALF, LANES), f32),
            pltpu.VMEM((CORE, KD * CYCLES, HALF), bf16),
            pltpu.VMEM((CORE, KD * CYCLES, HALF), bf16),
            pltpu.VMEM((CORE, KD, CYCLES, ANG), bf16),
            pltpu.SemaphoreType.DMA((CORE, len(GROUPS) + 1)),
        ],
        1000,
        1000,
        {3: 0} if extra else None,
        [HBM],
    )(place.reshape(1), inverse, hats, *extra)


def body(particles, group_ids, ctf_table, references):
    core, x_lo = lax.axis_index("core"), lax.axis_index("x_lo")
    forward = jnp.asarray(forward_table())
    place = jnp.stack([core, x_lo])

    messages = share(group_ids, particles, ctf_table, forward)
    own = lax.all_to_all(messages, ("x_lo", "x_hi", "y"), 0, 0, tiled=True)
    start = (core * PER_CORE + x_lo * (KD - 1)).reshape(1)
    rmat, power = classes(start, references, forward)
    part = lax.axis_index("z_lo").reshape(1)
    own, rmat, power, part = lax.optimization_barrier((own, rmat, power, part))
    other = swap("core", own)

    expo, stats, by_class, csq, ydata = scores(
        place, own, other, rmat, power, jnp.asarray(search_table().reshape(3 * ROT, ANG))
    )
    all_stats = lax.all_to_all(stats, ("core", "x_lo", "x_hi", "y"), 0, 0, tiled=True)
    post = posts(expo, jnp.asarray(post_table().reshape(3 * ANG, ROT)))
    sums = sums_of(all_stats, stats, by_class, csq, post, ydata)

    near = lax.all_to_all(sums, "z_lo", 0, 0, tiled=True)
    near = call(fold_kernel, [VMEM], [((SLOT, LANES), bf16)], [], 10**6, 10**6, limit=20)(near)
    near = lax.all_gather(near, "z_hi")
    hat = call(hat_kernel, [SMEM, VMEM], [((SLOT, LANES), bf16)], [], 10**6, 10**6, limit=20)(part, near)

    inverse = jnp.asarray(inverse_table())
    near = lax.all_gather(hat, "z_lo")
    far = swap("x_lo", near)
    result = images(x_lo, lax.all_gather(near, "core"), inverse, None)
    far, result = lax.optimization_barrier((far, result))
    return images(1 - x_lo, lax.all_gather(far, "core"), inverse, result)


def solution(mesh):
    fine = Mesh(mesh.devices.reshape(X, ZH, ZL, CORE, 2, 4), DOM + CLS)
    in_specs = (P(DOM + CLS, None, None), P(DOM + CLS), P(), P(CLS, None, None))
    return jax.shard_map(body, mesh=fine, in_specs=in_specs, out_specs=P(CLS, None, None), check_vma=False)
```

```python
import math

import jax
import jax.numpy as jnp
import ml_dtypes
import numpy as np
from jax import lax
from jax.experimental import pallas as pl
from jax.experimental.pallas import tpu as pltpu
from jax.sharding import Mesh
from jax.sharding import PartitionSpec as P

CYCLES = 64
ANG = 288
ROT = 72
HALF = ANG // 2
LANES = 2 * CYCLES
PRIOR_WEIGHT = 1.0
SCORE_SCALE = 4.0 / math.sqrt(CYCLES * ANG)

X, Z, CORE, SIDE = 2, 16, 2, 8
ZH, ZL = 4, 4
MINE = 2
PER_CORE = 25
KD = 13
KPAD = 16
KROWS = KPAD // 2
PARTS = 2
GROUPS = ((0, 5), (5, 9), (9, 13))
SOURCES = X * SIDE
COUNT = MINE * CORE * SOURCES
MSG = MINE * HALF + 16
CHUNK = KD * HALF // ZL
SPAN = -(-CHUNK // HALF) + 1
SLOT = 480

DOM = ("x_lo", "z_hi", "z_lo", "core")
CLS = ("x_hi", "y")

NT = (((1,), (1,)), ((), ()))
NN = (((1,), (0,)), ((), ()))
f32 = jnp.float32
bf16 = jnp.bfloat16


def angles(rows, cols, factor):
    index = np.arange(rows)[:, None] * factor * np.arange(cols)[None, :] % ANG
    return 2.0 * math.pi * index / ANG


def split(table, count):
    rest, pieces = table.astype(np.float32), []
    for _ in range(count):
        pieces.append(rest.astype(ml_dtypes.bfloat16))
        rest = rest - pieces[-1].astype(np.float32)
    return np.stack(pieces)


def forward_table():
    angle = angles(HALF + 1, ANG, 1)
    real = np.cos(angle[:HALF])
    imag = np.concatenate([np.cos(angle[HALF:]), np.sin(angle[1:HALF])])
    return split(np.concatenate([real, imag]), 3)


def weights_of_rows():
    return np.where(np.arange(HALF) == 0, 1.0, 2.0)[:, None] / ANG


def search_table():
    angle = angles(HALF, ROT, ANG // ROT)
    scale = weights_of_rows()
    return split(np.concatenate([np.cos(angle) * scale, -np.sin(angle) * scale]).T, 3)


def post_table():
    angle = angles(HALF, ROT, ANG // ROT)
    return split(np.concatenate([np.cos(angle), np.sin(angle)]), 3)


def inverse_table():
    angle = angles(HALF + 1, ANG, 1)
    scale = weights_of_rows()
    real = np.cos(angle[:HALF]) * scale
    imag = np.concatenate([np.cos(angle[HALF:]), np.sin(angle[1:HALF])]) * scale
    return np.concatenate([split(real, 2), split(imag, 2)])


def dot(a, b, dims=NN):
    return lax.dot_general(a, b, dims, preferred_element_type=f32)


def halves(values):
    high = values.astype(bf16)
    return high, (values - high.astype(f32)).astype(bf16)


def thirds(values):
    high = values.astype(bf16)
    rest = values - high.astype(f32)
    mid = rest.astype(bf16)
    return high, mid, (rest - mid.astype(f32)).astype(bf16)


def dot3(table, values):
    high, mid, low = thirds(values)
    rows = table.shape[0] // 3
    first = dot(table[...], high)
    second = dot(table[: 2 * rows], mid)
    small = (first[2 * rows :] + second[rows:]) + dot(table[:rows], low)
    return first[:rows] + (first[rows : 2 * rows] + second[:rows] + small)


def transform(table, images):
    return dot(table[0], images, NT) + (dot(table[1], images, NT) + dot(table[2], images, NT))


def turn(values):
    return pltpu.roll(values, CYCLES, 1)


def left(shape):
    return lax.broadcasted_iota(jnp.int32, shape, len(shape) - 1) < CYCLES


def fold(spec):
    real, imag = spec[:HALF], spec[HALF:]
    side = left(real.shape)
    return jnp.where(side, real, turn(imag)), jnp.where(side, turn(real), imag)


def share_kernel(ids, x, ctf, table, outs, out, sem):
    images = x[...].reshape(MINE * CYCLES, ANG)
    factor = jnp.concatenate([ctf[pl.ds(ids[0], 1), :], ctf[pl.ds(ids[1], 1), :]], axis=1)
    spec = transform(table, images) * factor
    first, second = fold(spec)
    out[0:HALF] = first.astype(bf16)
    out[HALF : 2 * HALF] = second.astype(bf16)
    high, mid, low = thirds(factor)
    row = lax.broadcasted_iota(jnp.int32, (16, LANES), 0)
    tags = jnp.where(row == 0, high.astype(f32), jnp.where(row == 1, mid.astype(f32), jnp.where(row == 2, low.astype(f32), 0.0)))
    out[2 * HALF : MSG] = tags.astype(bf16)
    copies = [pltpu.make_async_copy(out, outs.at[s], sem.at[s]) for s in range(SOURCES)]
    for copy in copies:
        copy.start()
    for copy in copies:
        copy.wait()


def class_kernel(start, refs, table, out, power, images, rows, sem):
    copy = pltpu.make_async_copy(refs.at[pl.ds(start[0], KD)], images.at[pl.ds(0, KD)], sem)
    copy.start()
    images[KD:] = jnp.zeros((KPAD - KD, CYCLES, ANG), bf16)
    ones = jnp.ones((8, ANG), bf16)
    copy.wait()
    for step in range(KPAD // 4):
        block = images[4 * step : 4 * step + 4].reshape(4 * CYCLES, ANG)
        spec = transform(table, block)
        wide = block.astype(f32)
        high, low = halves(wide * wide)
        energy = dot(ones, high, NT) + dot(ones, low, NT)
        for pair in range(2):
            k = 4 * step + 2 * pair
            lanes = slice(pair * LANES, (pair + 1) * LANES)
            first, second = fold(spec[:, lanes])
            rows[k * HALF : (k + 1) * HALF] = first.astype(bf16).astype(f32)
            rows[(k + 1) * HALF : (k + 2) * HALF] = second.astype(bf16).astype(f32)
            part = energy[:, lanes]
            side = left(part.shape)
            power[k : k + 1] = jnp.where(side, part, 0.0)[0:1]
            power[k + 1 : k + 2] = jnp.where(side, turn(part), 0.0)[0:1]

    def step(j, carry):
        plain = rows[pl.ds(j, KPAD, stride=HALF), :]
        out[j] = plain.astype(bf16)
        return carry

    lax.fori_loop(0, HALF, step, 0, unroll=36)


def score_kernel(place, own, other, rmat, power, table, expo, stats, by_class, csq, far, wide, pairs, ydata, sem):
    core, x_lo = place[0], place[1]

    def widen(s, carry):
        mine = pl.multiple_of((core * SOURCES + s) * MSG, 8)
        theirs = pl.multiple_of(((1 - core) * SOURCES + s) * MSG, 8)
        wide[pl.ds(mine, MSG), :] = own[s].astype(f32)
        wide[pl.ds(theirs, MSG), :] = other[s].astype(f32)
        return carry

    lax.fori_loop(0, SOURCES, widen, 0, unroll=2)
    many = CORE * SOURCES
    factor = wide[pl.ds(2 * HALF, many, stride=MSG), :] + wide[pl.ds(2 * HALF + 1, many, stride=MSG), :]
    factor = factor + wide[pl.ds(2 * HALF + 2, many, stride=MSG), :]
    square = factor * factor
    side = left(square.shape)
    square = jnp.concatenate([jnp.where(side, square, 0.0), jnp.where(side, turn(square), 0.0)], axis=0)
    csq[...] = square
    energy = lax.dot_general(
        power[...],
        jnp.concatenate([square, square], axis=0),
        NT,
        precision=lax.Precision.HIGHEST,
        preferred_element_type=f32,
    )
    side = left((KROWS, LANES))
    energy = jnp.where(side, energy[:KROWS], energy[KROWS:])

    def step(j, carry):
        rows = jnp.concatenate([wide[pl.ds(j, many, stride=MSG), :], wide[pl.ds(HALF + j, many, stride=MSG), :]], axis=0)
        rows = rows.astype(bf16)
        ydata[j] = rows
        plain = rmat[j].astype(f32)
        cross = turn(plain)
        cross = jnp.where(left(cross.shape), cross, -cross)
        both = dot(jnp.concatenate([plain, cross], axis=0).astype(bf16), rows, NT)
        straight = jnp.concatenate([both[:KROWS], both[KROWS : 2 * KROWS]], axis=1)
        crossed = jnp.concatenate([both[2 * KROWS : 3 * KROWS], both[3 * KROWS :]], axis=1)
        pairs[pl.ds(j, KROWS, stride=ANG), :] = straight
        pairs[pl.ds(HALF + j, KROWS, stride=ANG), :] = crossed
        return carry

    lax.fori_loop(0, HALF, step, 0, unroll=48)
    keep = pltpu.make_async_copy(ydata, far, sem)
    keep.start()
    top = jnp.full((1, LANES), -3.0e38, f32)
    lane_side = left((ROT, LANES))
    crosses = []
    for kk in range(0, KROWS, 2):
        two = [pairs[k * ANG : (k + 1) * ANG] for k in (kk, kk + 1)]
        wide_cross = dot3(table, jnp.concatenate(two, axis=1))
        crosses += [wide_cross[:, :LANES], wide_cross[:, LANES:]]
    for kk in range(KROWS):
        cross = crosses[kk]
        score = SCORE_SCALE * (cross - 0.5 * energy[kk : kk + 1])
        if kk + KROWS >= KD:
            score = jnp.where(lane_side, score, -3.0e38)
        if kk == 0:
            score = jnp.where(jnp.logical_and(lane_side, x_lo == 1), -3.0e38, score)
        expo[:, kk * LANES : (kk + 1) * LANES] = score
        top = jnp.maximum(top, jnp.max(score, axis=0, keepdims=True))
    top = jnp.maximum(top, turn(top))
    total = jnp.zeros((1, LANES), f32)
    for kk in range(KROWS):
        value = jnp.exp(expo[:, kk * LANES : (kk + 1) * LANES] - top)
        expo[:, kk * LANES : (kk + 1) * LANES] = value
        part = jnp.sum(value, axis=0, keepdims=True)
        by_class[kk : kk + 1] = part
        total = total + part
    total = total + turn(total)
    pair = jnp.where(lax.broadcasted_iota(jnp.int32, (8, LANES), 0) == 0, top, total)
    for s in range(CORE * SOURCES):
        stats[s] = pair
    keep.wait()


def post_kernel(expo, table, far, rows, out, sem):
    for kk in range(0, KROWS, 2):
        both = dot3(table, expo[:, kk * LANES : (kk + 2) * LANES])
        rows[kk * ANG : (kk + 1) * ANG] = both[:, :LANES]
        rows[(kk + 1) * ANG : (kk + 2) * ANG] = both[:, LANES:]

    def step(j, carry):
        real = rows[pl.ds(j, KROWS, stride=ANG), :]
        imag = rows[pl.ds(HALF + j, KROWS, stride=ANG), :]
        out[j] = jnp.concatenate([real, imag], axis=0)
        return carry

    lax.fori_loop(0, HALF, step, 0, unroll=36)
    keep = pltpu.make_async_copy(out, far, sem)
    keep.start()
    keep.wait()


def sum_kernel(*refs):
    far_small, (far_post, far_ydata, out, rows, slots, post, ydata) = refs[:4], refs[4:11]
    small, (sem, small_sem) = refs[11:15], refs[15:]
    all_stats, stats, by_class, csq = small
    first_copies = [pltpu.make_async_copy(a, b, small_sem.at[i]) for i, (a, b) in enumerate(zip(far_small, small))]
    for copy in first_copies:
        copy.start()
    copies = []
    for part in range(PARTS):
        lines = pl.ds(part * HALF // PARTS, HALF // PARTS)
        copies.append(pltpu.make_async_copy(far_post.at[lines], post.at[lines], sem.at[0, part]))
        copies.append(pltpu.make_async_copy(far_ydata.at[lines], ydata.at[lines], sem.at[1, part]))
    for copy in copies:
        copy.start()
    for copy in first_copies:
        copy.wait()
    tops, totals = all_stats[:, 0, :], all_stats[:, 1, :]
    top = jnp.max(tops, axis=0, keepdims=True)
    total = jnp.sum(totals * jnp.exp(tops - top), axis=0, keepdims=True)
    share = jnp.exp(stats[0, 0:1] - top) / total

    def step(j, carry):
        wide = post[j] * share
        real, imag = wide[:KROWS], wide[KROWS:]
        weights = jnp.concatenate([real, turn(real), imag, turn(imag)], axis=0)[:, :CYCLES]
        both = dot(weights.astype(bf16), ydata[j])
        other = turn(both[KPAD:])
        other = jnp.where(left(other.shape), other, -other)
        rows[pl.ds(j, KPAD, stride=HALF), :] = both[:KPAD] + other
        return carry

    for part in range(PARTS):
        copies[2 * part].wait()
        copies[2 * part + 1].wait()
        lax.fori_loop(part * HALF // PARTS, (part + 1) * HALF // PARTS, step, 0, unroll=HALF // PARTS)
    mass = by_class[...] * share
    mass = jnp.concatenate([mass, turn(mass)], axis=0)[:, :CYCLES]
    weight = lax.dot_general(mass, csq[...], NN, precision=lax.Precision.HIGHEST, preferred_element_type=f32)
    high, low = halves(weight)
    scales = jnp.where(left(weight.shape), high.astype(f32), turn(low.astype(f32)))
    for part in range(ZL):
        first = part * CHUNK // HALF
        base = part * SLOT
        slots[base + CHUNK : base + SLOT] = jnp.zeros((SLOT - CHUNK, LANES), f32)
        slots[base : base + CHUNK] = rows[part * CHUNK : (part + 1) * CHUNK]
        slots[base + CHUNK : base + CHUNK + SPAN] = scales[first : first + SPAN]
        out[part] = slots[base : base + SLOT].astype(bf16)


LAST = CHUNK // 8 * 8


def fold_kernel(pieces, out):
    total = pieces[0].astype(f32)
    for s in range(1, ZL):
        total = total + pieces[s].astype(f32)
    rows = total[LAST:]
    scales = rows + turn(rows)
    high = scales.astype(bf16).astype(f32)
    scales = jnp.where(left(scales.shape), high, scales - high)
    row = lax.broadcasted_iota(jnp.int32, rows.shape, 0)
    rows = jnp.where(row < CHUNK - LAST, rows, scales)
    out[...] = jnp.concatenate([total[:LAST], rows], axis=0).astype(bf16)


def hat_kernel(part, pieces, out):
    total = pieces[0].astype(f32)
    for s in range(1, ZH):
        total = total + pieces[s].astype(f32)
    scales = total[CHUNK : CHUNK + SPAN]
    scales = 1.0 / (scales + turn(scales) + PRIOR_WEIGHT)
    row = lax.broadcasted_iota(jnp.int32, total.shape, 0) + part[0] * (CHUNK % HALF)
    factor = jnp.broadcast_to(scales[SPAN - 1 :], total.shape)
    for i in range(SPAN - 2, -1, -1):
        factor = jnp.where(row < (i + 1) * HALF, scales[i : i + 1], factor)
    out[...] = (total * factor).astype(bf16)


def image_kernel(place, table, hats, *refs):
    out, flat, real, imag, stage, sem = refs[-6:]
    x_lo = place[0]
    copies, shares = [], []
    for core in range(CORE):
        i = core
        base = core * PER_CORE + x_lo * (KD - 1)
        for part in range(ZL):
            flat[i, part * CHUNK : (part + 1) * CHUNK] = hats[i, part].astype(f32)[:CHUNK]
        for step, (first, last) in enumerate(GROUPS):
            for k in range(first, last):
                rows = flat[i, k * HALF : (k + 1) * HALF].T.astype(bf16)
                real[i, k * CYCLES : (k + 1) * CYCLES] = rows[:CYCLES]
                imag[i, k * CYCLES : (k + 1) * CYCLES] = rows[CYCLES:]
            lines = slice(first * CYCLES, last * CYCLES)
            image = dot(real[i, lines], table[0]) + dot(imag[i, lines], table[2])
            image = image + (dot(real[i, lines], table[1]) + dot(imag[i, lines], table[3]))
            stage[i, first:last] = image.astype(bf16).reshape(last - first, CYCLES, ANG)
            begin = max(first, 1)
            here, there = pl.ds(begin, last - begin), pl.ds(base + begin, last - begin)
            copy = pltpu.make_async_copy(stage.at[i, here], out.at[there], sem.at[i, step])
            copy.start()
            copies.append(copy)

        shared = pltpu.make_async_copy(stage.at[i, pl.ds(0, 1)], out.at[pl.ds(base, 1)], sem.at[i, len(GROUPS)])
        pl.when(x_lo == 0)(shared.start)
        shares.append(shared)

    for copy in copies:
        copy.wait()
    for shared in shares:
        pl.when(x_lo == 0)(shared.wait)


VMEM = pl.BlockSpec(memory_space=pltpu.VMEM)
SMEM = pl.BlockSpec(memory_space=pltpu.SMEM)
HBM = pl.BlockSpec(memory_space=pltpu.HBM)


def call(kernel, ins, outs, scratch, flops, nbytes, aliases=None, out_specs=None, limit=48):
    out_shape = [jax.ShapeDtypeStruct(shape, dtype) for shape, dtype in outs]
    single = len(out_shape) == 1
    specs = out_specs or [VMEM] * len(out_shape)
    return pl.pallas_call(
        kernel,
        out_shape=out_shape[0] if single else out_shape,
        in_specs=ins,
        out_specs=specs[0] if single else specs,
        scratch_shapes=scratch,
        input_output_aliases=aliases or {},
        compiler_params=pltpu.CompilerParams(vmem_limit_bytes=limit * 2**20),
        cost_estimate=pl.CostEstimate(flops=flops, bytes_accessed=nbytes, transcendentals=0),
    )


def swap(axis, value):
    return lax.ppermute(value, axis, [(0, 1), (1, 0)])


def share(group_ids, particles, ctf_table, forward):
    return call(
        share_kernel,
        [SMEM, VMEM, VMEM, VMEM],
        [((SOURCES, MSG, LANES), bf16)],
        [pltpu.VMEM((MSG, LANES), bf16), pltpu.SemaphoreType.DMA((SOURCES,))],
        10**7,
        10**6,
        out_specs=[HBM],
        limit=64,
    )(group_ids, particles, ctf_table, forward)


def classes(start, references, forward):
    return call(
        class_kernel,
        [SMEM, HBM, VMEM],
        [((HALF, KPAD, LANES), bf16), ((KPAD, LANES), f32)],
        [
            pltpu.VMEM((KPAD, CYCLES, ANG), bf16),
            pltpu.VMEM(((KPAD + 1) * HALF, LANES), f32),
            pltpu.SemaphoreType.DMA,
        ],
        10**9,
        4 * 10**6,
        limit=64,
    )(start, references, forward)


def scores(place, own, other, rmat, power, table):
    return call(
        score_kernel,
        [SMEM] + [VMEM] * 5,
        [
            ((ROT, KROWS * LANES), f32),
            ((CORE * SOURCES, 8, LANES), f32),
            ((KROWS, LANES), f32),
            ((COUNT, LANES), f32),
            ((HALF, COUNT, LANES), bf16),
        ],
        [
            pltpu.VMEM(((CORE * SOURCES + 1) * MSG, LANES), f32),
            pltpu.VMEM(((KROWS + 1) * ANG, LANES), f32),
            pltpu.VMEM((HALF, COUNT, LANES), bf16),
            pltpu.SemaphoreType.DMA,
        ],
        10**9,
        8 * 10**6,
        limit=64,
        out_specs=[VMEM] * 4 + [HBM],
    )(place, own, other, rmat, power, table)


def posts(expo, table):
    return call(
        post_kernel,
        [VMEM, VMEM],
        [((HALF, KPAD, LANES), f32)],
        [
            pltpu.VMEM(((KROWS + 1) * ANG, LANES), f32),
            pltpu.VMEM((HALF, KPAD, LANES), f32),
            pltpu.SemaphoreType.DMA,
        ],
        10**9,
        3 * 10**6,
        limit=64,
        out_specs=[HBM],
    )(expo, table)


def sums_of(all_stats, stats, by_class, csq, post, ydata):
    return call(
        sum_kernel,
        [HBM] * 6,
        [((ZL, SLOT, LANES), bf16)],
        [
            pltpu.VMEM(((KPAD + 1) * HALF, LANES), f32),
            pltpu.VMEM((ZL * SLOT, LANES), f32),
            pltpu.VMEM((HALF, KPAD, LANES), f32),
            pltpu.VMEM((HALF, COUNT, LANES), bf16),
            pltpu.VMEM((CORE * SOURCES, 8, LANES), f32),
            pltpu.VMEM((CORE * SOURCES, 8, LANES), f32),
            pltpu.VMEM((KROWS, LANES), f32),
            pltpu.VMEM((COUNT, LANES), f32),
            pltpu.SemaphoreType.DMA((2, PARTS)),
            pltpu.SemaphoreType.DMA((4,)),
        ],
        10**9,
        8 * 10**6,
        limit=64,
    )(all_stats, stats, by_class, csq, post, ydata)


def images(place, hats, inverse, result):
    extra = [] if result is None else [result]
    return call(
        image_kernel,
        [SMEM, VMEM, VMEM] + [HBM] * len(extra),
        [((CORE * PER_CORE, CYCLES, ANG), bf16)],
        [
            pltpu.VMEM((CORE, KD * HALF, LANES), f32),
            pltpu.VMEM((CORE, KD * CYCLES, HALF), bf16),
            pltpu.VMEM((CORE, KD * CYCLES, HALF), bf16),
            pltpu.VMEM((CORE, KD, CYCLES, ANG), bf16),
            pltpu.SemaphoreType.DMA((CORE, len(GROUPS) + 1)),
        ],
        1000,
        1000,
        {3: 0} if extra else None,
        [HBM],
    )(place.reshape(1), inverse, hats, *extra)


def body(particles, group_ids, ctf_table, references):
    core, x_lo = lax.axis_index("core"), lax.axis_index("x_lo")
    forward = jnp.asarray(forward_table())
    place = jnp.stack([core, x_lo])

    messages = share(group_ids, particles, ctf_table, forward)
    own = lax.all_to_all(messages, ("x_lo", "x_hi", "y"), 0, 0, tiled=True)
    start = (core * PER_CORE + x_lo * (KD - 1)).reshape(1)
    rmat, power = classes(start, references, forward)
    part = lax.axis_index("z_lo").reshape(1)
    own, rmat, power, part = lax.optimization_barrier((own, rmat, power, part))
    other = swap("core", own)

    expo, stats, by_class, csq, ydata = scores(
        place, own, other, rmat, power, jnp.asarray(search_table().reshape(3 * ROT, ANG))
    )
    all_stats = lax.all_to_all(stats, ("core", "x_lo", "x_hi", "y"), 0, 0, tiled=True)
    post = posts(expo, jnp.asarray(post_table().reshape(3 * ANG, ROT)))
    sums = sums_of(all_stats, stats, by_class, csq, post, ydata)

    near = lax.all_to_all(sums, "z_lo", 0, 0, tiled=True)
    near = call(fold_kernel, [VMEM], [((SLOT, LANES), bf16)], [], 10**6, 10**6, limit=20)(near)
    near = lax.all_gather(near, "z_hi")
    hat = call(hat_kernel, [SMEM, VMEM], [((SLOT, LANES), bf16)], [], 10**6, 10**6, limit=20)(part, near)

    inverse = jnp.asarray(inverse_table())
    near = lax.all_gather(hat, "z_lo")
    far = swap("x_lo", near)
    result = images(x_lo, lax.all_gather(near, "core"), inverse, None)
    far, result = lax.optimization_barrier((far, result))
    return images(1 - x_lo, lax.all_gather(far, "core"), inverse, result)


def solution(mesh):
    fine = Mesh(mesh.devices.reshape(X, ZH, ZL, CORE, 2, 4), DOM + CLS)
    in_specs = (P(DOM + CLS, None, None), P(DOM + CLS), P(), P(CLS, None, None))
    return jax.shard_map(body, mesh=fine, in_specs=in_specs, out_specs=P(CLS, None, None), check_vma=False)
```

```python
import math

import jax
import jax.numpy as jnp
import ml_dtypes
import numpy as np
from jax import lax
from jax.experimental import pallas as pl
from jax.experimental.pallas import tpu as pltpu
from jax.sharding import Mesh
from jax.sharding import PartitionSpec as P

CYCLES = 64
ANG = 288
ROT = 72
HALF = ANG // 2
LANES = 2 * CYCLES
PRIOR_WEIGHT = 1.0
SCORE_SCALE = 4.0 / math.sqrt(CYCLES * ANG)

X, Z, CORE, SIDE = 2, 16, 2, 8
ZH, ZL = 4, 4
MINE = 2
PER_CORE = 25
KD = 13
KPAD = 16
KROWS = KPAD // 2
PARTS = 2
EXPO = 8 * 72
KEPT = EXPO + 8 + 64
ROOMY = 36000
LONG = 1100
GROUPS = ((0, 5), (5, 9), (9, 13))
SOURCES = X * SIDE
COUNT = MINE * CORE * SOURCES
MSG = MINE * HALF + 16
CHUNK = KD * HALF // ZL
SPAN = -(-CHUNK // HALF) + 1
SLOT = 480

DOM = ("x_lo", "z_hi", "z_lo", "core")
CLS = ("x_hi", "y")

NT = (((1,), (1,)), ((), ()))
NN = (((1,), (0,)), ((), ()))
f32 = jnp.float32
bf16 = jnp.bfloat16


def angles(rows, cols, factor):
    index = np.arange(rows)[:, None] * factor * np.arange(cols)[None, :] % ANG
    return 2.0 * math.pi * index / ANG


def split(table, count):
    rest, pieces = table.astype(np.float32), []
    for _ in range(count):
        pieces.append(rest.astype(ml_dtypes.bfloat16))
        rest = rest - pieces[-1].astype(np.float32)
    return np.stack(pieces)


def forward_table():
    angle = angles(HALF + 1, ANG, 1)
    real = np.cos(angle[:HALF])
    imag = np.concatenate([np.cos(angle[HALF:]), np.sin(angle[1:HALF])])
    return split(np.concatenate([real, imag]), 3)


def weights_of_rows():
    return np.where(np.arange(HALF) == 0, 1.0, 2.0)[:, None] / ANG


def search_table():
    angle = angles(HALF, ROT, ANG // ROT)
    scale = weights_of_rows()
    return split(np.concatenate([np.cos(angle) * scale, -np.sin(angle) * scale]).T, 3)


def post_table():
    angle = angles(HALF, ROT, ANG // ROT)
    return split(np.concatenate([np.cos(angle), np.sin(angle)]), 3)


def inverse_table():
    angle = angles(HALF + 1, ANG, 1)
    scale = weights_of_rows()
    real = np.cos(angle[:HALF]) * scale
    imag = np.concatenate([np.cos(angle[HALF:]), np.sin(angle[1:HALF])]) * scale
    return np.concatenate([split(real, 2), split(imag, 2)])


def dot(a, b, dims=NN):
    return lax.dot_general(a, b, dims, preferred_element_type=f32)


def halves(values):
    high = values.astype(bf16)
    return high, (values - high.astype(f32)).astype(bf16)


def thirds(values):
    high = values.astype(bf16)
    rest = values - high.astype(f32)
    mid = rest.astype(bf16)
    return high, mid, (rest - mid.astype(f32)).astype(bf16)


def dot3(table, values):
    high, mid, low = thirds(values)
    rows = table.shape[0] // 3
    first = dot(table[...], high)
    second = dot(table[: 2 * rows], mid)
    small = (first[2 * rows :] + second[rows:]) + dot(table[:rows], low)
    return first[:rows] + (first[rows : 2 * rows] + second[:rows] + small)


def transform(table, images):
    return dot(table[0], images, NT) + (dot(table[1], images, NT) + dot(table[2], images, NT))


def turn(values):
    return pltpu.roll(values, CYCLES, 1)


def left(shape):
    return lax.broadcasted_iota(jnp.int32, shape, len(shape) - 1) < CYCLES


def fold(spec):
    real, imag = spec[:HALF], spec[HALF:]
    side = left(real.shape)
    return jnp.where(side, real, turn(imag)), jnp.where(side, turn(real), imag)


def share_kernel(ids, x, ctf, table, outs, out, sem):
    images = x[...].reshape(MINE * CYCLES, ANG)
    factor = jnp.concatenate([ctf[pl.ds(ids[0], 1), :], ctf[pl.ds(ids[1], 1), :]], axis=1)
    spec = transform(table, images) * factor
    first, second = fold(spec)
    out[0:HALF] = first.astype(bf16)
    out[HALF : 2 * HALF] = second.astype(bf16)
    high, mid, low = thirds(factor)
    row = lax.broadcasted_iota(jnp.int32, (16, LANES), 0)
    tags = jnp.where(row == 0, high.astype(f32), jnp.where(row == 1, mid.astype(f32), jnp.where(row == 2, low.astype(f32), 0.0)))
    out[2 * HALF : MSG] = tags.astype(bf16)
    copies = [pltpu.make_async_copy(out, outs.at[s], sem.at[s]) for s in range(SOURCES)]
    for copy in copies:
        copy.start()
    for copy in copies:
        copy.wait()


def class_kernel(start, refs, table, out, power, images, rows, sem):
    copy = pltpu.make_async_copy(refs.at[pl.ds(start[0], KD)], images.at[pl.ds(0, KD)], sem)
    copy.start()
    images[KD:] = jnp.zeros((KPAD - KD, CYCLES, ANG), bf16)
    ones = jnp.ones((8, ANG), bf16)
    copy.wait()
    for step in range(KPAD // 4):
        block = images[4 * step : 4 * step + 4].reshape(4 * CYCLES, ANG)
        spec = transform(table, block)
        wide = block.astype(f32)
        high, low = halves(wide * wide)
        energy = dot(ones, high, NT) + dot(ones, low, NT)
        for pair in range(2):
            k = 4 * step + 2 * pair
            lanes = slice(pair * LANES, (pair + 1) * LANES)
            first, second = fold(spec[:, lanes])
            rows[k * HALF : (k + 1) * HALF] = first.astype(bf16).astype(f32)
            rows[(k + 1) * HALF : (k + 2) * HALF] = second.astype(bf16).astype(f32)
            part = energy[:, lanes]
            side = left(part.shape)
            power[k : k + 1] = jnp.where(side, part, 0.0)[0:1]
            power[k + 1 : k + 2] = jnp.where(side, turn(part), 0.0)[0:1]

    def step(j, carry):
        plain = rows[pl.ds(j, KPAD, stride=HALF), :]
        out[j] = plain.astype(bf16)
        return carry

    lax.fori_loop(0, HALF, step, 0, unroll=36)


def score_kernel(place, own, other, rmat, power, table, stats, far_kept, far, wide, pairs, ydata, kept, sem):
    core, x_lo = place[0], place[1]

    def widen(s, carry):
        mine = pl.multiple_of((core * SOURCES + s) * MSG, 8)
        theirs = pl.multiple_of(((1 - core) * SOURCES + s) * MSG, 8)
        wide[pl.ds(mine, MSG), :] = own[s].astype(f32)
        wide[pl.ds(theirs, MSG), :] = other[s].astype(f32)
        return carry

    lax.fori_loop(0, SOURCES, widen, 0, unroll=2)
    many = CORE * SOURCES
    factor = wide[pl.ds(2 * HALF, many, stride=MSG), :] + wide[pl.ds(2 * HALF + 1, many, stride=MSG), :]
    factor = factor + wide[pl.ds(2 * HALF + 2, many, stride=MSG), :]
    square = factor * factor
    side = left(square.shape)
    square = jnp.concatenate([jnp.where(side, square, 0.0), jnp.where(side, turn(square), 0.0)], axis=0)
    kept[EXPO + KROWS : KEPT] = square
    energy = lax.dot_general(
        power[...],
        jnp.concatenate([square, square], axis=0),
        NT,
        precision=lax.Precision.HIGHEST,
        preferred_element_type=f32,
    )
    side = left((KROWS, LANES))
    energy = jnp.where(side, energy[:KROWS], energy[KROWS:])

    def step(j, carry):
        rows = jnp.concatenate([wide[pl.ds(j, many, stride=MSG), :], wide[pl.ds(HALF + j, many, stride=MSG), :]], axis=0)
        rows = rows.astype(bf16)
        ydata[j] = rows
        plain = rmat[j].astype(f32)
        cross = turn(plain)
        cross = jnp.where(left(cross.shape), cross, -cross)
        both = dot(jnp.concatenate([plain, cross], axis=0).astype(bf16), rows, NT)
        straight = jnp.concatenate([both[:KROWS], both[KROWS : 2 * KROWS]], axis=1)
        crossed = jnp.concatenate([both[2 * KROWS : 3 * KROWS], both[3 * KROWS :]], axis=1)
        pairs[pl.ds(j, KROWS, stride=ANG), :] = straight
        pairs[pl.ds(HALF + j, KROWS, stride=ANG), :] = crossed
        return carry

    lax.fori_loop(0, HALF, step, 0, unroll=48)
    keep = pltpu.make_async_copy(ydata, far.at[pl.ds(0, HALF)], sem.at[0])
    keep.start()
    top = jnp.full((1, LANES), -3.0e38, f32)
    lane_side = left((ROT, LANES))
    crosses = []
    for kk in range(0, KROWS, 2):
        two = [pairs[k * ANG : (k + 1) * ANG] for k in (kk, kk + 1)]
        wide_cross = dot3(table, jnp.concatenate(two, axis=1))
        crosses += [wide_cross[:, :LANES], wide_cross[:, LANES:]]
    for kk in range(KROWS):
        cross = crosses[kk]
        score = SCORE_SCALE * (cross - 0.5 * energy[kk : kk + 1])
        if kk + KROWS >= KD:
            score = jnp.where(lane_side, score, -3.0e38)
        if kk == 0:
            score = jnp.where(jnp.logical_and(lane_side, x_lo == 1), -3.0e38, score)
        kept[kk * ROT : (kk + 1) * ROT] = score
        top = jnp.maximum(top, jnp.max(score, axis=0, keepdims=True))
    top = jnp.maximum(top, turn(top))
    total = jnp.zeros((1, LANES), f32)
    for kk in range(KROWS):
        value = jnp.exp(kept[kk * ROT : (kk + 1) * ROT] - top)
        kept[kk * ROT : (kk + 1) * ROT] = value
        part = jnp.sum(value, axis=0, keepdims=True)
        kept[EXPO + kk : EXPO + kk + 1] = part
        total = total + part
    total = total + turn(total)
    store = pltpu.make_async_copy(kept, far_kept.at[pl.ds(0, KEPT)], sem.at[1])
    store.start()
    pair = jnp.where(lax.broadcasted_iota(jnp.int32, (8, LANES), 0) == 0, top, total)
    for s in range(CORE * SOURCES):
        stats[s] = pair
    keep.wait()
    store.wait()


def post_kernel(far_kept, table, far, rows, out, expo, sem):
    fetch = pltpu.make_async_copy(far_kept.at[pl.ds(0, EXPO)], expo, sem)
    fetch.start()
    fetch.wait()
    for kk in range(0, KROWS, 2):
        both = dot3(table, jnp.concatenate([expo[k * ROT : (k + 1) * ROT] for k in (kk, kk + 1)], axis=1))
        rows[kk * ANG : (kk + 1) * ANG] = both[:, :LANES]
        rows[(kk + 1) * ANG : (kk + 2) * ANG] = both[:, LANES:]

    def step(j, carry):
        real = rows[pl.ds(j, KROWS, stride=ANG), :]
        imag = rows[pl.ds(HALF + j, KROWS, stride=ANG), :]
        out[j] = jnp.concatenate([real, imag], axis=0)
        return carry

    lax.fori_loop(0, HALF, step, 0, unroll=36)
    keep = pltpu.make_async_copy(out, far, sem)
    keep.start()
    keep.wait()


def sum_kernel(*refs):
    kept = refs[2]
    far_small = refs[:2] + (kept.at[pl.ds(EXPO, KROWS)], kept.at[pl.ds(EXPO + KROWS, COUNT)])
    far_post, far_ydata, out, rows, slots, post, ydata = refs[3:10]
    small, (sem, small_sem) = refs[10:14], refs[14:]
    all_stats, stats, by_class, csq = small
    first_copies = [pltpu.make_async_copy(a, b, small_sem.at[i]) for i, (a, b) in enumerate(zip(far_small, small))]
    for copy in first_copies:
        copy.start()
    copies = []
    for part in range(PARTS):
        lines = pl.ds(part * HALF // PARTS, HALF // PARTS)
        copies.append(pltpu.make_async_copy(far_post.at[lines], post.at[lines], sem.at[0, part]))
        copies.append(pltpu.make_async_copy(far_ydata.at[lines], ydata.at[lines], sem.at[1, part]))
    for copy in copies:
        copy.start()
    for copy in first_copies:
        copy.wait()
    tops, totals = all_stats[:, 0, :], all_stats[:, 1, :]
    top = jnp.max(tops, axis=0, keepdims=True)
    total = jnp.sum(totals * jnp.exp(tops - top), axis=0, keepdims=True)
    share = jnp.exp(stats[0, 0:1] - top) / total

    def step(j, carry):
        wide = post[j] * share
        real, imag = wide[:KROWS], wide[KROWS:]
        weights = jnp.concatenate([real, turn(real), imag, turn(imag)], axis=0)[:, :CYCLES]
        both = dot(weights.astype(bf16), ydata[j])
        other = turn(both[KPAD:])
        other = jnp.where(left(other.shape), other, -other)
        rows[pl.ds(j, KPAD, stride=HALF), :] = both[:KPAD] + other
        return carry

    for part in range(PARTS):
        copies[2 * part].wait()
        copies[2 * part + 1].wait()
        lax.fori_loop(part * HALF // PARTS, (part + 1) * HALF // PARTS, step, 0, unroll=HALF // PARTS)
    mass = by_class[...] * share
    mass = jnp.concatenate([mass, turn(mass)], axis=0)[:, :CYCLES]
    weight = lax.dot_general(mass, csq[...], NN, precision=lax.Precision.HIGHEST, preferred_element_type=f32)
    high, low = halves(weight)
    scales = jnp.where(left(weight.shape), high.astype(f32), turn(low.astype(f32)))
    for part in range(ZL):
        first = part * CHUNK // HALF
        base = part * SLOT
        slots[base + CHUNK : base + SLOT] = jnp.zeros((SLOT - CHUNK, LANES), f32)
        slots[base : base + CHUNK] = rows[part * CHUNK : (part + 1) * CHUNK]
        slots[base + CHUNK : base + CHUNK + SPAN] = scales[first : first + SPAN]
        out[part] = slots[base : base + SLOT].astype(bf16)


LAST = CHUNK // 8 * 8


def fold_kernel(pieces, out):
    total = pieces[0].astype(f32)
    for s in range(1, ZL):
        total = total + pieces[s].astype(f32)
    rows = total[LAST:]
    scales = rows + turn(rows)
    high = scales.astype(bf16).astype(f32)
    scales = jnp.where(left(scales.shape), high, scales - high)
    row = lax.broadcasted_iota(jnp.int32, rows.shape, 0)
    rows = jnp.where(row < CHUNK - LAST, rows, scales)
    out[...] = jnp.concatenate([total[:LAST], rows], axis=0).astype(bf16)


def hat_kernel(part, pieces, out):
    total = pieces[0].astype(f32)
    for s in range(1, ZH):
        total = total + pieces[s].astype(f32)
    scales = total[CHUNK : CHUNK + SPAN]
    scales = 1.0 / (scales + turn(scales) + PRIOR_WEIGHT)
    row = lax.broadcasted_iota(jnp.int32, total.shape, 0) + part[0] * (CHUNK % HALF)
    factor = jnp.broadcast_to(scales[SPAN - 1 :], total.shape)
    for i in range(SPAN - 2, -1, -1):
        factor = jnp.where(row < (i + 1) * HALF, scales[i : i + 1], factor)
    out[...] = (total * factor).astype(bf16)


def image_kernel(place, table, hats, *refs):
    out, flat, real, imag, stage, sem = refs[-6:]
    x_lo = place[0]
    copies, shares = [], []
    for core in range(CORE):
        i = core
        base = core * PER_CORE + x_lo * (KD - 1)
        for part in range(ZL):
            flat[i, part * CHUNK : (part + 1) * CHUNK] = hats[i, part].astype(f32)[:CHUNK]
        for step, (first, last) in enumerate(GROUPS):
            for k in range(first, last):
                rows = flat[i, k * HALF : (k + 1) * HALF].T.astype(bf16)
                real[i, k * CYCLES : (k + 1) * CYCLES] = rows[:CYCLES]
                imag[i, k * CYCLES : (k + 1) * CYCLES] = rows[CYCLES:]
            lines = slice(first * CYCLES, last * CYCLES)
            image = dot(real[i, lines], table[0]) + dot(imag[i, lines], table[2])
            image = image + (dot(real[i, lines], table[1]) + dot(imag[i, lines], table[3]))
            stage[i, first:last] = image.astype(bf16).reshape(last - first, CYCLES, ANG)
            begin = max(first, 1)
            here, there = pl.ds(begin, last - begin), pl.ds(base + begin, last - begin)
            copy = pltpu.make_async_copy(stage.at[i, here], out.at[there], sem.at[i, step])
            copy.start()
            copies.append(copy)

        shared = pltpu.make_async_copy(stage.at[i, pl.ds(0, 1)], out.at[pl.ds(base, 1)], sem.at[i, len(GROUPS)])
        pl.when(x_lo == 0)(shared.start)
        shares.append(shared)

    for copy in copies:
        copy.wait()
    for shared in shares:
        pl.when(x_lo == 0)(shared.wait)


VMEM = pl.BlockSpec(memory_space=pltpu.VMEM)
SMEM = pl.BlockSpec(memory_space=pltpu.SMEM)
HBM = pl.BlockSpec(memory_space=pltpu.HBM)


def call(kernel, ins, outs, scratch, flops, nbytes, aliases=None, out_specs=None, limit=48):
    out_shape = [jax.ShapeDtypeStruct(shape, dtype) for shape, dtype in outs]
    single = len(out_shape) == 1
    specs = out_specs or [VMEM] * len(out_shape)
    return pl.pallas_call(
        kernel,
        out_shape=out_shape[0] if single else out_shape,
        in_specs=ins,
        out_specs=specs[0] if single else specs,
        scratch_shapes=scratch,
        input_output_aliases=aliases or {},
        compiler_params=pltpu.CompilerParams(vmem_limit_bytes=limit * 2**20),
        cost_estimate=pl.CostEstimate(flops=flops, bytes_accessed=nbytes, transcendentals=0),
    )


def swap(axis, value):
    return lax.ppermute(value, axis, [(0, 1), (1, 0)])


def share(group_ids, particles, ctf_table, forward):
    return call(
        share_kernel,
        [SMEM, VMEM, VMEM, VMEM],
        [((SOURCES, MSG, LANES), bf16)],
        [pltpu.VMEM((MSG, LANES), bf16), pltpu.SemaphoreType.DMA((SOURCES,))],
        10**7,
        10**6,
        out_specs=[HBM],
        limit=64,
    )(group_ids, particles, ctf_table, forward)


def classes(start, references, forward):
    return call(
        class_kernel,
        [SMEM, HBM, VMEM],
        [((HALF, KPAD, LANES), bf16), ((KPAD, LANES), f32)],
        [
            pltpu.VMEM((KPAD, CYCLES, ANG), bf16),
            pltpu.VMEM(((KPAD + 1) * HALF, LANES), f32),
            pltpu.SemaphoreType.DMA,
        ],
        10**9,
        4 * 10**6,
        limit=24,
    )(start, references, forward)


def scores(place, own, other, rmat, power, table):
    return call(
        score_kernel,
        [SMEM] + [VMEM] * 5,
        [
            ((CORE * SOURCES, 8, LANES), f32),
            ((ROOMY, LANES), f32),
            ((LONG, COUNT, LANES), bf16),
        ],
        [
            pltpu.VMEM(((CORE * SOURCES + 1) * MSG, LANES), f32),
            pltpu.VMEM(((KROWS + 1) * ANG, LANES), f32),
            pltpu.VMEM((HALF, COUNT, LANES), bf16),
            pltpu.VMEM((KEPT, LANES), f32),
            pltpu.SemaphoreType.DMA((2,)),
        ],
        10**9,
        8 * 10**6,
        limit=48,
        out_specs=[VMEM, HBM, HBM],
    )(place, own, other, rmat, power, table)


def posts(expo, table):
    return call(
        post_kernel,
        [HBM, VMEM],
        [((HALF, KPAD, LANES), f32)],
        [
            pltpu.VMEM(((KROWS + 1) * ANG, LANES), f32),
            pltpu.VMEM((HALF, KPAD, LANES), f32),
            pltpu.VMEM((EXPO, LANES), f32),
            pltpu.SemaphoreType.DMA,
        ],
        10**9,
        3 * 10**6,
        limit=64,
        out_specs=[HBM],
    )(expo, table)


def sums_of(all_stats, stats, kept, post, ydata):
    return call(
        sum_kernel,
        [HBM] * 5,
        [((ZL, SLOT, LANES), bf16)],
        [
            pltpu.VMEM(((KPAD + 1) * HALF, LANES), f32),
            pltpu.VMEM((ZL * SLOT, LANES), f32),
            pltpu.VMEM((HALF, KPAD, LANES), f32),
            pltpu.VMEM((HALF, COUNT, LANES), bf16),
            pltpu.VMEM((CORE * SOURCES, 8, LANES), f32),
            pltpu.VMEM((CORE * SOURCES, 8, LANES), f32),
            pltpu.VMEM((KROWS, LANES), f32),
            pltpu.VMEM((COUNT, LANES), f32),
            pltpu.SemaphoreType.DMA((2, PARTS)),
            pltpu.SemaphoreType.DMA((4,)),
        ],
        10**9,
        8 * 10**6,
        limit=64,
    )(all_stats, stats, kept, post, ydata)


def images(place, hats, inverse, result):
    extra = [] if result is None else [result]
    return call(
        image_kernel,
        [SMEM, VMEM, VMEM] + [HBM] * len(extra),
        [((CORE * PER_CORE, CYCLES, ANG), bf16)],
        [
            pltpu.VMEM((CORE, KD * HALF, LANES), f32),
            pltpu.VMEM((CORE, KD * CYCLES, HALF), bf16),
            pltpu.VMEM((CORE, KD * CYCLES, HALF), bf16),
            pltpu.VMEM((CORE, KD, CYCLES, ANG), bf16),
            pltpu.SemaphoreType.DMA((CORE, len(GROUPS) + 1)),
        ],
        1000,
        1000,
        {3: 0} if extra else None,
        [HBM],
    )(place.reshape(1), inverse, hats, *extra)


def body(particles, group_ids, ctf_table, references):
    core, x_lo = lax.axis_index("core"), lax.axis_index("x_lo")
    forward = jnp.asarray(forward_table())
    place = jnp.stack([core, x_lo])

    messages = share(group_ids, particles, ctf_table, forward)
    own = lax.all_to_all(messages, ("x_lo", "x_hi", "y"), 0, 0, tiled=True)
    start = (core * PER_CORE + x_lo * (KD - 1)).reshape(1)
    rmat, power = classes(start, references, forward)
    part = lax.axis_index("z_lo").reshape(1)
    own, part = lax.optimization_barrier((own, part))
    other = swap("core", own)

    stats, kept, ydata = scores(
        place, own, other, rmat, power, jnp.asarray(search_table().reshape(3 * ROT, ANG))
    )
    all_stats = lax.all_to_all(stats, ("core", "x_lo", "x_hi", "y"), 0, 0, tiled=True)
    post = posts(kept, jnp.asarray(post_table().reshape(3 * ANG, ROT)))
    sums = sums_of(all_stats, stats, kept, post, ydata)

    near = lax.all_to_all(sums, "z_lo", 0, 0, tiled=True)
    near = call(fold_kernel, [VMEM], [((SLOT, LANES), bf16)], [], 10**6, 10**6, limit=20)(near)
    near = lax.all_gather(near, "z_hi")
    hat = call(hat_kernel, [SMEM, VMEM], [((SLOT, LANES), bf16)], [], 10**6, 10**6, limit=20)(part, near)

    inverse = jnp.asarray(inverse_table())
    near = lax.all_gather(hat, "z_lo")
    far = swap("x_lo", near)
    result = images(x_lo, lax.all_gather(near, "core"), inverse, None)
    far, result = lax.optimization_barrier((far, result))
    return images(1 - x_lo, lax.all_gather(far, "core"), inverse, result)


def solution(mesh):
    fine = Mesh(mesh.devices.reshape(X, ZH, ZL, CORE, 2, 4), DOM + CLS)
    in_specs = (P(DOM + CLS, None, None), P(DOM + CLS), P(), P(CLS, None, None))
    return jax.shard_map(body, mesh=fine, in_specs=in_specs, out_specs=P(CLS, None, None), check_vma=False)
```

```python
import math

import jax
import jax.numpy as jnp
import ml_dtypes
import numpy as np
from jax import lax
from jax.experimental import pallas as pl
from jax.experimental.pallas import tpu as pltpu
from jax.sharding import Mesh
from jax.sharding import PartitionSpec as P

CYCLES = 64
ANG = 288
ROT = 72
HALF = ANG // 2
LANES = 2 * CYCLES
PRIOR_WEIGHT = 1.0
SCORE_SCALE = 4.0 / math.sqrt(CYCLES * ANG)

X, Z, CORE, SIDE = 2, 16, 2, 8
ZH, ZL = 4, 4
MINE = 2
PER_CORE = 25
KD = 13
KPAD = 16
KROWS = KPAD // 2
PARTS = 2
EXPO = 8 * 72
KEPT = EXPO + 8 + 64
ROOMY = 36000
LONG = 1100
GROUPS = ((0, 5), (5, 9), (9, 13))
SOURCES = X * SIDE
COUNT = MINE * CORE * SOURCES
MSG = MINE * HALF + 16
CHUNK = KD * HALF // ZL
SPAN = -(-CHUNK // HALF) + 1
SLOT = 480

DOM = ("x_lo", "z_hi", "z_lo", "core")
CLS = ("x_hi", "y")

NT = (((1,), (1,)), ((), ()))
NN = (((1,), (0,)), ((), ()))
f32 = jnp.float32
bf16 = jnp.bfloat16


def angles(rows, cols, factor):
    index = np.arange(rows)[:, None] * factor * np.arange(cols)[None, :] % ANG
    return 2.0 * math.pi * index / ANG


def split(table, count):
    rest, pieces = table.astype(np.float32), []
    for _ in range(count):
        pieces.append(rest.astype(ml_dtypes.bfloat16))
        rest = rest - pieces[-1].astype(np.float32)
    return np.stack(pieces)


def forward_table():
    angle = angles(HALF + 1, ANG, 1)
    real = np.cos(angle[:HALF])
    imag = np.concatenate([np.cos(angle[HALF:]), np.sin(angle[1:HALF])])
    return split(np.concatenate([real, imag]), 3)


def weights_of_rows():
    return np.where(np.arange(HALF) == 0, 1.0, 2.0)[:, None] / ANG


def search_table():
    angle = angles(HALF, ROT, ANG // ROT)
    scale = weights_of_rows()
    return split(np.concatenate([np.cos(angle) * scale, -np.sin(angle) * scale]).T, 3)


def post_table():
    angle = angles(HALF, ROT, ANG // ROT)
    return split(np.concatenate([np.cos(angle), np.sin(angle)]), 3)


def inverse_table():
    angle = angles(HALF + 1, ANG, 1)
    scale = weights_of_rows()
    real = np.cos(angle[:HALF]) * scale
    imag = np.concatenate([np.cos(angle[HALF:]), np.sin(angle[1:HALF])]) * scale
    return np.concatenate([split(real, 2), split(imag, 2)])


def dot(a, b, dims=NN):
    return lax.dot_general(a, b, dims, preferred_element_type=f32)


def halves(values):
    high = values.astype(bf16)
    return high, (values - high.astype(f32)).astype(bf16)


def thirds(values):
    high = values.astype(bf16)
    rest = values - high.astype(f32)
    mid = rest.astype(bf16)
    return high, mid, (rest - mid.astype(f32)).astype(bf16)


def dot3(table, values):
    high, mid, low = thirds(values)
    rows = table.shape[0] // 3
    first = dot(table[...], high)
    second = dot(table[: 2 * rows], mid)
    small = (first[2 * rows :] + second[rows:]) + dot(table[:rows], low)
    return first[:rows] + (first[rows : 2 * rows] + second[:rows] + small)


def transform(table, images):
    return dot(table[0], images, NT) + (dot(table[1], images, NT) + dot(table[2], images, NT))


def turn(values):
    return pltpu.roll(values, CYCLES, 1)


def left(shape):
    return lax.broadcasted_iota(jnp.int32, shape, len(shape) - 1) < CYCLES


def fold(spec):
    real, imag = spec[:HALF], spec[HALF:]
    side = left(real.shape)
    return jnp.where(side, real, turn(imag)), jnp.where(side, turn(real), imag)


def share_kernel(ids, x, ctf, table, outs, out, sem):
    images = x[...].reshape(MINE * CYCLES, ANG)
    factor = jnp.concatenate([ctf[pl.ds(ids[0], 1), :], ctf[pl.ds(ids[1], 1), :]], axis=1)
    spec = transform(table, images) * factor
    first, second = fold(spec)
    out[0:HALF] = first.astype(bf16)
    out[HALF : 2 * HALF] = second.astype(bf16)
    high, mid, low = thirds(factor)
    row = lax.broadcasted_iota(jnp.int32, (16, LANES), 0)
    tags = jnp.where(row == 0, high.astype(f32), jnp.where(row == 1, mid.astype(f32), jnp.where(row == 2, low.astype(f32), 0.0)))
    out[2 * HALF : MSG] = tags.astype(bf16)
    copies = [pltpu.make_async_copy(out, outs.at[s], sem.at[s]) for s in range(SOURCES)]
    for copy in copies:
        copy.start()
    for copy in copies:
        copy.wait()


def class_kernel(refs, table, out, power, images, rows, sem):
    copy = pltpu.make_async_copy(refs, images.at[pl.ds(0, KD)], sem)
    copy.start()
    images[KD:] = jnp.zeros((KPAD - KD, CYCLES, ANG), bf16)
    ones = jnp.ones((8, ANG), bf16)
    copy.wait()
    for step in range(KPAD // 4):
        block = images[4 * step : 4 * step + 4].reshape(4 * CYCLES, ANG)
        spec = transform(table, block)
        wide = block.astype(f32)
        high, low = halves(wide * wide)
        energy = dot(ones, high, NT) + dot(ones, low, NT)
        for pair in range(2):
            k = 4 * step + 2 * pair
            lanes = slice(pair * LANES, (pair + 1) * LANES)
            first, second = fold(spec[:, lanes])
            rows[k * HALF : (k + 1) * HALF] = first.astype(bf16).astype(f32)
            rows[(k + 1) * HALF : (k + 2) * HALF] = second.astype(bf16).astype(f32)
            part = energy[:, lanes]
            side = left(part.shape)
            power[k : k + 1] = jnp.where(side, part, 0.0)[0:1]
            power[k + 1 : k + 2] = jnp.where(side, turn(part), 0.0)[0:1]

    def step(j, carry):
        plain = rows[pl.ds(j, KPAD, stride=HALF), :]
        out[j] = plain.astype(bf16)
        return carry

    lax.fori_loop(0, HALF, step, 0, unroll=36)


def score_kernel(place, own, other, rmat, power, table, stats, far_kept, far, wide, pairs, ydata, kept, sem):
    core, x_lo = place[0], place[1]

    def widen(s, carry):
        mine = pl.multiple_of((core * SOURCES + s) * MSG, 8)
        theirs = pl.multiple_of(((1 - core) * SOURCES + s) * MSG, 8)
        wide[pl.ds(mine, MSG), :] = own[s].astype(f32)
        wide[pl.ds(theirs, MSG), :] = other[s].astype(f32)
        return carry

    lax.fori_loop(0, SOURCES, widen, 0, unroll=2)
    many = CORE * SOURCES
    factor = wide[pl.ds(2 * HALF, many, stride=MSG), :] + wide[pl.ds(2 * HALF + 1, many, stride=MSG), :]
    factor = factor + wide[pl.ds(2 * HALF + 2, many, stride=MSG), :]
    square = factor * factor
    side = left(square.shape)
    square = jnp.concatenate([jnp.where(side, square, 0.0), jnp.where(side, turn(square), 0.0)], axis=0)
    kept[EXPO + KROWS : KEPT] = square
    energy = lax.dot_general(
        power[...],
        jnp.concatenate([square, square], axis=0),
        NT,
        precision=lax.Precision.HIGHEST,
        preferred_element_type=f32,
    )
    side = left((KROWS, LANES))
    energy = jnp.where(side, energy[:KROWS], energy[KROWS:])

    def step(j, carry):
        rows = jnp.concatenate([wide[pl.ds(j, many, stride=MSG), :], wide[pl.ds(HALF + j, many, stride=MSG), :]], axis=0)
        rows = rows.astype(bf16)
        ydata[j] = rows
        plain = rmat[j].astype(f32)
        cross = turn(plain)
        cross = jnp.where(left(cross.shape), cross, -cross)
        both = dot(jnp.concatenate([plain, cross], axis=0).astype(bf16), rows, NT)
        straight = jnp.concatenate([both[:KROWS], both[KROWS : 2 * KROWS]], axis=1)
        crossed = jnp.concatenate([both[2 * KROWS : 3 * KROWS], both[3 * KROWS :]], axis=1)
        pairs[pl.ds(j, KROWS, stride=ANG), :] = straight
        pairs[pl.ds(HALF + j, KROWS, stride=ANG), :] = crossed
        return carry

    lax.fori_loop(0, HALF, step, 0, unroll=48)
    keep = pltpu.make_async_copy(ydata, far.at[pl.ds(0, HALF)], sem.at[0])
    keep.start()
    top = jnp.full((1, LANES), -3.0e38, f32)
    lane_side = left((ROT, LANES))
    crosses = []
    for kk in range(0, KROWS, 2):
        two = [pairs[k * ANG : (k + 1) * ANG] for k in (kk, kk + 1)]
        wide_cross = dot3(table, jnp.concatenate(two, axis=1))
        crosses += [wide_cross[:, :LANES], wide_cross[:, LANES:]]
    for kk in range(KROWS):
        cross = crosses[kk]
        score = SCORE_SCALE * (cross - 0.5 * energy[kk : kk + 1])
        if kk + KROWS >= KD:
            score = jnp.where(lane_side, score, -3.0e38)
        if kk == 0:
            score = jnp.where(jnp.logical_and(lane_side, x_lo == 1), -3.0e38, score)
        kept[kk * ROT : (kk + 1) * ROT] = score
        top = jnp.maximum(top, jnp.max(score, axis=0, keepdims=True))
    top = jnp.maximum(top, turn(top))
    total = jnp.zeros((1, LANES), f32)
    for kk in range(KROWS):
        value = jnp.exp(kept[kk * ROT : (kk + 1) * ROT] - top)
        kept[kk * ROT : (kk + 1) * ROT] = value
        part = jnp.sum(value, axis=0, keepdims=True)
        kept[EXPO + kk : EXPO + kk + 1] = part
        total = total + part
    total = total + turn(total)
    store = pltpu.make_async_copy(kept, far_kept.at[pl.ds(0, KEPT)], sem.at[1])
    store.start()
    pair = jnp.where(lax.broadcasted_iota(jnp.int32, (8, LANES), 0) == 0, top, total)
    for s in range(CORE * SOURCES):
        stats[s] = pair
    keep.wait()
    store.wait()


def post_kernel(far_kept, table, far, rows, out, expo, sem):
    fetch = pltpu.make_async_copy(far_kept.at[pl.ds(0, EXPO)], expo, sem)
    fetch.start()
    fetch.wait()
    for kk in range(0, KROWS, 2):
        both = dot3(table, jnp.concatenate([expo[k * ROT : (k + 1) * ROT] for k in (kk, kk + 1)], axis=1))
        rows[kk * ANG : (kk + 1) * ANG] = both[:, :LANES]
        rows[(kk + 1) * ANG : (kk + 2) * ANG] = both[:, LANES:]

    def step(j, carry):
        real = rows[pl.ds(j, KROWS, stride=ANG), :]
        imag = rows[pl.ds(HALF + j, KROWS, stride=ANG), :]
        out[j] = jnp.concatenate([real, imag], axis=0)
        return carry

    lax.fori_loop(0, HALF, step, 0, unroll=36)
    keep = pltpu.make_async_copy(out, far, sem)
    keep.start()
    keep.wait()


def sum_kernel(*refs):
    kept = refs[2]
    far_small = refs[:2] + (kept.at[pl.ds(EXPO, KROWS)], kept.at[pl.ds(EXPO + KROWS, COUNT)])
    far_post, far_ydata, out, rows, slots, post, ydata = refs[3:10]
    small, (sem, small_sem) = refs[10:14], refs[14:]
    all_stats, stats, by_class, csq = small
    first_copies = [pltpu.make_async_copy(a, b, small_sem.at[i]) for i, (a, b) in enumerate(zip(far_small, small))]
    for copy in first_copies:
        copy.start()
    copies = []
    for part in range(PARTS):
        lines = pl.ds(part * HALF // PARTS, HALF // PARTS)
        copies.append(pltpu.make_async_copy(far_post.at[lines], post.at[lines], sem.at[0, part]))
        copies.append(pltpu.make_async_copy(far_ydata.at[lines], ydata.at[lines], sem.at[1, part]))
    for copy in copies:
        copy.start()
    for copy in first_copies:
        copy.wait()
    tops, totals = all_stats[:, 0, :], all_stats[:, 1, :]
    top = jnp.max(tops, axis=0, keepdims=True)
    total = jnp.sum(totals * jnp.exp(tops - top), axis=0, keepdims=True)
    share = jnp.exp(stats[0, 0:1] - top) / total

    def step(j, carry):
        wide = post[j] * share
        real, imag = wide[:KROWS], wide[KROWS:]
        weights = jnp.concatenate([real, turn(real), imag, turn(imag)], axis=0)[:, :CYCLES]
        both = dot(weights.astype(bf16), ydata[j])
        other = turn(both[KPAD:])
        other = jnp.where(left(other.shape), other, -other)
        rows[pl.ds(j, KPAD, stride=HALF), :] = both[:KPAD] + other
        return carry

    for part in range(PARTS):
        copies[2 * part].wait()
        copies[2 * part + 1].wait()
        lax.fori_loop(part * HALF // PARTS, (part + 1) * HALF // PARTS, step, 0, unroll=HALF // PARTS)
    mass = by_class[...] * share
    mass = jnp.concatenate([mass, turn(mass)], axis=0)[:, :CYCLES]
    weight = lax.dot_general(mass, csq[...], NN, precision=lax.Precision.HIGHEST, preferred_element_type=f32)
    high, low = halves(weight)
    scales = jnp.where(left(weight.shape), high.astype(f32), turn(low.astype(f32)))
    for part in range(ZL):
        first = part * CHUNK // HALF
        base = part * SLOT
        slots[base + CHUNK : base + SLOT] = jnp.zeros((SLOT - CHUNK, LANES), f32)
        slots[base : base + CHUNK] = rows[part * CHUNK : (part + 1) * CHUNK]
        slots[base + CHUNK : base + CHUNK + SPAN] = scales[first : first + SPAN]
        out[part] = slots[base : base + SLOT].astype(bf16)


LAST = CHUNK // 8 * 8


def fold_kernel(pieces, out):
    total = pieces[0].astype(f32)
    for s in range(1, ZL):
        total = total + pieces[s].astype(f32)
    rows = total[LAST:]
    scales = rows + turn(rows)
    high = scales.astype(bf16).astype(f32)
    scales = jnp.where(left(scales.shape), high, scales - high)
    row = lax.broadcasted_iota(jnp.int32, rows.shape, 0)
    rows = jnp.where(row < CHUNK - LAST, rows, scales)
    out[...] = jnp.concatenate([total[:LAST], rows], axis=0).astype(bf16)


def hat_kernel(part, pieces, out):
    total = pieces[0].astype(f32)
    for s in range(1, ZH):
        total = total + pieces[s].astype(f32)
    scales = total[CHUNK : CHUNK + SPAN]
    scales = 1.0 / (scales + turn(scales) + PRIOR_WEIGHT)
    row = lax.broadcasted_iota(jnp.int32, total.shape, 0) + part[0] * (CHUNK % HALF)
    factor = jnp.broadcast_to(scales[SPAN - 1 :], total.shape)
    for i in range(SPAN - 2, -1, -1):
        factor = jnp.where(row < (i + 1) * HALF, scales[i : i + 1], factor)
    out[...] = (total * factor).astype(bf16)


def image_kernel(place, table, hats, *refs):
    out, flat, real, imag, stage, sem = refs[-6:]
    x_lo = place[0]
    copies, shares = [], []
    for core in range(CORE):
        i = core
        base = core * PER_CORE + x_lo * (KD - 1)
        for part in range(ZL):
            flat[i, part * CHUNK : (part + 1) * CHUNK] = hats[i, part].astype(f32)[:CHUNK]
        for step, (first, last) in enumerate(GROUPS):
            for k in range(first, last):
                rows = flat[i, k * HALF : (k + 1) * HALF].T.astype(bf16)
                real[i, k * CYCLES : (k + 1) * CYCLES] = rows[:CYCLES]
                imag[i, k * CYCLES : (k + 1) * CYCLES] = rows[CYCLES:]
            lines = slice(first * CYCLES, last * CYCLES)
            image = dot(real[i, lines], table[0]) + dot(imag[i, lines], table[2])
            image = image + (dot(real[i, lines], table[1]) + dot(imag[i, lines], table[3]))
            stage[i, first:last] = image.astype(bf16).reshape(last - first, CYCLES, ANG)
            begin = max(first, 1)
            here, there = pl.ds(begin, last - begin), pl.ds(base + begin, last - begin)
            copy = pltpu.make_async_copy(stage.at[i, here], out.at[there], sem.at[i, step])
            copy.start()
            copies.append(copy)

        shared = pltpu.make_async_copy(stage.at[i, pl.ds(0, 1)], out.at[pl.ds(base, 1)], sem.at[i, len(GROUPS)])
        pl.when(x_lo == 0)(shared.start)
        shares.append(shared)

    for copy in copies:
        copy.wait()
    for shared in shares:
        pl.when(x_lo == 0)(shared.wait)


VMEM = pl.BlockSpec(memory_space=pltpu.VMEM)
SMEM = pl.BlockSpec(memory_space=pltpu.SMEM)
HBM = pl.BlockSpec(memory_space=pltpu.HBM)


def call(kernel, ins, outs, scratch, flops, nbytes, aliases=None, out_specs=None, limit=48):
    out_shape = [jax.ShapeDtypeStruct(shape, dtype) for shape, dtype in outs]
    single = len(out_shape) == 1
    specs = out_specs or [VMEM] * len(out_shape)
    return pl.pallas_call(
        kernel,
        out_shape=out_shape[0] if single else out_shape,
        in_specs=ins,
        out_specs=specs[0] if single else specs,
        scratch_shapes=scratch,
        input_output_aliases=aliases or {},
        compiler_params=pltpu.CompilerParams(vmem_limit_bytes=limit * 2**20),
        cost_estimate=pl.CostEstimate(flops=flops, bytes_accessed=nbytes, transcendentals=0),
    )


def swap(axis, value):
    return lax.ppermute(value, axis, [(0, 1), (1, 0)])


def share(group_ids, particles, ctf_table, forward):
    return call(
        share_kernel,
        [SMEM, VMEM, VMEM, VMEM],
        [((SOURCES, MSG, LANES), bf16)],
        [pltpu.VMEM((MSG, LANES), bf16), pltpu.SemaphoreType.DMA((SOURCES,))],
        10**7,
        10**6,
        out_specs=[HBM],
        limit=64,
    )(group_ids, particles, ctf_table, forward)


def classes(references, forward):
    return call(
        class_kernel,
        [HBM, VMEM],
        [((HALF, KPAD, LANES), bf16), ((KPAD, LANES), f32)],
        [
            pltpu.VMEM((KPAD, CYCLES, ANG), bf16),
            pltpu.VMEM(((KPAD + 1) * HALF, LANES), f32),
            pltpu.SemaphoreType.DMA,
        ],
        10**9,
        4 * 10**6,
        limit=24,
    )(references, forward)


def scores(place, own, other, rmat, power, table):
    return call(
        score_kernel,
        [SMEM] + [VMEM] * 5,
        [
            ((CORE * SOURCES, 8, LANES), f32),
            ((ROOMY, LANES), f32),
            ((LONG, COUNT, LANES), bf16),
        ],
        [
            pltpu.VMEM(((CORE * SOURCES + 1) * MSG, LANES), f32),
            pltpu.VMEM(((KROWS + 1) * ANG, LANES), f32),
            pltpu.VMEM((HALF, COUNT, LANES), bf16),
            pltpu.VMEM((KEPT, LANES), f32),
            pltpu.SemaphoreType.DMA((2,)),
        ],
        10**9,
        8 * 10**6,
        limit=48,
        out_specs=[VMEM, HBM, HBM],
    )(place, own, other, rmat, power, table)


def posts(expo, table):
    return call(
        post_kernel,
        [HBM, VMEM],
        [((HALF, KPAD, LANES), f32)],
        [
            pltpu.VMEM(((KROWS + 1) * ANG, LANES), f32),
            pltpu.VMEM((HALF, KPAD, LANES), f32),
            pltpu.VMEM((EXPO, LANES), f32),
            pltpu.SemaphoreType.DMA,
        ],
        10**9,
        3 * 10**6,
        limit=64,
        out_specs=[HBM],
    )(expo, table)


def sums_of(all_stats, stats, kept, post, ydata):
    return call(
        sum_kernel,
        [HBM] * 5,
        [((ZL, SLOT, LANES), bf16)],
        [
            pltpu.VMEM(((KPAD + 1) * HALF, LANES), f32),
            pltpu.VMEM((ZL * SLOT, LANES), f32),
            pltpu.VMEM((HALF, KPAD, LANES), f32),
            pltpu.VMEM((HALF, COUNT, LANES), bf16),
            pltpu.VMEM((CORE * SOURCES, 8, LANES), f32),
            pltpu.VMEM((CORE * SOURCES, 8, LANES), f32),
            pltpu.VMEM((KROWS, LANES), f32),
            pltpu.VMEM((COUNT, LANES), f32),
            pltpu.SemaphoreType.DMA((2, PARTS)),
            pltpu.SemaphoreType.DMA((4,)),
        ],
        10**9,
        8 * 10**6,
        limit=64,
    )(all_stats, stats, kept, post, ydata)


def images(place, hats, inverse, result):
    extra = [] if result is None else [result]
    return call(
        image_kernel,
        [SMEM, VMEM, VMEM] + [HBM] * len(extra),
        [((CORE * PER_CORE, CYCLES, ANG), bf16)],
        [
            pltpu.VMEM((CORE, KD * HALF, LANES), f32),
            pltpu.VMEM((CORE, KD * CYCLES, HALF), bf16),
            pltpu.VMEM((CORE, KD * CYCLES, HALF), bf16),
            pltpu.VMEM((CORE, KD, CYCLES, ANG), bf16),
            pltpu.SemaphoreType.DMA((CORE, len(GROUPS) + 1)),
        ],
        1000,
        1000,
        {3: 0} if extra else None,
        [HBM],
    )(place.reshape(1), inverse, hats, *extra)


def body(particles, group_ids, ctf_table, references):
    core, x_lo = lax.axis_index("core"), lax.axis_index("x_lo")
    forward = jnp.asarray(forward_table())
    place = jnp.stack([core, x_lo])

    messages = share(group_ids, particles, ctf_table, forward)
    own = lax.all_to_all(messages, ("x_lo", "x_hi", "y"), 0, 0, tiled=True)
    mine = lax.dynamic_slice_in_dim(references, core * PER_CORE + x_lo * (KD - 1), KD, 0)
    part = lax.axis_index("z_lo").reshape(1)
    own, part, mine = lax.optimization_barrier((own, part, mine))
    rmat, power = classes(mine, forward)
    other = swap("core", own)

    stats, kept, ydata = scores(
        place, own, other, rmat, power, jnp.asarray(search_table().reshape(3 * ROT, ANG))
    )
    all_stats = lax.all_to_all(stats, ("core", "x_lo", "x_hi", "y"), 0, 0, tiled=True)
    post = posts(kept, jnp.asarray(post_table().reshape(3 * ANG, ROT)))
    sums = sums_of(all_stats, stats, kept, post, ydata)

    near = lax.all_to_all(sums, "z_lo", 0, 0, tiled=True)
    near = call(fold_kernel, [VMEM], [((SLOT, LANES), bf16)], [], 10**6, 10**6, limit=20)(near)
    near = lax.all_gather(near, "z_hi")
    hat = call(hat_kernel, [SMEM, VMEM], [((SLOT, LANES), bf16)], [], 10**6, 10**6, limit=20)(part, near)

    inverse = jnp.asarray(inverse_table())
    near = lax.all_gather(hat, "z_lo")
    far = swap("x_lo", near)
    result = images(x_lo, lax.all_gather(near, "core"), inverse, None)
    far, result = lax.optimization_barrier((far, result))
    return images(1 - x_lo, lax.all_gather(far, "core"), inverse, result)


def solution(mesh):
    fine = Mesh(mesh.devices.reshape(X, ZH, ZL, CORE, 2, 4), DOM + CLS)
    in_specs = (P(DOM + CLS, None, None), P(DOM + CLS), P(), P(CLS, None, None))
    return jax.shard_map(body, mesh=fine, in_specs=in_specs, out_specs=P(CLS, None, None), check_vma=False)
```

```python
import math

import jax
import jax.numpy as jnp
import ml_dtypes
import numpy as np
from jax import lax
from jax.experimental import pallas as pl
from jax.experimental.pallas import tpu as pltpu
from jax.sharding import Mesh
from jax.sharding import PartitionSpec as P

CYCLES = 64
ANG = 288
ROT = 72
HALF = ANG // 2
LANES = 2 * CYCLES
PRIOR_WEIGHT = 1.0
SCORE_SCALE = 4.0 / math.sqrt(CYCLES * ANG)

X, Z, CORE, SIDE = 2, 16, 2, 8
ZH, ZL = 4, 4
MINE = 2
PER_CORE = 25
KD = 13
KPAD = 16
KROWS = KPAD // 2
PARTS = 2
EXPO = 8 * 72
KEPT = EXPO + 8 + 64
ROOMY = 36000
LONG = 1100
GROUPS = ((0, 5), (5, 9), (9, 13))
SOURCES = X * SIDE
COUNT = MINE * CORE * SOURCES
MSG = MINE * HALF + 16
CHUNK = KD * HALF // ZL
SPAN = -(-CHUNK // HALF) + 1
SLOT = 480

DOM = ("x_lo", "z_hi", "z_lo", "core")
CLS = ("x_hi", "y")

NT = (((1,), (1,)), ((), ()))
NN = (((1,), (0,)), ((), ()))
f32 = jnp.float32
bf16 = jnp.bfloat16


def angles(rows, cols, factor):
    index = np.arange(rows)[:, None] * factor * np.arange(cols)[None, :] % ANG
    return 2.0 * math.pi * index / ANG


def split(table, count):
    rest, pieces = table.astype(np.float32), []
    for _ in range(count):
        pieces.append(rest.astype(ml_dtypes.bfloat16))
        rest = rest - pieces[-1].astype(np.float32)
    return np.stack(pieces)


def forward_table():
    angle = angles(HALF + 1, ANG, 1)
    real = np.cos(angle[:HALF])
    imag = np.concatenate([np.cos(angle[HALF:]), np.sin(angle[1:HALF])])
    return split(np.concatenate([real, imag]), 3)


def weights_of_rows():
    return np.where(np.arange(HALF) == 0, 1.0, 2.0)[:, None] / ANG


def search_table():
    angle = angles(HALF, ROT, ANG // ROT)
    scale = weights_of_rows()
    return split(np.concatenate([np.cos(angle) * scale, -np.sin(angle) * scale]).T, 3)


def post_table():
    angle = angles(HALF, ROT, ANG // ROT)
    return split(np.concatenate([np.cos(angle), np.sin(angle)]), 3)


def inverse_table():
    angle = angles(HALF + 1, ANG, 1)
    scale = weights_of_rows()
    real = np.cos(angle[:HALF]) * scale
    imag = np.concatenate([np.cos(angle[HALF:]), np.sin(angle[1:HALF])]) * scale
    return np.concatenate([split(real, 2), split(imag, 2)])


def dot(a, b, dims=NN):
    return lax.dot_general(a, b, dims, preferred_element_type=f32)


def halves(values):
    high = values.astype(bf16)
    return high, (values - high.astype(f32)).astype(bf16)


def thirds(values):
    high = values.astype(bf16)
    rest = values - high.astype(f32)
    mid = rest.astype(bf16)
    return high, mid, (rest - mid.astype(f32)).astype(bf16)


def dot3(table, values):
    high, mid, low = thirds(values)
    rows = table.shape[0] // 3
    first = dot(table[...], high)
    second = dot(table[: 2 * rows], mid)
    small = (first[2 * rows :] + second[rows:]) + dot(table[:rows], low)
    return first[:rows] + (first[rows : 2 * rows] + second[:rows] + small)


def transform(table, images):
    return dot(table[0], images, NT) + (dot(table[1], images, NT) + dot(table[2], images, NT))


def turn(values):
    return pltpu.roll(values, CYCLES, 1)


def left(shape):
    return lax.broadcasted_iota(jnp.int32, shape, len(shape) - 1) < CYCLES


def fold(spec):
    real, imag = spec[:HALF], spec[HALF:]
    side = left(real.shape)
    return jnp.where(side, real, turn(imag)), jnp.where(side, turn(real), imag)


def share_kernel(ids, x, ctf, table, outs, out, sem):
    images = x[...].reshape(MINE * CYCLES, ANG)
    factor = jnp.concatenate([ctf[pl.ds(ids[0], 1), :], ctf[pl.ds(ids[1], 1), :]], axis=1)
    spec = transform(table, images) * factor
    first, second = fold(spec)
    out[0:HALF] = first.astype(bf16)
    out[HALF : 2 * HALF] = second.astype(bf16)
    high, mid, low = thirds(factor)
    row = lax.broadcasted_iota(jnp.int32, (16, LANES), 0)
    tags = jnp.where(row == 0, high.astype(f32), jnp.where(row == 1, mid.astype(f32), jnp.where(row == 2, low.astype(f32), 0.0)))
    out[2 * HALF : MSG] = tags.astype(bf16)
    copies = [pltpu.make_async_copy(out, outs.at[s], sem.at[s]) for s in range(SOURCES)]
    for copy in copies:
        copy.start()
    for copy in copies:
        copy.wait()


def class_kernel(refs, table, out, power, images, rows, sem):
    copy = pltpu.make_async_copy(refs, images.at[pl.ds(0, KD)], sem)
    copy.start()
    images[KD:] = jnp.zeros((KPAD - KD, CYCLES, ANG), bf16)
    ones = jnp.ones((8, ANG), bf16)
    copy.wait()
    for step in range(KPAD // 4):
        block = images[4 * step : 4 * step + 4].reshape(4 * CYCLES, ANG)
        spec = transform(table, block)
        wide = block.astype(f32)
        high, low = halves(wide * wide)
        energy = dot(ones, high, NT) + dot(ones, low, NT)
        for pair in range(2):
            k = 4 * step + 2 * pair
            lanes = slice(pair * LANES, (pair + 1) * LANES)
            first, second = fold(spec[:, lanes])
            rows[k * HALF : (k + 1) * HALF] = first.astype(bf16).astype(f32)
            rows[(k + 1) * HALF : (k + 2) * HALF] = second.astype(bf16).astype(f32)
            part = energy[:, lanes]
            side = left(part.shape)
            power[k : k + 1] = jnp.where(side, part, 0.0)[0:1]
            power[k + 1 : k + 2] = jnp.where(side, turn(part), 0.0)[0:1]

    def step(j, carry):
        plain = rows[pl.ds(j, KPAD, stride=HALF), :]
        out[j] = plain.astype(bf16)
        return carry

    lax.fori_loop(0, HALF, step, 0, unroll=36)


def score_kernel(place, own, other, rmat, power, table, stats, far_kept, far, wide, pairs, ydata, kept, sem):
    core, x_lo = place[0], place[1]

    def widen(s, carry):
        mine = pl.multiple_of((core * SOURCES + s) * MSG, 8)
        theirs = pl.multiple_of(((1 - core) * SOURCES + s) * MSG, 8)
        wide[pl.ds(mine, MSG), :] = own[s].astype(f32)
        wide[pl.ds(theirs, MSG), :] = other[s].astype(f32)
        return carry

    lax.fori_loop(0, SOURCES, widen, 0, unroll=2)
    many = CORE * SOURCES
    factor = wide[pl.ds(2 * HALF, many, stride=MSG), :] + wide[pl.ds(2 * HALF + 1, many, stride=MSG), :]
    factor = factor + wide[pl.ds(2 * HALF + 2, many, stride=MSG), :]
    square = factor * factor
    side = left(square.shape)
    square = jnp.concatenate([jnp.where(side, square, 0.0), jnp.where(side, turn(square), 0.0)], axis=0)
    kept[EXPO + KROWS : KEPT] = square
    energy = lax.dot_general(
        power[...],
        jnp.concatenate([square, square], axis=0),
        NT,
        precision=lax.Precision.HIGHEST,
        preferred_element_type=f32,
    )
    side = left((KROWS, LANES))
    energy = jnp.where(side, energy[:KROWS], energy[KROWS:])

    def step(j, carry):
        rows = jnp.concatenate([wide[pl.ds(j, many, stride=MSG), :], wide[pl.ds(HALF + j, many, stride=MSG), :]], axis=0)
        rows = rows.astype(bf16)
        ydata[j] = rows
        plain = rmat[j].astype(f32)
        cross = turn(plain)
        cross = jnp.where(left(cross.shape), cross, -cross)
        both = dot(jnp.concatenate([plain, cross], axis=0).astype(bf16), rows, NT)
        straight = jnp.concatenate([both[:KROWS], both[KROWS : 2 * KROWS]], axis=1)
        crossed = jnp.concatenate([both[2 * KROWS : 3 * KROWS], both[3 * KROWS :]], axis=1)
        pairs[pl.ds(j, KROWS, stride=ANG), :] = straight
        pairs[pl.ds(HALF + j, KROWS, stride=ANG), :] = crossed
        return carry

    lax.fori_loop(0, HALF, step, 0, unroll=48)
    keep = pltpu.make_async_copy(ydata, far.at[pl.ds(0, HALF)], sem.at[0])
    keep.start()
    top = jnp.full((1, LANES), -3.0e38, f32)
    lane_side = left((ROT, LANES))
    crosses = []
    for kk in range(0, KROWS, 2):
        two = [pairs[k * ANG : (k + 1) * ANG] for k in (kk, kk + 1)]
        wide_cross = dot3(table, jnp.concatenate(two, axis=1))
        crosses += [wide_cross[:, :LANES], wide_cross[:, LANES:]]
    for kk in range(KROWS):
        cross = crosses[kk]
        score = SCORE_SCALE * (cross - 0.5 * energy[kk : kk + 1])
        if kk + KROWS >= KD:
            score = jnp.where(lane_side, score, -3.0e38)
        if kk == 0:
            score = jnp.where(jnp.logical_and(lane_side, x_lo == 1), -3.0e38, score)
        kept[kk * ROT : (kk + 1) * ROT] = score
        top = jnp.maximum(top, jnp.max(score, axis=0, keepdims=True))
    top = jnp.maximum(top, turn(top))
    total = jnp.zeros((1, LANES), f32)
    for kk in range(KROWS):
        value = jnp.exp(kept[kk * ROT : (kk + 1) * ROT] - top)
        kept[kk * ROT : (kk + 1) * ROT] = value
        part = jnp.sum(value, axis=0, keepdims=True)
        kept[EXPO + kk : EXPO + kk + 1] = part
        total = total + part
    total = total + turn(total)
    store = pltpu.make_async_copy(kept, far_kept.at[pl.ds(0, KEPT)], sem.at[1])
    store.start()
    pair = jnp.where(lax.broadcasted_iota(jnp.int32, (8, LANES), 0) == 0, top, total)
    for s in range(CORE * SOURCES):
        stats[s] = pair
    keep.wait()
    store.wait()


def post_kernel(far_kept, table, far, rows, out, expo, sem):
    fetch = pltpu.make_async_copy(far_kept.at[pl.ds(0, EXPO)], expo, sem)
    fetch.start()
    fetch.wait()
    for kk in range(0, KROWS, 2):
        both = dot3(table, jnp.concatenate([expo[k * ROT : (k + 1) * ROT] for k in (kk, kk + 1)], axis=1))
        rows[kk * ANG : (kk + 1) * ANG] = both[:, :LANES]
        rows[(kk + 1) * ANG : (kk + 2) * ANG] = both[:, LANES:]

    def step(j, carry):
        real = rows[pl.ds(j, KROWS, stride=ANG), :]
        imag = rows[pl.ds(HALF + j, KROWS, stride=ANG), :]
        out[j] = jnp.concatenate([real, imag], axis=0)
        return carry

    lax.fori_loop(0, HALF, step, 0, unroll=36)
    keep = pltpu.make_async_copy(out, far, sem)
    keep.start()
    keep.wait()


def sum_kernel(*refs):
    kept = refs[2]
    far_small = refs[:2] + (kept.at[pl.ds(EXPO, KROWS)], kept.at[pl.ds(EXPO + KROWS, COUNT)])
    far_post, far_ydata, out, rows, slots, post, ydata = refs[3:10]
    small, (sem, small_sem) = refs[10:14], refs[14:]
    all_stats, stats, by_class, csq = small
    first_copies = [pltpu.make_async_copy(a, b, small_sem.at[i]) for i, (a, b) in enumerate(zip(far_small, small))]
    for copy in first_copies:
        copy.start()
    copies = []
    for part in range(PARTS):
        lines = pl.ds(part * HALF // PARTS, HALF // PARTS)
        copies.append(pltpu.make_async_copy(far_post.at[lines], post.at[lines], sem.at[0, part]))
        copies.append(pltpu.make_async_copy(far_ydata.at[lines], ydata.at[lines], sem.at[1, part]))
    for copy in copies:
        copy.start()
    for copy in first_copies:
        copy.wait()
    tops, totals = all_stats[:, 0, :], all_stats[:, 1, :]
    top = jnp.max(tops, axis=0, keepdims=True)
    total = jnp.sum(totals * jnp.exp(tops - top), axis=0, keepdims=True)
    share = jnp.exp(stats[0, 0:1] - top) / total

    def step(j, carry):
        wide = post[j] * share
        real, imag = wide[:KROWS], wide[KROWS:]
        weights = jnp.concatenate([real, turn(real), imag, turn(imag)], axis=0)[:, :CYCLES]
        both = dot(weights.astype(bf16), ydata[j])
        other = turn(both[KPAD:])
        other = jnp.where(left(other.shape), other, -other)
        rows[pl.ds(j, KPAD, stride=HALF), :] = both[:KPAD] + other
        return carry

    for part in range(PARTS):
        copies[2 * part].wait()
        copies[2 * part + 1].wait()
        lax.fori_loop(part * HALF // PARTS, (part + 1) * HALF // PARTS, step, 0, unroll=HALF // PARTS)
    mass = by_class[...] * share
    mass = jnp.concatenate([mass, turn(mass)], axis=0)[:, :CYCLES]
    weight = lax.dot_general(mass, csq[...], NN, precision=lax.Precision.HIGHEST, preferred_element_type=f32)
    high, low = halves(weight)
    scales = jnp.where(left(weight.shape), high.astype(f32), turn(low.astype(f32)))
    for part in range(ZL):
        first = part * CHUNK // HALF
        base = part * SLOT
        slots[base + CHUNK : base + SLOT] = jnp.zeros((SLOT - CHUNK, LANES), f32)
        slots[base : base + CHUNK] = rows[part * CHUNK : (part + 1) * CHUNK]
        slots[base + CHUNK : base + CHUNK + SPAN] = scales[first : first + SPAN]
        out[part] = slots[base : base + SLOT].astype(bf16)


LAST = CHUNK // 8 * 8


def fold_kernel(pieces, out):
    total = pieces[0].astype(f32)
    for s in range(1, ZL):
        total = total + pieces[s].astype(f32)
    rows = total[LAST:]
    scales = rows + turn(rows)
    high = scales.astype(bf16).astype(f32)
    scales = jnp.where(left(scales.shape), high, scales - high)
    row = lax.broadcasted_iota(jnp.int32, rows.shape, 0)
    rows = jnp.where(row < CHUNK - LAST, rows, scales)
    out[...] = jnp.concatenate([total[:LAST], rows], axis=0).astype(bf16)


def hat_kernel(part, pieces, out):
    total = pieces[0].astype(f32)
    for s in range(1, ZH):
        total = total + pieces[s].astype(f32)
    scales = total[CHUNK : CHUNK + SPAN]
    scales = 1.0 / (scales + turn(scales) + PRIOR_WEIGHT)
    row = lax.broadcasted_iota(jnp.int32, total.shape, 0) + part[0] * (CHUNK % HALF)
    factor = jnp.broadcast_to(scales[SPAN - 1 :], total.shape)
    for i in range(SPAN - 2, -1, -1):
        factor = jnp.where(row < (i + 1) * HALF, scales[i : i + 1], factor)
    out[...] = (total * factor).astype(bf16)


def image_kernel(place, table, hats, *refs):
    out, flat, real, imag, stage, sem = refs[-6:]
    x_lo = place[0]
    copies, shares = [], []
    for core in range(CORE):
        i = core
        base = core * PER_CORE + x_lo * (KD - 1)
        for part in range(ZL):
            flat[i, part * CHUNK : (part + 1) * CHUNK] = hats[i, part].astype(f32)[:CHUNK]
        for step, (first, last) in enumerate(GROUPS):
            for k in range(first, last):
                rows = flat[i, k * HALF : (k + 1) * HALF].T.astype(bf16)
                real[i, k * CYCLES : (k + 1) * CYCLES] = rows[:CYCLES]
                imag[i, k * CYCLES : (k + 1) * CYCLES] = rows[CYCLES:]
            lines = slice(first * CYCLES, last * CYCLES)
            image = dot(real[i, lines], table[0]) + dot(imag[i, lines], table[2])
            image = image + (dot(real[i, lines], table[1]) + dot(imag[i, lines], table[3]))
            stage[i, first:last] = image.astype(bf16).reshape(last - first, CYCLES, ANG)
            begin = max(first, 1)
            here, there = pl.ds(begin, last - begin), pl.ds(base + begin, last - begin)
            copy = pltpu.make_async_copy(stage.at[i, here], out.at[there], sem.at[i, step])
            copy.start()
            copies.append(copy)

        shared = pltpu.make_async_copy(stage.at[i, pl.ds(0, 1)], out.at[pl.ds(base, 1)], sem.at[i, len(GROUPS)])
        pl.when(x_lo == 0)(shared.start)
        shares.append(shared)

    for copy in copies:
        copy.wait()
    for shared in shares:
        pl.when(x_lo == 0)(shared.wait)


VMEM = pl.BlockSpec(memory_space=pltpu.VMEM)
SMEM = pl.BlockSpec(memory_space=pltpu.SMEM)
HBM = pl.BlockSpec(memory_space=pltpu.HBM)


def call(kernel, ins, outs, scratch, flops, nbytes, aliases=None, out_specs=None, limit=48):
    out_shape = [jax.ShapeDtypeStruct(shape, dtype) for shape, dtype in outs]
    single = len(out_shape) == 1
    specs = out_specs or [VMEM] * len(out_shape)
    return pl.pallas_call(
        kernel,
        out_shape=out_shape[0] if single else out_shape,
        in_specs=ins,
        out_specs=specs[0] if single else specs,
        scratch_shapes=scratch,
        input_output_aliases=aliases or {},
        compiler_params=pltpu.CompilerParams(vmem_limit_bytes=limit * 2**20),
        cost_estimate=pl.CostEstimate(flops=flops, bytes_accessed=nbytes, transcendentals=0),
    )


def swap(axis, value):
    return lax.ppermute(value, axis, [(0, 1), (1, 0)])


def share(group_ids, particles, ctf_table, forward):
    return call(
        share_kernel,
        [SMEM, VMEM, VMEM, VMEM],
        [((SOURCES, MSG, LANES), bf16)],
        [pltpu.VMEM((MSG, LANES), bf16), pltpu.SemaphoreType.DMA((SOURCES,))],
        10**7,
        10**6,
        out_specs=[HBM],
        limit=64,
    )(group_ids, particles, ctf_table, forward)


def classes(references, forward):
    return call(
        class_kernel,
        [HBM, VMEM],
        [((HALF, KPAD, LANES), bf16), ((KPAD, LANES), f32)],
        [
            pltpu.VMEM((KPAD, CYCLES, ANG), bf16),
            pltpu.VMEM(((KPAD + 1) * HALF, LANES), f32),
            pltpu.SemaphoreType.DMA,
        ],
        10**9,
        4 * 10**6,
        limit=24,
    )(references, forward)


def scores(place, own, other, rmat, power, table):
    return call(
        score_kernel,
        [SMEM] + [VMEM] * 5,
        [
            ((CORE * SOURCES, 8, LANES), f32),
            ((ROOMY, LANES), f32),
            ((LONG, COUNT, LANES), bf16),
        ],
        [
            pltpu.VMEM(((CORE * SOURCES + 1) * MSG, LANES), f32),
            pltpu.VMEM(((KROWS + 1) * ANG, LANES), f32),
            pltpu.VMEM((HALF, COUNT, LANES), bf16),
            pltpu.VMEM((KEPT, LANES), f32),
            pltpu.SemaphoreType.DMA((2,)),
        ],
        10**9,
        8 * 10**6,
        limit=48,
        out_specs=[VMEM, HBM, HBM],
    )(place, own, other, rmat, power, table)


def posts(expo, table):
    return call(
        post_kernel,
        [HBM, VMEM],
        [((HALF, KPAD, LANES), f32)],
        [
            pltpu.VMEM(((KROWS + 1) * ANG, LANES), f32),
            pltpu.VMEM((HALF, KPAD, LANES), f32),
            pltpu.VMEM((EXPO, LANES), f32),
            pltpu.SemaphoreType.DMA,
        ],
        10**9,
        3 * 10**6,
        limit=64,
        out_specs=[HBM],
    )(expo, table)


def sums_of(all_stats, stats, kept, post, ydata):
    return call(
        sum_kernel,
        [HBM] * 5,
        [((ZL, SLOT, LANES), bf16)],
        [
            pltpu.VMEM(((KPAD + 1) * HALF, LANES), f32),
            pltpu.VMEM((ZL * SLOT, LANES), f32),
            pltpu.VMEM((HALF, KPAD, LANES), f32),
            pltpu.VMEM((HALF, COUNT, LANES), bf16),
            pltpu.VMEM((CORE * SOURCES, 8, LANES), f32),
            pltpu.VMEM((CORE * SOURCES, 8, LANES), f32),
            pltpu.VMEM((KROWS, LANES), f32),
            pltpu.VMEM((COUNT, LANES), f32),
            pltpu.SemaphoreType.DMA((2, PARTS)),
            pltpu.SemaphoreType.DMA((4,)),
        ],
        10**9,
        8 * 10**6,
        limit=48,
    )(all_stats, stats, kept, post, ydata)


def images(place, hats, inverse, result):
    extra = [] if result is None else [result]
    return call(
        image_kernel,
        [SMEM, VMEM, VMEM] + [HBM] * len(extra),
        [((CORE * PER_CORE, CYCLES, ANG), bf16)],
        [
            pltpu.VMEM((CORE, KD * HALF, LANES), f32),
            pltpu.VMEM((CORE, KD * CYCLES, HALF), bf16),
            pltpu.VMEM((CORE, KD * CYCLES, HALF), bf16),
            pltpu.VMEM((CORE, KD, CYCLES, ANG), bf16),
            pltpu.SemaphoreType.DMA((CORE, len(GROUPS) + 1)),
        ],
        1000,
        1000,
        {3: 0} if extra else None,
        [HBM],
    )(place.reshape(1), inverse, hats, *extra)


def body(particles, group_ids, ctf_table, references):
    core, x_lo = lax.axis_index("core"), lax.axis_index("x_lo")
    forward = jnp.asarray(forward_table())
    place = jnp.stack([core, x_lo])

    messages = share(group_ids, particles, ctf_table, forward)
    own = lax.all_to_all(messages, ("x_lo", "x_hi", "y"), 0, 0, tiled=True)
    mine = lax.dynamic_slice_in_dim(references, core * PER_CORE + x_lo * (KD - 1), KD, 0)
    part = lax.axis_index("z_lo").reshape(1)
    own, part, mine = lax.optimization_barrier((own, part, mine))
    rmat, power = classes(mine, forward)
    other = swap("core", own)

    stats, kept, ydata = scores(
        place, own, other, rmat, power, jnp.asarray(search_table().reshape(3 * ROT, ANG))
    )
    all_stats = lax.all_to_all(stats, ("core", "x_lo", "x_hi", "y"), 0, 0, tiled=True)
    post = posts(kept, jnp.asarray(post_table().reshape(3 * ANG, ROT)))
    sums = sums_of(all_stats, stats, kept, post, ydata)

    near = lax.all_to_all(sums, "z_lo", 0, 0, tiled=True)
    near = call(fold_kernel, [VMEM], [((SLOT, LANES), bf16)], [], 10**6, 10**6, limit=20)(near)
    near = lax.all_gather(near, "z_hi")
    hat = call(hat_kernel, [SMEM, VMEM], [((SLOT, LANES), bf16)], [], 10**6, 10**6, limit=20)(part, near)

    inverse = jnp.asarray(inverse_table())
    near = lax.all_gather(hat, "z_lo")
    far = swap("x_lo", near)
    result = images(x_lo, lax.all_gather(near, "core"), inverse, None)
    far, result = lax.optimization_barrier((far, result))
    return images(1 - x_lo, lax.all_gather(far, "core"), inverse, result)


def solution(mesh):
    fine = Mesh(mesh.devices.reshape(X, ZH, ZL, CORE, 2, 4), DOM + CLS)
    in_specs = (P(DOM + CLS, None, None), P(DOM + CLS), P(), P(CLS, None, None))
    return jax.shard_map(body, mesh=fine, in_specs=in_specs, out_specs=P(CLS, None, None), check_vma=False)
```
